512 devices in a mesh: gx: 4 (over z_hi, core), gy: 8 (over y), gz: 16 (over x, z_lo).
Axes of the slice: x: 4, y: 8, z: 8 (z_hi: 2, z_lo: 4; z = z_hi * 4 + z_lo), core: 2. Of those that a mesh axis runs over, the one named last changes fastest.
Arguments:
- features: bfloat16 [32, 64, 2048, 128], P('gx', 'gy', 'gz'), may hold values from -6 to 6
- positions: float32 [3, 32, 64, 2048], P(None, 'gx', 'gy', 'gz'), may hold values from 0 to 1
- box_counts: int32 [32, 64, 64], P('gx', 'gy', 'gz'), may hold values from 1 to 32, as said below
- w_hidden: bfloat16 [128, 128], replicated, may hold values from -0.5 to 0.5
- w_charge: bfloat16 [128], replicated, may hold values from -0.5 to 0.5
- wave_numbers: float32 [3, 128], replicated, may hold values from -24 to 24
- phases: float32 [128], replicated, may hold values from -3.140625 to 3.140625
- upward: bfloat16 [2, 8, 128, 128], replicated, may hold values from -0.1875 to 0.1875
- downward: bfloat16 [2, 8, 128, 128], replicated, may hold values from -0.5 to 0.5
- transfer: bfloat16 [3, 128, 128], replicated, may hold values from -0.5 to 0.5
- out_scale: float32 [3, 343, 128], replicated, may hold values from -0.018 to 0.018
- in_scale: float32 [3, 343, 128], replicated, may hold values from 0.5 to 2
Outputs:
- forces: float32 [3, 32, 64, 2048], P(None, 'gx', 'gy', 'gz')
- virial: float32 [3, 3], replicated
The draws below stay inside these ranges and needn't reach their ends.
Inputs may be any that keep to these rules, and one draw needn't show every extreme that they name: `box_counts`: the live atoms of a box fill its first slots; some box holds 32 atoms.
All inputs are finite; a program needn't handle non-finite values.
Results may differ from the reference program's by a relative error of at most 0.012.
Values sent between devices are 32-bit elements; how exact they have to be, the bound alone decides.
No kernel may reach another device: no remote copies, remote signals or barrier semaphores. Data moves between devices by JAX's collectives and lax.ppermute only.
A program may use at most 64 MiB of HBM per device.

```python
import math
import jax
import jax.numpy as jnp
import numpy as np
from jax import lax

F = 128
H = 128
P_SIZE = 128
SLOTS = 32
LEVELS = 3
OFFSETS = 343
NBX = 32
NBY = 64
NBZ = 64
ATOMS = 4194304


def draw_box_counts(key, part):
    first, second, third, fourth = jax.random.split(key, 4)
    counts = jax.random.randint(first, (NBX, NBY, NBZ), 1, SLOTS + 1)
    spot_x = jax.random.randint(second, (), 0, NBX)
    spot_y = jax.random.randint(third, (), 0, NBY)
    spot_z = jax.random.randint(fourth, (), 0, NBZ)
    return counts.at[spot_x, spot_y, spot_z].set(SLOTS).astype(jnp.int32)


def steps_of(key, dims, pieces, low, top_value):
    def one(position, shards_of):
        heights = jax.random.uniform(jax.random.fold_in(jax.random.fold_in(key, 6), position), (shards_of,), jnp.float32, low / len(pieces), top_value / len(pieces))
        return jnp.repeat(jnp.exp(heights), dims[position] // shards_of).reshape((-1,) + (1,) * (len(dims) - position - 1))

    level = one(*pieces[0])
    for cut in pieces[1:]:
        level = level * one(*cut)
    return level


def normal_values(key, shape, scale, limit, cuts=(), kind=jnp.bfloat16):
    loudness = steps_of(key, shape, cuts, -0.22, 0.18) if cuts else 1.0
    array = jax.random.normal(key, shape, jnp.float32) * scale * loudness
    return jnp.minimum(jnp.maximum(array, -limit), limit).astype(kind)


def setup_inputs(seed: int = 0) -> dict:
    keys = jax.random.split(jax.random.key(seed), 13)
    features = normal_values(keys[0], (NBX, NBY, NBZ * SLOTS, F), 1.0, 6.0, ((0, 4), (1, 8), (2, 16)))
    positions = jnp.clip(1.0 * jax.random.uniform(keys[1], (3, NBX, NBY, NBZ * SLOTS), jnp.float32) ** steps_of(keys[1], (3, NBX, NBY, NBZ * SLOTS), ((1, 4), (2, 8), (3, 16)), -0.2, 0.2), 0.0, 1.0)
    box_counts = draw_box_counts(jax.random.fold_in(keys[12], 71), 0)
    w_hidden = normal_values(keys[3], (F, H), F ** -0.5, 0.5)
    w_charge = normal_values(keys[4], (H,), H ** -0.5, 0.5)
    wave_numbers = normal_values(keys[5], (3, P_SIZE), 6.0, 24.0, (), jnp.float32)
    phases = jnp.clip(jax.random.uniform(keys[6], (P_SIZE,), jnp.float32, -3.140625, 3.140625), -3.140625, 3.140625)
    upward = normal_values(keys[7], (LEVELS - 1, 8, P_SIZE, P_SIZE), (8 * P_SIZE) ** -0.5, 0.1875)
    downward = normal_values(keys[8], (LEVELS - 1, 8, P_SIZE, P_SIZE), P_SIZE ** -0.5, 0.5)
    transfer = normal_values(keys[9], (LEVELS, P_SIZE, P_SIZE), P_SIZE ** -0.5, 0.5)
    out_scale = normal_values(keys[10], (LEVELS, OFFSETS, P_SIZE), 0.003, 0.018, (), jnp.float32)
    in_scale = jnp.clip(jnp.exp(jax.random.uniform(keys[11], (LEVELS, OFFSETS, P_SIZE), jnp.float32, math.log(0.5), math.log(2.0))), 0.5, 2.0)
    return dict(features=features, positions=positions, box_counts=box_counts, w_hidden=w_hidden, w_charge=w_charge, wave_numbers=wave_numbers, phases=phases, upward=upward, downward=downward, transfer=transfer, out_scale=out_scale, in_scale=in_scale)


def offset_tables():
    index_rows = np.zeros((216, 8), np.int32)
    keep_rows = np.zeros((216, 8), np.float32)
    for along_x in range(6):
        for along_y in range(6):
            for along_z in range(6):
                row = (along_x * 6 + along_y) * 6 + along_z
                for child in range(8):
                    delta_x = along_x - 2 - child // 4
                    delta_y = along_y - 2 - child // 2 % 2
                    delta_z = along_z - 2 - child % 2
                    index_rows[row, child] = (delta_x + 3) * 49 + (delta_y + 3) * 7 + delta_z + 3
                    near = abs(delta_x) <= 1 and abs(delta_y) <= 1 and (abs(delta_z) <= 1)
                    keep_rows[row, child] = 0.0 if near else 1.0
    return (index_rows, keep_rows)

def translate(padded, out_table, in_table, transfer_level):
    width_x = padded.shape[0] - 4
    width_y = padded.shape[1] - 4
    width_z = padded.shape[2] - 4
    coeffs = padded.shape[3]
    parents = width_x // 2 * (width_y // 2) * (width_z // 2)
    stencil = jnp.stack([lax.slice_in_dim(padded, start, start + width_x - 1, 2, 0) for start in range(6)])
    stencil = jnp.stack([lax.slice_in_dim(stencil, start, start + width_y - 1, 2, 2) for start in range(6)], axis=1)
    stencil = jnp.stack([lax.slice_in_dim(stencil, start, start + width_z - 1, 2, 4) for start in range(6)], axis=2)
    stencil = stencil.reshape(8, 27, parents, coeffs)
    index_rows, keep_rows = offset_tables()
    flat = index_rows.reshape(-1)
    in_rows = jnp.take(in_table, flat, axis=0).reshape(8, 27, 8, coeffs) * jnp.asarray(keep_rows).reshape(8, 27, 8, 1)
    out_rows = jnp.take(out_table, flat, axis=0).reshape(8, 27, 8, coeffs)

    def add_block(block, total):
        sources = lax.dynamic_index_in_dim(stencil, block, 0, keepdims=False)
        scaled = lax.dynamic_index_in_dim(in_rows, block, 0, keepdims=False)
        outer = lax.dynamic_index_in_dim(out_rows, block, 0, keepdims=False)
        operand = (sources[:, None] * scaled[:, :, None, :]).astype(jnp.bfloat16)
        image = jnp.dot(operand.reshape(-1, coeffs), transfer_level, preferred_element_type=jnp.float32)
        image = image.reshape(27, 8, parents, coeffs) * outer[:, :, None, :]
        return total + lax.optimization_barrier(jnp.sum(image, axis=0))
    total = lax.fori_loop(0, 8, add_block, jnp.zeros((8, parents, coeffs), jnp.float32))
    total = total.reshape(2, 2, 2, width_x // 2, width_y // 2, width_z // 2, coeffs)
    return total.transpose(3, 0, 4, 1, 5, 2, 6).reshape(width_x, width_y, width_z, coeffs)

def phase_terms(place, wave_numbers, phases):
    centered = place - 0.5
    return phases + centered[0][..., None] * wave_numbers[0] + centered[1][..., None] * wave_numbers[1] + centered[2][..., None] * wave_numbers[2]

def lift(moments, upward_level):
    grid_x, grid_y, grid_z, coeffs = moments.shape
    children = moments.astype(jnp.bfloat16).reshape(grid_x // 2, 2, grid_y // 2, 2, grid_z // 2, 2, coeffs)
    children = children.transpose(0, 2, 4, 1, 3, 5, 6).reshape(-1, 8 * coeffs)
    parent = jnp.dot(children, upward_level.reshape(8 * coeffs, coeffs), preferred_element_type=jnp.float32)
    return parent.reshape(grid_x // 2, grid_y // 2, grid_z // 2, coeffs)

def descend(local, downward_level):
    grid_x, grid_y, grid_z, coeffs = local.shape
    table = downward_level.transpose(1, 0, 2).reshape(coeffs, 8 * coeffs)
    spread = jnp.dot(local.reshape(-1, coeffs), table, preferred_element_type=jnp.float32)
    spread = spread.reshape(grid_x, grid_y, grid_z, 2, 2, 2, coeffs).transpose(0, 3, 1, 4, 2, 5, 6)
    return spread.reshape(2 * grid_x, 2 * grid_y, 2 * grid_z, coeffs)

def far_field(moments, out_table, in_table, transfer_level):
    grid_x, grid_y, grid_z, coeffs = moments.shape
    padded = jnp.pad(moments, ((2, 2), (2, 2), (2, 2), (0, 0)), mode='wrap')

    def slab(start):
        piece = lax.dynamic_slice_in_dim(padded, start * 2, 6, 0)
        return translate(piece, out_table, in_table, transfer_level)
    slabs = lax.map(slab, jnp.arange(grid_x // 2, dtype=jnp.int32))
    return slabs.reshape(grid_x, grid_y, grid_z, coeffs)

def reference(features, positions, box_counts, w_hidden, w_charge, wave_numbers, phases, upward, downward, transfer, out_scale, in_scale):
    place_rows = positions.transpose(1, 0, 2, 3)

    def leaf_row(row):
        feats_row, place_row, count_row = row
        hidden = jax.nn.silu(jnp.dot(feats_row.reshape(-1, F), w_hidden, preferred_element_type=jnp.float32)).astype(jnp.bfloat16)
        charge = jnp.dot(hidden, w_charge, preferred_element_type=jnp.float32).reshape(NBY, NBZ * SLOTS)
        slot_index = jnp.arange(NBZ * SLOTS, dtype=jnp.int32) % SLOTS
        live = (slot_index[None, :] < jnp.repeat(count_row, SLOTS, axis=1)).astype(jnp.float32)
        charge = charge * live
        angle = phase_terms(place_row, wave_numbers, phases)
        moments = (charge[..., None] * jnp.cos(angle)).reshape(NBY, NBZ, SLOTS, P_SIZE).sum(axis=2)
        return (charge, moments)
    charges, moment_leaf = lax.map(leaf_row, (features, place_rows, box_counts))
    moment_mid = lift(moment_leaf, upward[0])
    moment_top = lift(moment_mid, upward[1])
    local_top = far_field(moment_top, out_scale[2], in_scale[2], transfer[2]).astype(jnp.bfloat16)
    local_mid = (far_field(moment_mid, out_scale[1], in_scale[1], transfer[1]) + descend(local_top, downward[1])).astype(jnp.bfloat16)
    local_leaf = far_field(moment_leaf, out_scale[0], in_scale[0], transfer[0]) + descend(local_mid, downward[0])

    def force_row(row):
        place_row, charge_row, local_row = row
        angle = phase_terms(place_row, wave_numbers, phases)
        weight = (charge_row[..., None] * jnp.sin(angle)).reshape(NBY, NBZ, SLOTS, P_SIZE) * local_row[:, :, None, :]
        result = jnp.einsum('yzsk,dk->dyzs', weight, wave_numbers, precision=lax.Precision.HIGHEST)
        return result.reshape(3, NBY, NBZ * SLOTS)
    forces = lax.map(force_row, (place_rows, charges, local_leaf)).transpose(1, 0, 2, 3)
    place_x = (jnp.arange(NBX, dtype=jnp.float32)[:, None, None] + positions[0]) / NBX
    place_y = (jnp.arange(NBY, dtype=jnp.float32)[None, :, None] + positions[1]) / NBY
    box_z = (jnp.arange(NBZ * SLOTS, dtype=jnp.int32) // SLOTS).astype(jnp.float32)
    place_z = (box_z[None, None, :] + positions[2]) / NBZ
    place = jnp.stack([place_x, place_y, place_z])
    virial = jnp.einsum('dxyn,exyn->de', place, forces, precision=lax.Precision.HIGHEST) * (1.0 / math.sqrt(ATOMS))
    return (forces, virial)
```

```python
import math

import jax
import jax.numpy as jnp
import numpy as np
from jax import lax
from jax.experimental import pallas as pl
from jax.experimental.pallas import tpu as pltpu
from jax.sharding import PartitionSpec as P

F32 = jnp.float32
BF16 = jnp.bfloat16
TURN = 1.0 / (2.0 * math.pi)
SIN_HALF = (4.4428679, -7.30744342, 3.59478808, -0.78437403)
COS_HALF = (1.4142135, -6.97885099, 5.73946117, -1.88356299, 0.31069819)
NT = (((1,), (1,)), ((), ()))
VMEM = pl.BlockSpec(memory_space=pltpu.VMEM)


def dot(a, b):
    return jnp.dot(a, b, preferred_element_type=F32)


def atoms_kernel(
    feat_hbm, pos_hbm, cnt_ref, wh_hbm, wc_ref, wave_ref, ph_ref, up_hbm,
    charge_ref, sin_ref, leaf_ref, mid_ref, top_ref, sa_ref, sb_ref,
    feat_ref, pos_ref, wh_ref, up_ref, cols_ref, cos_ref, low_ref, plane_sems, sems,
):
    def plane(x):
        return pltpu.make_async_copy(feat_hbm.at[x], feat_ref.at[x], plane_sems.at[x])

    others = [
        pltpu.make_async_copy(wh_hbm, wh_ref, sems.at[0]),
        pltpu.make_async_copy(pos_hbm, pos_ref, sems.at[1]),
        pltpu.make_async_copy(up_hbm, up_ref, sems.at[2]),
    ]
    plane(0).start()
    others[0].start()
    others[1].start()
    for x in range(1, 8):
        plane(x).start()
    others[2].start()

    table = jnp.concatenate(
        [wave_ref[...] * TURN, ph_ref[...] * TURN, jnp.zeros((4, 128), F32)], axis=0
    )
    columns = jnp.concatenate([table] * 16, axis=0).T
    for d in range(4):
        cols_ref[d] = jnp.broadcast_to(columns[:, d : d + 1], (128, 128))
    others[0].wait()
    others[1].wait()

    @pl.loop(0, 8)
    def _(x):
        plane(x).wait()
        atoms_plane(
            x, feat_ref, pos_ref, cnt_ref, wh_ref, wc_ref, charge_ref, sin_ref, leaf_ref,
            cols_ref, cos_ref, low_ref,
        )

    others[2].wait()
    atoms_lift(leaf_ref, up_ref, mid_ref, top_ref, sa_ref, sb_ref)


def atoms_plane(
    step, feat_ref, pos_ref, cnt_ref, wh_ref, wc_ref, charge_ref, sin_ref, leaf_ref,
    cols_ref, cos_ref, low_ref,
):
    lane_box = lax.broadcasted_iota(jnp.int32, (8, 128), 1) // 32
    lane_slot = lax.broadcasted_iota(jnp.int32, (8, 128), 1) % 32
    row_y = lax.broadcasted_iota(jnp.int32, (8, 128), 0)
    counts = jnp.zeros((8, 128), jnp.int32)
    columns = cnt_ref[step].T
    for z in range(4):
        counts = jnp.where(
            lane_box == z, jnp.broadcast_to(columns[:, z : z + 1], (8, 128)), counts
        )
    live = jnp.where(lane_slot < counts, 1.0, 0.0).astype(F32)

    hidden = dot(feat_ref[step].reshape(1024, 128), wh_ref[...])
    half = hidden * 0.5
    hidden = (half + half * jnp.tanh(half)).astype(BF16)
    wc = jnp.broadcast_to(wc_ref[...], (8, 128))
    raw = lax.dot_general(wc, hidden, NT, preferred_element_type=F32)
    charge = jnp.zeros((8, 128), F32)
    for y in range(8):
        charge = jnp.where(row_y == y, raw[:, y * 128 : (y + 1) * 128], charge)
    charge = charge * live
    charge_ref[step] = charge

    spread = []
    for z in range(4):
        spread.append(
            jnp.concatenate(
                [
                    jnp.where((row_y == y) & (lane_box == z), charge, 0.0)
                    for y in range(8)
                ],
                axis=1,
            )
        )
    spread = jnp.concatenate(spread, axis=0)
    spread_high = spread.astype(BF16)
    spread_low = (spread - spread_high.astype(F32)).astype(BF16)

    for y in range(8):
        p0 = pos_ref[0, step, y : y + 1, :] - 0.5
        p1 = pos_ref[1, step, y : y + 1, :] - 0.5
        p2 = pos_ref[2, step, y : y + 1, :] - 0.5
        turns = cols_ref[3] + cols_ref[0] * p0 + cols_ref[1] * p1 + cols_ref[2] * p2
        r = turns - jnp.round(turns)
        u = r * r
        s = SIN_HALF[3]
        for coef in SIN_HALF[2::-1]:
            s = s * u + coef
        s = s * r
        c = COS_HALF[4]
        for coef in COS_HALF[3::-1]:
            c = c * u + coef
        cosine = 1.0 - s * s
        cosine_high = cosine.astype(BF16)
        cos_ref[:, y * 128 : (y + 1) * 128] = cosine_high
        low_ref[:, y * 128 : (y + 1) * 128] = (cosine - cosine_high.astype(F32)).astype(BF16)
        sin_ref[step, :, y * 128 : (y + 1) * 128] = (s * c).astype(BF16)
    moments = lax.dot_general(
        jnp.concatenate([spread_high, spread_low], axis=0), cos_ref[...], NT,
        preferred_element_type=F32,
    )
    fine = lax.dot_general(spread_high, low_ref[...], NT, preferred_element_type=F32)
    moments = moments[0:32] + (moments[32:64] + fine)
    for z in range(4):
        leaf_ref[step, z] = moments[z * 8 : (z + 1) * 8]


def atoms_lift(leaf_ref, up_ref, mid_ref, top_ref, sa_ref, sb_ref):
    total = jnp.zeros((32, 128), F32)
    for child in range(8):
        cx, cy, cz = child // 4, child // 2 % 2, child % 2
        rows = jnp.concatenate(
            [
                leaf_ref[2 * x + cx, 2 * z + cz, pl.ds(cy, 4, stride=2), :]
                for x in range(4)
                for z in range(2)
            ],
            axis=0,
        )
        total = total + dot(rows.astype(BF16), up_ref[0, child])
    for x in range(4):
        for z in range(2):
            for y in range(4):
                row = (x * 2 + z) * 4 + y
                mid_ref[x, y, z : z + 1, :] = total[row : row + 1]
    crown = jnp.zeros((8, 128), F32)
    for child in range(8):
        cx, cy, cz = child // 4, child // 2 % 2, child % 2
        rows = jnp.concatenate(
            [
                mid_ref[2 * x + cx, 2 * y + cy, cz : cz + 1, :]
                for x in range(2)
                for y in range(2)
            ]
            + [jnp.zeros((4, 128), F32)],
            axis=0,
        )
        crown = crown + dot(rows.astype(BF16), up_ref[1, child])
    top_ref[...] = crown[0:4]
    odd = lax.axis_index("gx") % 2
    for ref, high in ((sa_ref, 1 - odd), (sb_ref, odd)):
        for x in range(2):
            for z in range(4):
                row = (x * 4 + z) * 8
                ref[row : row + 8, :] = leaf_ref[high * 6 + x, z]
            for y in range(4):
                row = 64 + (x * 4 + y) * 2
                ref[row : row + 2, :] = mid_ref[high * 2 + x, y]
        ref[80:84, :] = crown[0:4]
        ref[84:88, :] = jnp.zeros((4, 128), F32)


def run_atoms(features, positions, box_counts, w_hidden, w_charge, wave, phases, upward):
    hbm = pl.BlockSpec(memory_space=pltpu.HBM)
    return pl.pallas_call(
        atoms_kernel,
        in_specs=[hbm, hbm, VMEM, hbm, VMEM, VMEM, VMEM, hbm],
        out_specs=[VMEM] * 7,
        out_shape=[
            jax.ShapeDtypeStruct((8, 8, 128), F32),
            jax.ShapeDtypeStruct((8, 128, 1024), BF16),
            jax.ShapeDtypeStruct((8, 4, 8, 128), F32),
            jax.ShapeDtypeStruct((4, 4, 2, 128), F32),
            jax.ShapeDtypeStruct((4, 128), F32),
            jax.ShapeDtypeStruct((88, 128), F32),
            jax.ShapeDtypeStruct((88, 128), F32),
        ],
        scratch_shapes=[
            pltpu.VMEM((8, 8, 128, 128), BF16),
            pltpu.VMEM((3, 8, 8, 128), F32),
            pltpu.VMEM((128, 128), BF16),
            pltpu.VMEM((2, 8, 128, 128), BF16),
            pltpu.VMEM((4, 128, 128), F32),
            pltpu.VMEM((128, 1024), BF16),
            pltpu.VMEM((128, 1024), BF16),
            pltpu.SemaphoreType.DMA((8,)),
            pltpu.SemaphoreType.DMA((3,)),
        ],
        compiler_params=pltpu.CompilerParams(vmem_limit_bytes=58 << 20),
        name="atoms",
    )(features, positions, box_counts, w_hidden, w_charge, wave, phases, upward)


def glue_x_kernel(ra_ref, rb_ref, leaf_ref, mid_ref, top_ref, leafx_ref, midx_ref, topx_ref, ya_ref, yb_ref):
    odd = lax.axis_index("gx") % 2
    leafx_ref[2:10] = leaf_ref[...]
    midx_ref[2:6] = mid_ref[...]
    for ref, high in ((ra_ref, 1 - odd), (rb_ref, odd)):
        for x in range(2):
            for z in range(4):
                row = (x * 4 + z) * 8
                leafx_ref[high * 10 + x, z] = ref[row : row + 8, :]
            for y in range(4):
                row = 64 + (x * 4 + y) * 2
                midx_ref[high * 6 + x, y] = ref[row : row + 2, :]
    ta, tb = ra_ref[80:84, :], rb_ref[80:84, :]
    topx_ref[...] = jnp.concatenate(
        [
            jnp.where(odd == 1, ta, tb),
            top_ref[...],
            jnp.where(odd == 1, tb, ta),
            jnp.zeros((4, 128), F32),
        ],
        axis=0,
    )
    odd_y = lax.axis_index("gy") % 2
    for x in range(12):
        for z in range(4):
            tile = leafx_ref[x, z]
            low, high = tile[0:2], tile[6:8]
            row = (x * 4 + z) * 2
            ya_ref[row : row + 2, :] = jnp.where(odd_y == 1, low, high)
            yb_ref[row : row + 2, :] = jnp.where(odd_y == 1, high, low)
    for ref, side in ((ya_ref, 1 - odd_y), (yb_ref, odd_y)):
        for x in range(8):
            for y in range(2):
                row = 96 + (x * 2 + y) * 2
                ref[row : row + 2, :] = midx_ref[x, side * 2 + y]
        ref[128:144, :] = topx_ref[...]


def glue_x(ra, rb, leaf, mid, top):
    return pl.pallas_call(
        glue_x_kernel,
        in_specs=[VMEM] * 5,
        out_specs=[VMEM] * 5,
        out_shape=[
            jax.ShapeDtypeStruct((12, 4, 8, 128), F32),
            jax.ShapeDtypeStruct((8, 4, 2, 128), F32),
            jax.ShapeDtypeStruct((16, 128), F32),
            jax.ShapeDtypeStruct((144, 128), F32),
            jax.ShapeDtypeStruct((144, 128), F32),
        ],
        compiler_params=pltpu.CompilerParams(vmem_limit_bytes=8 << 20),
        name="glue_x",
    )(ra, rb, leaf, mid, top)


def glue_y_kernel(ra_ref, rb_ref, leafx_ref, midx_ref, topx_ref, leafxy_ref, midxy_ref, topxy_ref, za_ref, zb_ref):
    odd = lax.axis_index("gy") % 2
    for x in range(12):
        for z in range(4):
            row = (x * 4 + z) * 2
            a, b = ra_ref[row : row + 2, :], rb_ref[row : row + 2, :]
            leafxy_ref[x, z, 0:2, :] = jnp.where(odd == 1, a, b)
            leafxy_ref[x, z, 2:10, :] = leafx_ref[x, z]
            leafxy_ref[x, z, 10:12, :] = jnp.where(odd == 1, b, a)
    for x in range(8):
        midxy_ref[x, 2:6] = midx_ref[x]
        for ref, high in ((ra_ref, 1 - odd), (rb_ref, odd)):
            for y in range(2):
                row = 96 + (x * 2 + y) * 2
                midxy_ref[x, high * 6 + y] = ref[row : row + 2, :]
    for x in range(6):
        row = 128 + x * 2
        a, b = ra_ref[row : row + 2, :], rb_ref[row : row + 2, :]
        topxy_ref[x * 6 : x * 6 + 2, :] = jnp.where(odd == 1, a, b)
        topxy_ref[x * 6 + 2 : x * 6 + 4, :] = topx_ref[x * 2 : x * 2 + 2, :]
        topxy_ref[x * 6 + 4 : x * 6 + 6, :] = jnp.where(odd == 1, b, a)
    topxy_ref[36:40, :] = jnp.zeros((4, 128), F32)
    odd_z = lax.axis_index("gz") % 2
    for ref, side in ((za_ref, 1 - odd_z), (zb_ref, odd_z)):
        for x in range(12):
            for z in range(2):
                row = (x * 2 + z) * 12
                ref[row : row + 12, :] = leafxy_ref[x, side * 2 + z]
        for x in range(8):
            for y in range(8):
                row = 288 + (x * 8 + y) * 2
                ref[row : row + 2, :] = midxy_ref[x, y]
    za_ref[416:456, :] = topxy_ref[...]


def glue_y(ra, rb, leafx, midx, topx):
    return pl.pallas_call(
        glue_y_kernel,
        in_specs=[VMEM] * 5,
        out_specs=[VMEM] * 5,
        out_shape=[
            jax.ShapeDtypeStruct((12, 4, 12, 128), F32),
            jax.ShapeDtypeStruct((8, 8, 2, 128), F32),
            jax.ShapeDtypeStruct((40, 128), F32),
            jax.ShapeDtypeStruct((456, 128), F32),
            jax.ShapeDtypeStruct((416, 128), F32),
        ],
        compiler_params=pltpu.CompilerParams(vmem_limit_bytes=8 << 20),
        name="glue_y",
    )(ra, rb, leafx, midx, topx)


def glue_z_kernel(ra_ref, topxy_ref, pair_ref):
    odd = lax.axis_index("gz") % 2
    mine, other = topxy_ref[0:36, :], ra_ref[416:452, :]
    pair_ref[...] = jnp.concatenate(
        [jnp.where(odd == 1, other, mine), jnp.where(odd == 1, mine, other)], axis=0
    )


def glue_z(ra, topxy):
    return pl.pallas_call(
        glue_z_kernel,
        in_specs=[VMEM] * 2,
        out_specs=VMEM,
        out_shape=jax.ShapeDtypeStruct((72, 128), F32),
        compiler_params=pltpu.CompilerParams(vmem_limit_bytes=8 << 20),
        name="glue_z",
    )(ra, topxy)


def block_diagonal(core):
    zero = jnp.zeros((128, 128), BF16)
    return jnp.concatenate(
        [jnp.concatenate([core, zero], axis=1), jnp.concatenate([zero, core], axis=1)], axis=0
    )


def offset_tiles(out_ref, table, cz, masked):
    zero = jnp.zeros((2, 128), F32)
    keep_rows = lax.broadcasted_iota(jnp.int32, (8, 128), 0)
    near = (keep_rows >= 1 + cz) & (keep_rows <= 3 + cz)
    for xy in range(49):
        start = xy * 7 + 1 - cz
        tile = jnp.concatenate([table[start : start + 6, :], zero], axis=0)
        if masked and 2 <= xy // 7 <= 4 and 2 <= xy % 7 <= 4:
            tile = jnp.where(near, 0.0, tile)
        out_ref[xy] = tile


def far_kernel(
    leafxy_ref, midxy_ref, ra_ref, rb_ref, in_ref, out_ref, core_ref,
    far0_ref, far1_ref,
    leaf_ref, mid_ref, scale_ref, tin_ref, tout_ref, acc_ref,
):
    odd = lax.axis_index("gz") % 2
    leaf_ref[:, 2:6] = leafxy_ref[...]
    for ref, high in ((ra_ref, 1 - odd), (rb_ref, odd)):
        for x in range(12):
            for z in range(2):
                row = (x * 2 + z) * 12
                leaf_ref[x, high * 6 + z] = ref[row : row + 12, :]
    for x in range(8):
        for y in range(8):
            row = 288 + (x * 8 + y) * 2
            a, b = ra_ref[row : row + 2, :], rb_ref[row : row + 2, :]
            mid_ref[x, y] = jnp.concatenate(
                [
                    jnp.where(odd == 1, a, b),
                    midxy_ref[x, y],
                    jnp.where(odd == 1, b, a),
                    jnp.zeros((2, 128), F32),
                ],
                axis=0,
            )
    scale_ref[...] = in_ref[0]
    for x in range(2, 5):
        for y in range(2, 5):
            row = x * 49 + y * 7 + 2
            scale_ref[row : row + 3, :] = jnp.zeros((3, 128), F32)
    for cz in range(2):
        offset_tiles(tin_ref.at[cz], in_ref.at[1], cz, True)
        offset_tiles(tout_ref.at[cz], out_ref.at[1], cz, False)

    far0_ref[...] = jnp.zeros((8, 32, 128), F32)
    core0 = block_diagonal(core_ref[0])

    @pl.loop(0, 36)
    def _(step):
        qx, qz = step // 6, step % 6
        blocks = []
        for qy in range(6):
            tiles = []
            for x in range(4):
                for z in range(2):
                    tiles.append(leaf_ref[2 * x + qx, 2 * z + qz, pl.ds(qy, 4, stride=2), :])
            source = jnp.concatenate(tiles, axis=0)
            for pair in range(4):
                cx, cy = pair // 2, pair % 2
                halves = []
                for cz in range(2):
                    row = (qx + 1 - cx) * 49 + (qy + 1 - cy) * 7 + qz + 1 - cz
                    scale = jnp.broadcast_to(scale_ref[pl.ds(row, 1), :], (32, 128))
                    halves.append((source * scale).astype(BF16))
                blocks.append(jnp.concatenate(halves, axis=1))
        image = dot(jnp.concatenate(blocks, axis=0), core0)
        for pair in range(4):
            cx, cy = pair // 2, pair % 2
            for cz in range(2):
                total = far0_ref[pair * 2 + cz]
                for qy in range(6):
                    row = (qx + 1 - cx) * 49 + (qy + 1 - cy) * 7 + qz + 1 - cz
                    scale = jnp.broadcast_to(out_ref[0, pl.ds(row, 1), :], (32, 128))
                    start = (qy * 4 + pair) * 32
                    total = total + scale * image[start : start + 32, cz * 128 : cz * 128 + 128]
                far0_ref[pair * 2 + cz] = total

    acc_ref[...] = jnp.zeros((8, 32, 128), F32)
    core1 = block_diagonal(core_ref[1])

    @pl.loop(0, 6)
    def _(qx):
        blocks = []
        for qy in range(6):
            tiles = [mid_ref[2 * x + qx, 2 * y + qy] for x in range(2) for y in range(2)]
            for pair in range(4):
                cx, cy = pair // 2, pair % 2
                xy = (qx + 1 - cx) * 7 + qy + 1 - cy
                halves = []
                for cz in range(2):
                    scale = tin_ref[cz, xy]
                    halves.append(
                        jnp.concatenate([tile * scale for tile in tiles], axis=0).astype(BF16)
                    )
                blocks.append(jnp.concatenate(halves, axis=1))
        image = dot(jnp.concatenate(blocks, axis=0), core1)
        for pair in range(4):
            cx, cy = pair // 2, pair % 2
            for cz in range(2):
                total = acc_ref[pair * 2 + cz]
                for qy in range(6):
                    scale = tout_ref[cz, (qx + 1 - cx) * 7 + qy + 1 - cy]
                    scale = jnp.concatenate([scale] * 4, axis=0)
                    start = (qy * 4 + pair) * 32
                    total = total + scale * image[start : start + 32, cz * 128 : cz * 128 + 128]
                acc_ref[pair * 2 + cz] = total

    for child in range(8):
        for parent in range(4):
            tile = acc_ref[child, parent * 8 : parent * 8 + 8, :]
            far1_ref[child * 4 + parent : child * 4 + parent + 1, :] = jnp.sum(
                tile, axis=0, keepdims=True
            )


def run_far(leafxy, midxy, ra, rb, in_scale, out_scale, transfer):
    return pl.pallas_call(
        far_kernel,
        in_specs=[VMEM] * 7,
        out_specs=[VMEM] * 2,
        out_shape=[
            jax.ShapeDtypeStruct((8, 32, 128), F32),
            jax.ShapeDtypeStruct((32, 128), F32),
        ],
        scratch_shapes=[
            pltpu.VMEM((12, 8, 12, 128), F32),
            pltpu.VMEM((8, 8, 8, 128), F32),
            pltpu.VMEM((343, 128), F32),
            pltpu.VMEM((2, 49, 8, 128), F32),
            pltpu.VMEM((2, 49, 8, 128), F32),
            pltpu.VMEM((8, 32, 128), F32),
        ],
        cost_estimate=pl.CostEstimate(flops=4 << 30, bytes_accessed=4 << 20, transcendentals=0),
        compiler_params=pltpu.CompilerParams(vmem_limit_bytes=24 << 20),
        name="far",
    )(leafxy, midxy, ra, rb, in_scale, out_scale, transfer)


def force_kernel(
    far0_ref, far1_ref, pair_ref, near_ref, next_ref, in_ref, out_ref, core_ref, down_ref,
    charge_ref, sin_ref, pos_ref, wave_ref,
    forces_ref, share_ref,
    window_ref, tin_ref, tout_ref, operand_ref, mid_ref, local_ref,
):
    odd = lax.axis_index("gz") % 2
    for xy in range(36):
        rows = [
            (ref[xy : xy + 1, :], ref[36 + xy : 37 + xy, :]) for ref in (near_ref, next_ref)
        ]
        low = [jnp.where(odd == 1, rows[1][z], rows[0][z]) for z in range(2)]
        high = [jnp.where(odd == 1, rows[0][z], rows[1][z]) for z in range(2)]
        window_ref[xy] = jnp.concatenate(
            low
            + [pair_ref[xy : xy + 1, :], pair_ref[36 + xy : 37 + xy, :]]
            + high
            + [jnp.zeros((2, 128), F32)],
            axis=0,
        )
    lanes = lax.broadcasted_iota(jnp.int32, (8, 128), 0)
    near = (lanes >= 1 + odd) & (lanes <= 3 + odd)
    for xy in range(49):
        for ref, table, masked in ((tin_ref, in_ref, True), (tout_ref, out_ref, False)):
            rows = table[2, xy * 7 : xy * 7 + 7, :]
            tile = jnp.where(odd == 1, rows[0:6], rows[1:7])
            tile = jnp.concatenate([tile, jnp.zeros((2, 128), F32)], axis=0)
            if masked and 2 <= xy // 7 <= 4 and 2 <= xy % 7 <= 4:
                tile = jnp.where(near, 0.0, tile)
            ref[xy] = tile
    for qx in range(6):
        for qy in range(6):
            source = window_ref[qx * 6 + qy]
            tiles = []
            for pair in range(4):
                cx, cy = pair // 2, pair % 2
                tiles.append(source * tin_ref[(qx + 1 - cx) * 7 + qy + 1 - cy])
            start = (qx * 6 + qy) * 32
            operand_ref[start : start + 32, :] = jnp.concatenate(tiles, axis=0).astype(BF16)
    totals = [jnp.zeros((8, 128), F32) for _ in range(4)]
    for qx in range(6):
        image = dot(operand_ref[qx * 192 : qx * 192 + 192, :], core_ref[2])
        for qy in range(6):
            for pair in range(4):
                cx, cy = pair // 2, pair % 2
                scale = tout_ref[(qx + 1 - cx) * 7 + qy + 1 - cy]
                start = qy * 32 + pair * 8
                totals[pair] = totals[pair] + scale * image[start : start + 8]
    local_top = jnp.concatenate(
        [jnp.sum(total, axis=0, keepdims=True) for total in totals] + [jnp.zeros((4, 128), F32)],
        axis=0,
    ).astype(BF16)
    for child in range(8):
        cx, cy, cz = child // 4, child // 2 % 2, child % 2
        rows = far1_ref[child * 4 : child * 4 + 4, :] + dot(local_top, down_ref[1, child])[0:4]
        for parent in range(4):
            row = ((2 * (parent // 2) + cx) * 2 + cz) * 4 + 2 * (parent % 2) + cy
            mid_ref[row : row + 1, :] = rows[parent : parent + 1]
    local_mid = mid_ref[...].astype(BF16)
    for child in range(8):
        cx, cy, cz = child // 4, child // 2 % 2, child % 2
        rows = far0_ref[child] + dot(local_mid, down_ref[0, child])
        for x in range(4):
            for z in range(2):
                start = (x * 2 + z) * 4
                local_ref[2 * x + cx, 2 * z + cz, pl.ds(cy, 4, stride=2), :] = rows[start : start + 4]

    lane_box = lax.broadcasted_iota(jnp.int32, (8, 128), 1) // 32
    row_y = lax.broadcasted_iota(jnp.int32, (8, 128), 0)
    base_x = lax.axis_index("gx") * 8
    base_y = lax.axis_index("gy") * 8
    base_z = lax.axis_index("gz") * 4
    place_y0 = (base_y + row_y).astype(F32)
    place_z0 = (base_z + lane_box).astype(F32)

    def one_plane(x, sums):
        local = local_ref[x].reshape(32, 128)
        weights = jnp.concatenate([local * wave_ref[d : d + 1, :] for d in range(3)], axis=0)
        high = weights.astype(BF16)
        low = (weights - high.astype(F32)).astype(BF16)
        sines = sin_ref[x]
        product = dot(
            jnp.concatenate([high, low], axis=1), jnp.concatenate([sines, sines], axis=0)
        )
        charge = charge_ref[x]
        found = []
        for d in range(3):
            picked = jnp.zeros((8, 128), F32)
            for z in range(4):
                start = (d * 4 + z) * 8
                for y in range(8):
                    picked = jnp.where(
                        (row_y == y) & (lane_box == z),
                        product[start : start + 8, y * 128 : y * 128 + 128],
                        picked,
                    )
            picked = picked * charge
            forces_ref[d, x] = picked
            found.append(picked)
        places = (
            ((base_x + x).astype(F32) + pos_ref[0, x]) * (1.0 / 32),
            (place_y0 + pos_ref[1, x]) * (1.0 / 64),
            (place_z0 + pos_ref[2, x]) * (1.0 / 64),
        )
        return tuple(
            sums[d * 3 + e] + places[d] * found[e] for d in range(3) for e in range(3)
        )

    sums = lax.fori_loop(0, 8, one_plane, (jnp.zeros((8, 128), F32),) * 9)
    lane = lax.broadcasted_iota(jnp.int32, (8, 128), 1)
    row = jnp.zeros((8, 128), F32)
    for i in range(9):
        row = jnp.where(lane == i, jnp.sum(sums[i]), row)
    share_ref[...] = jnp.broadcast_to(row[0:1], (512, 128))


def run_forces(far0, far1, pair, near, following, in_scale, out_scale, transfer, downward, charge, sines, positions, wave):
    return pl.pallas_call(
        force_kernel,
        in_specs=[VMEM] * 13,
        out_specs=[VMEM] * 2,
        out_shape=[
            jax.ShapeDtypeStruct((3, 8, 8, 128), F32),
            jax.ShapeDtypeStruct((512, 128), F32),
        ],
        scratch_shapes=[
            pltpu.VMEM((36, 8, 128), F32),
            pltpu.VMEM((49, 8, 128), F32),
            pltpu.VMEM((49, 8, 128), F32),
            pltpu.VMEM((1152, 128), BF16),
            pltpu.VMEM((32, 128), F32),
            pltpu.VMEM((8, 4, 8, 128), F32),
        ],
        compiler_params=pltpu.CompilerParams(vmem_limit_bytes=24 << 20),
        name="forces",
    )(far0, far1, pair, near, following, in_scale, out_scale, transfer, downward, charge, sines, positions, wave)


def virial_kernel(scale, rows_ref, virial_ref):
    row = jnp.sum(rows_ref[...], axis=0, keepdims=True) * scale
    for d in range(3):
        virial_ref[d : d + 1, :] = row[:, d * 3 : d * 3 + 3]


def run_virial(rows, scale):
    return pl.pallas_call(
        lambda rows_ref, virial_ref: virial_kernel(scale, rows_ref, virial_ref),
        in_specs=[VMEM],
        out_specs=VMEM,
        out_shape=jax.ShapeDtypeStruct((3, 3), F32),
        compiler_params=pltpu.CompilerParams(vmem_limit_bytes=8 << 20),
        name="virial",
    )(rows)


def swapped(value, axis, kind):
    count = lax.axis_size(axis)
    pairs = []
    for i in range(count):
        hop = (1, -1, 3)[kind]
        pairs.append((i, (i + hop) % count if i % 2 == 0 else (i - hop) % count))
    return lax.ppermute(value, axis, pairs)


def shards(
    features, positions, box_counts, w_hidden, w_charge, wave_numbers, phases,
    upward, downward, transfer, out_scale, in_scale,
):
    charge, sines, leaf, mid, top, xa, xb = run_atoms(
        features, positions, box_counts.transpose(0, 2, 1), w_hidden, w_charge.reshape(1, 128), wave_numbers,
        phases.reshape(1, 128), upward,
    )
    ra, rb = swapped(xa, "gx", 0), swapped(xb, "gx", 1)
    leaf, mid, top, ya, yb = glue_x(ra, rb, leaf, mid, top)
    ra, rb = swapped(ya, "gy", 0), swapped(yb, "gy", 1)
    leaf, mid, top, za, zb = glue_y(ra, rb, leaf, mid, top)
    ra, rb = swapped(za, "gz", 0), swapped(zb, "gz", 1)
    pair = glue_z(ra, top)
    near, following = swapped(pair, "gz", 1), swapped(pair, "gz", 2)
    far0, far1 = run_far(leaf, mid, ra, rb, in_scale, out_scale, transfer)
    forces, share = run_forces(
        far0, far1, pair, near, following, in_scale, out_scale, transfer, downward, charge, sines,
        positions, wave_numbers,
    )
    rows = lax.all_to_all(share, ("gx", "gy", "gz"), 0, 0, tiled=True)
    return forces, run_virial(rows, 1.0 / math.sqrt(4194304))


def solution(mesh):
    in_specs = (
        P("gx", "gy", "gz", None),
        P(None, "gx", "gy", "gz"),
        P("gx", "gy", "gz"),
    ) + (P(),) * 9
    out_specs = (P(None, "gx", "gy", "gz"), P())
    return jax.shard_map(shards, mesh=mesh, in_specs=in_specs, out_specs=out_specs, check_vma=False)
```

```python
import math

import jax
import jax.numpy as jnp
import numpy as np
from jax import lax
from jax.experimental import pallas as pl
from jax.experimental.pallas import tpu as pltpu
from jax.sharding import PartitionSpec as P

F32 = jnp.float32
BF16 = jnp.bfloat16
TURN = 1.0 / (2.0 * math.pi)
SIN_HALF = (4.4428679, -7.30744342, 3.59478808, -0.78437403)
COS_HALF = (1.4142135, -6.97885099, 5.73946117, -1.88356299, 0.31069819)
NT = (((1,), (1,)), ((), ()))
VMEM = pl.BlockSpec(memory_space=pltpu.VMEM)


def dot(a, b):
    return jnp.dot(a, b, preferred_element_type=F32)


def atoms_kernel(
    feat_hbm, pos_hbm, cnt_ref, wh_hbm, wc_ref, wave_ref, ph_ref, up_hbm,
    charge_ref, sin_hbm, own_ref, send_ref,
    feat_ref, pos_ref, wh_ref, up_ref, cols_ref, cos_ref, low_ref, sin_ref, leaf_ref, mid_ref,
    plane_sems, sin_sems, sems,
):
    def plane(x):
        return pltpu.make_async_copy(feat_hbm.at[x], feat_ref.at[x], plane_sems.at[x])

    others = [
        pltpu.make_async_copy(wh_hbm, wh_ref, sems.at[0]),
        pltpu.make_async_copy(pos_hbm, pos_ref, sems.at[1]),
        pltpu.make_async_copy(up_hbm, up_ref, sems.at[2]),
    ]
    plane(0).start()
    others[0].start()
    others[1].start()
    for x in range(1, 8):
        plane(x).start()
    others[2].start()

    table = jnp.concatenate(
        [wave_ref[...] * TURN, ph_ref[...] * TURN, jnp.zeros((4, 128), F32)], axis=0
    )
    columns = jnp.concatenate([table] * 16, axis=0).T
    for d in range(4):
        cols_ref[d] = jnp.broadcast_to(columns[:, d : d + 1], (128, 128))
    others[0].wait()
    others[1].wait()

    @pl.loop(0, 8)
    def _(x):
        plane(x).wait()
        atoms_plane(
            x, feat_ref, pos_ref, cnt_ref, wh_ref, wc_ref, charge_ref, sin_ref, leaf_ref,
            cols_ref, cos_ref, low_ref,
        )
        pltpu.make_async_copy(sin_ref.at[x], sin_hbm.at[x], sin_sems.at[x]).start()

    others[2].wait()
    atoms_lift(leaf_ref, up_ref, mid_ref, own_ref, send_ref)
    for x in range(8):
        pltpu.make_async_copy(sin_ref.at[x], sin_hbm.at[x], sin_sems.at[x]).wait()


def atoms_plane(
    step, feat_ref, pos_ref, cnt_ref, wh_ref, wc_ref, charge_ref, sin_ref, leaf_ref,
    cols_ref, cos_ref, low_ref,
):
    lane_box = lax.broadcasted_iota(jnp.int32, (8, 128), 1) // 32
    lane_slot = lax.broadcasted_iota(jnp.int32, (8, 128), 1) % 32
    row_y = lax.broadcasted_iota(jnp.int32, (8, 128), 0)
    counts = jnp.zeros((8, 128), jnp.int32)
    columns = cnt_ref[step].T
    for z in range(4):
        counts = jnp.where(
            lane_box == z, jnp.broadcast_to(columns[:, z : z + 1], (8, 128)), counts
        )
    live = jnp.where(lane_slot < counts, 1.0, 0.0).astype(F32)

    hidden = dot(feat_ref[step].reshape(1024, 128), wh_ref[...])
    half = hidden * 0.5
    hidden = (half + half * jnp.tanh(half)).astype(BF16)
    wc = jnp.broadcast_to(wc_ref[...], (8, 128))
    raw = lax.dot_general(wc, hidden, NT, preferred_element_type=F32)
    charge = jnp.zeros((8, 128), F32)
    for y in range(8):
        charge = jnp.where(row_y == y, raw[:, y * 128 : (y + 1) * 128], charge)
    charge = charge * live
    charge_ref[step] = charge

    spread = []
    for z in range(4):
        spread.append(
            jnp.concatenate(
                [
                    jnp.where((row_y == y) & (lane_box == z), charge, 0.0)
                    for y in range(8)
                ],
                axis=1,
            )
        )
    spread = jnp.concatenate(spread, axis=0)
    spread_high = spread.astype(BF16)
    spread_low = (spread - spread_high.astype(F32)).astype(BF16)

    for y in range(8):
        p0 = pos_ref[0, step, y : y + 1, :] - 0.5
        p1 = pos_ref[1, step, y : y + 1, :] - 0.5
        p2 = pos_ref[2, step, y : y + 1, :] - 0.5
        turns = cols_ref[3] + cols_ref[0] * p0 + cols_ref[1] * p1 + cols_ref[2] * p2
        r = turns - jnp.round(turns)
        u = r * r
        s = SIN_HALF[3]
        for coef in SIN_HALF[2::-1]:
            s = s * u + coef
        s = s * r
        c = COS_HALF[4]
        for coef in COS_HALF[3::-1]:
            c = c * u + coef
        cosine = 1.0 - s * s
        cosine_high = cosine.astype(BF16)
        cos_ref[:, y * 128 : (y + 1) * 128] = cosine_high
        low_ref[:, y * 128 : (y + 1) * 128] = (cosine - cosine_high.astype(F32)).astype(BF16)
        sin_ref[step, :, y * 128 : (y + 1) * 128] = (s * c).astype(BF16)
    moments = lax.dot_general(
        jnp.concatenate([spread_high, spread_low], axis=0), cos_ref[...], NT,
        preferred_element_type=F32,
    )
    fine = lax.dot_general(spread_high, low_ref[...], NT, preferred_element_type=F32)
    moments = moments[0:32] + (moments[32:64] + fine)
    for z in range(4):
        leaf_ref[step, z] = moments[z * 8 : (z + 1) * 8]


def atoms_lift(leaf_ref, up_ref, mid_ref, own_ref, send_ref):
    total = jnp.zeros((32, 128), F32)
    for child in range(8):
        cx, cy, cz = child // 4, child // 2 % 2, child % 2
        rows = jnp.concatenate(
            [
                leaf_ref[2 * x + cx, 2 * z + cz, pl.ds(cy, 4, stride=2), :]
                for x in range(4)
                for z in range(2)
            ],
            axis=0,
        )
        total = total + dot(rows.astype(BF16), up_ref[0, child])
    for x in range(4):
        for z in range(2):
            for y in range(4):
                row = (x * 2 + z) * 4 + y
                mid_ref[x, y, z : z + 1, :] = total[row : row + 1]
    crown = jnp.zeros((8, 128), F32)
    for child in range(8):
        cx, cy, cz = child // 4, child // 2 % 2, child % 2
        rows = jnp.concatenate(
            [
                mid_ref[2 * x + cx, 2 * y + cy, cz : cz + 1, :]
                for x in range(2)
                for y in range(2)
            ]
            + [jnp.zeros((4, 128), F32)],
            axis=0,
        )
        crown = crown + dot(rows.astype(BF16), up_ref[1, child])
    odd = lax.axis_index("gz") % 2
    for x in range(8):
        for z in range(4):
            row = (x * 4 + z) * 8
            own_ref[row : row + 8, :] = leaf_ref[x, z]
        for z in range(2):
            row = (x * 2 + z) * 8
            send_ref[row : row + 8, :] = leaf_ref[x, 2 * (1 - odd) + z]
    for x in range(4):
        for y in range(4):
            row = (x * 4 + y) * 2
            own_ref[256 + row : 258 + row, :] = mid_ref[x, y]
            send_ref[128 + row : 130 + row, :] = mid_ref[x, y]
    own_ref[288:296, :] = crown
    send_ref[160:168, :] = crown


def run_atoms(features, positions, box_counts, w_hidden, w_charge, wave, phases, upward):
    hbm = pl.BlockSpec(memory_space=pltpu.HBM)
    return pl.pallas_call(
        atoms_kernel,
        in_specs=[hbm, hbm, VMEM, hbm, VMEM, VMEM, VMEM, hbm],
        out_specs=[VMEM, hbm, VMEM, VMEM],
        out_shape=[
            jax.ShapeDtypeStruct((8, 8, 128), F32),
            jax.ShapeDtypeStruct((8, 128, 1024), BF16),
            jax.ShapeDtypeStruct((296, 128), F32),
            jax.ShapeDtypeStruct((168, 128), F32),
        ],
        scratch_shapes=[
            pltpu.VMEM((8, 8, 128, 128), BF16),
            pltpu.VMEM((3, 8, 8, 128), F32),
            pltpu.VMEM((128, 128), BF16),
            pltpu.VMEM((2, 8, 128, 128), BF16),
            pltpu.VMEM((4, 128, 128), F32),
            pltpu.VMEM((128, 1024), BF16),
            pltpu.VMEM((128, 1024), BF16),
            pltpu.VMEM((8, 128, 1024), BF16),
            pltpu.VMEM((8, 4, 8, 128), F32),
            pltpu.VMEM((4, 4, 2, 128), F32),
            pltpu.SemaphoreType.DMA((8,)),
            pltpu.SemaphoreType.DMA((8,)),
            pltpu.SemaphoreType.DMA((3,)),
        ],
        compiler_params=pltpu.CompilerParams(vmem_limit_bytes=58 << 20),
        name="atoms",
    )(features, positions, box_counts, w_hidden, w_charge, wave, phases, upward)


def glue_z_kernel(got_ref, own_ref, leafz_ref, midz_ref, topz_ref, xa_ref, xb_ref):
    odd = lax.axis_index("gz") % 2
    for x in range(8):
        for z in range(4):
            row = (x * 4 + z) * 8
            leafz_ref[x, 2 * odd + z] = own_ref[row : row + 8, :]
        for z in range(2):
            row = (x * 2 + z) * 8
            leafz_ref[x, 4 * (1 - odd) + z] = got_ref[row : row + 8, :]
    for x in range(4):
        for y in range(4):
            row = (x * 4 + y) * 2
            mine, other = own_ref[256 + row : 258 + row, :], got_ref[128 + row : 130 + row, :]
            midz_ref[x, y] = jnp.concatenate(
                [jnp.where(odd == 1, other, mine), jnp.where(odd == 1, mine, other)], axis=0
            )
    mine, other = own_ref[288:292, :], got_ref[160:164, :]
    low, high = jnp.where(odd == 1, other, mine), jnp.where(odd == 1, mine, other)
    pair = jnp.concatenate(
        [piece[i : i + 1] for i in range(4) for piece in (low, high)], axis=0
    )
    topz_ref[...] = pair
    odd_x = lax.axis_index("gx") % 2
    for ref, side in ((xa_ref, 1 - odd_x), (xb_ref, odd_x)):
        for x in range(2):
            for z in range(6):
                row = (x * 6 + z) * 8
                ref[row : row + 8, :] = leafz_ref[side * 6 + x, z]
            for y in range(4):
                row = 96 + (x * 4 + y) * 4
                ref[row : row + 4, :] = midz_ref[side * 2 + x, y]
        ref[128:136, :] = pair


def glue_z(got, own):
    return pl.pallas_call(
        glue_z_kernel,
        in_specs=[VMEM] * 2,
        out_specs=[VMEM] * 5,
        out_shape=[
            jax.ShapeDtypeStruct((8, 6, 8, 128), F32),
            jax.ShapeDtypeStruct((4, 4, 4, 128), F32),
            jax.ShapeDtypeStruct((8, 128), F32),
            jax.ShapeDtypeStruct((136, 128), F32),
            jax.ShapeDtypeStruct((136, 128), F32),
        ],
        compiler_params=pltpu.CompilerParams(vmem_limit_bytes=8 << 20),
        name="glue_z",
    )(got, own)


def glue_x_kernel(ra_ref, rb_ref, leafz_ref, midz_ref, topz_ref, leafx_ref, midx_ref, topx_ref, ya_ref, yb_ref):
    odd = lax.axis_index("gx") % 2
    leafx_ref[2:10] = leafz_ref[...]
    midx_ref[2:6] = midz_ref[...]
    for ref, high in ((ra_ref, 1 - odd), (rb_ref, odd)):
        for x in range(2):
            for z in range(6):
                row = (x * 6 + z) * 8
                leafx_ref[high * 10 + x, z] = ref[row : row + 8, :]
            for y in range(4):
                row = 96 + (x * 4 + y) * 4
                midx_ref[high * 6 + x, y] = ref[row : row + 4, :]
    ta, tb = ra_ref[128:136, :], rb_ref[128:136, :]
    topx_ref[0:8, :] = jnp.where(odd == 1, ta, tb)
    topx_ref[8:16, :] = topz_ref[...]
    topx_ref[16:24, :] = jnp.where(odd == 1, tb, ta)
    odd_y = lax.axis_index("gy") % 2
    for x in range(12):
        for z in range(6):
            tile = leafx_ref[x, z]
            low, high = tile[0:2], tile[6:8]
            row = (x * 6 + z) * 2
            ya_ref[row : row + 2, :] = jnp.where(odd_y == 1, low, high)
            yb_ref[row : row + 2, :] = jnp.where(odd_y == 1, high, low)
    for ref, side in ((ya_ref, 1 - odd_y), (yb_ref, odd_y)):
        for x in range(8):
            for y in range(2):
                row = 144 + (x * 2 + y) * 4
                ref[row : row + 4, :] = midx_ref[x, side * 2 + y]
        ref[208:232, :] = topx_ref[...]


def glue_x(ra, rb, leaf, mid, top):
    return pl.pallas_call(
        glue_x_kernel,
        in_specs=[VMEM] * 5,
        out_specs=[VMEM] * 5,
        out_shape=[
            jax.ShapeDtypeStruct((12, 6, 8, 128), F32),
            jax.ShapeDtypeStruct((8, 4, 4, 128), F32),
            jax.ShapeDtypeStruct((24, 128), F32),
            jax.ShapeDtypeStruct((232, 128), F32),
            jax.ShapeDtypeStruct((232, 128), F32),
        ],
        compiler_params=pltpu.CompilerParams(vmem_limit_bytes=8 << 20),
        name="glue_x",
    )(ra, rb, leaf, mid, top)


def glue_y_kernel(ra_ref, rb_ref, leafx_ref, midx_ref, topx_ref, leafxy_ref, midxy_ref, topxy_ref, near_ref):
    odd = lax.axis_index("gy") % 2
    for x in range(12):
        for z in range(6):
            row = (x * 6 + z) * 2
            a, b = ra_ref[row : row + 2, :], rb_ref[row : row + 2, :]
            leafxy_ref[x, z, 0:2, :] = jnp.where(odd == 1, a, b)
            leafxy_ref[x, z, 2:10, :] = leafx_ref[x, z]
            leafxy_ref[x, z, 10:12, :] = jnp.where(odd == 1, b, a)
    for x in range(8):
        midxy_ref[x, 2:6] = midx_ref[x]
        for ref, high in ((ra_ref, 1 - odd), (rb_ref, odd)):
            for y in range(2):
                row = 144 + (x * 2 + y) * 4
                midxy_ref[x, high * 6 + y] = ref[row : row + 4, :]
    for x in range(6):
        row = 208 + x * 4
        a, b = ra_ref[row : row + 4, :], rb_ref[row : row + 4, :]
        topxy_ref[x * 12 : x * 12 + 4, :] = jnp.where(odd == 1, a, b)
        topxy_ref[x * 12 + 4 : x * 12 + 8, :] = topx_ref[x * 4 : x * 4 + 4, :]
        topxy_ref[x * 12 + 8 : x * 12 + 12, :] = jnp.where(odd == 1, b, a)
    odd_z = lax.axis_index("gz") % 2
    for x in range(12):
        for z in range(2):
            row = (x * 2 + z) * 12
            near_ref[row : row + 12, :] = leafxy_ref[x, 4 * odd_z + z]
    for x in range(8):
        for y in range(8):
            row = 288 + (x * 8 + y) * 2
            tile = midxy_ref[x, y]
            near_ref[row : row + 2, :] = jnp.where(odd_z == 1, tile[2:4], tile[0:2])
    near_ref[416:488, :] = topxy_ref[...]


def glue_y(ra, rb, leafx, midx, topx):
    return pl.pallas_call(
        glue_y_kernel,
        in_specs=[VMEM] * 5,
        out_specs=[VMEM] * 4,
        out_shape=[
            jax.ShapeDtypeStruct((12, 6, 12, 128), F32),
            jax.ShapeDtypeStruct((8, 8, 4, 128), F32),
            jax.ShapeDtypeStruct((72, 128), F32),
            jax.ShapeDtypeStruct((488, 128), F32),
        ],
        compiler_params=pltpu.CompilerParams(vmem_limit_bytes=8 << 20),
        name="glue_y",
    )(ra, rb, leafx, midx, topx)


def offset_tiles(out_ref, table, cz, masked):
    zero = jnp.zeros((2, 128), F32)
    keep_rows = lax.broadcasted_iota(jnp.int32, (8, 128), 0)
    near = (keep_rows >= 1 + cz) & (keep_rows <= 3 + cz)
    for xy in range(49):
        start = xy * 7 + 1 - cz
        tile = jnp.concatenate([table[start : start + 6, :], zero], axis=0)
        if masked and 2 <= xy // 7 <= 4 and 2 <= xy % 7 <= 4:
            tile = jnp.where(near, 0.0, tile)
        out_ref[xy] = tile


def far_kernel(
    leafxy_ref, midxy_ref, near_ref, in_ref, out_ref, core_ref,
    far0_ref, far1_ref,
    leaf_ref, mid_ref, scale_ref, tin_ref, tout_ref, acc_ref, even_ref, odd_ref,
):
    odd = lax.axis_index("gz") % 2
    for x in range(12):
        for z in range(6):
            leaf_ref[x, 2 * (1 - odd) + z] = leafxy_ref[x, z]
        for z in range(2):
            row = (x * 2 + z) * 12
            leaf_ref[x, 6 * odd + z] = near_ref[row : row + 12, :]
    zero = jnp.zeros((2, 128), F32)
    for x in range(8):
        for y in range(8):
            row = 288 + (x * 8 + y) * 2
            inner, outer = midxy_ref[x, y], near_ref[row : row + 2, :]
            mid_ref[x, y] = jnp.where(
                odd == 1,
                jnp.concatenate([inner, outer, zero], axis=0),
                jnp.concatenate([outer, inner, zero], axis=0),
            )
    scale_ref[...] = in_ref[0]
    for x in range(2, 5):
        for y in range(2, 5):
            row = x * 49 + y * 7 + 2
            scale_ref[row : row + 3, :] = jnp.zeros((3, 128), F32)
    for cz in range(2):
        offset_tiles(tin_ref.at[cz], in_ref.at[1], cz, True)
        offset_tiles(tout_ref.at[cz], out_ref.at[1], cz, False)

    far0_ref[...] = jnp.zeros((8, 32, 128), F32)
    core0 = core_ref[0]

    def row_of(qx, qy, qz, pair, cz):
        return (qx + 1 - pair // 2) * 49 + (qy + 1 - pair % 2) * 7 + qz + 1 - cz

    def build_leaf(step, operand_ref):
        qx, qz = step // 6, step % 6
        for qy in range(6):
            tiles = []
            for x in range(4):
                for z in range(2):
                    tiles.append(leaf_ref[2 * x + qx, 2 * z + qz, pl.ds(qy, 4, stride=2), :])
            source = jnp.concatenate(tiles, axis=0)
            for pair in range(4):
                for cz in range(2):
                    start = ((pair * 2 + cz) * 6 + qy) * 32
                    row = row_of(qx, qy, qz, pair, cz)
                    scale = jnp.broadcast_to(scale_ref[pl.ds(row, 1), :], (32, 128))
                    operand_ref[start : start + 32, :] = (source * scale).astype(BF16)

    def apply_leaf(step, image):
        qx, qz = step // 6, step % 6
        for pair in range(4):
            for cz in range(2):
                total = far0_ref[pair * 2 + cz]
                for qy in range(6):
                    row = row_of(qx, qy, qz, pair, cz)
                    scale = jnp.broadcast_to(out_ref[0, pl.ds(row, 1), :], (32, 128))
                    start = ((pair * 2 + cz) * 6 + qy) * 32
                    total = total + scale * image[start : start + 32]
                far0_ref[pair * 2 + cz] = total

    build_leaf(0, even_ref)

    @pl.loop(0, 18)
    def _(turn):
        image = dot(even_ref[...], core0)
        build_leaf(2 * turn + 1, odd_ref)
        apply_leaf(2 * turn, image)
        image = dot(odd_ref[...], core0)
        build_leaf(jnp.minimum(2 * turn + 2, 35), even_ref)
        apply_leaf(2 * turn + 1, image)

    acc_ref[...] = jnp.zeros((8, 32, 128), F32)
    core1 = core_ref[1]

    def build_mid(qx, operand_ref):
        for qy in range(6):
            tiles = [mid_ref[2 * x + qx, 2 * y + qy] for x in range(2) for y in range(2)]
            for pair in range(4):
                xy = (qx + 1 - pair // 2) * 7 + qy + 1 - pair % 2
                for cz in range(2):
                    scale = tin_ref[cz, xy]
                    start = ((pair * 2 + cz) * 6 + qy) * 32
                    operand_ref[start : start + 32, :] = jnp.concatenate(
                        [tile * scale for tile in tiles], axis=0
                    ).astype(BF16)

    def apply_mid(qx, image):
        for pair in range(4):
            for cz in range(2):
                total = acc_ref[pair * 2 + cz]
                for qy in range(6):
                    scale = tout_ref[cz, (qx + 1 - pair // 2) * 7 + qy + 1 - pair % 2]
                    scale = jnp.concatenate([scale] * 4, axis=0)
                    start = ((pair * 2 + cz) * 6 + qy) * 32
                    total = total + scale * image[start : start + 32]
                acc_ref[pair * 2 + cz] = total

    build_mid(0, even_ref)

    @pl.loop(0, 3)
    def _(turn):
        image = dot(even_ref[...], core1)
        build_mid(2 * turn + 1, odd_ref)
        apply_mid(2 * turn, image)
        image = dot(odd_ref[...], core1)
        build_mid(jnp.minimum(2 * turn + 2, 5), even_ref)
        apply_mid(2 * turn + 1, image)

    for child in range(8):
        for parent in range(4):
            tile = acc_ref[child, parent * 8 : parent * 8 + 8, :]
            far1_ref[child * 4 + parent : child * 4 + parent + 1, :] = jnp.sum(
                tile, axis=0, keepdims=True
            )


def run_far(leafxy, midxy, near, in_scale, out_scale, transfer):
    return pl.pallas_call(
        far_kernel,
        in_specs=[VMEM] * 6,
        out_specs=[VMEM] * 2,
        out_shape=[
            jax.ShapeDtypeStruct((8, 32, 128), F32),
            jax.ShapeDtypeStruct((32, 128), F32),
        ],
        scratch_shapes=[
            pltpu.VMEM((12, 8, 12, 128), F32),
            pltpu.VMEM((8, 8, 8, 128), F32),
            pltpu.VMEM((343, 128), F32),
            pltpu.VMEM((2, 49, 8, 128), F32),
            pltpu.VMEM((2, 49, 8, 128), F32),
            pltpu.VMEM((8, 32, 128), F32),
            pltpu.VMEM((1536, 128), BF16),
            pltpu.VMEM((1536, 128), BF16),
        ],
        cost_estimate=pl.CostEstimate(flops=4 << 30, bytes_accessed=4 << 20, transcendentals=0),
        compiler_params=pltpu.CompilerParams(vmem_limit_bytes=24 << 20),
        name="far",
    )(leafxy, midxy, near, in_scale, out_scale, transfer)


def force_kernel(
    far0_ref, far1_ref, pair_ref, near_ref, next_ref, in_ref, out_ref, core_ref, down_ref,
    charge_ref, sin_ref, pos_ref, wave_ref,
    forces_ref, share_ref,
    window_ref, tin_ref, tout_ref, operand_ref, mid_ref, local_ref,
):
    odd = lax.axis_index("gz") % 2
    for xy in range(36):
        near = near_ref[416 + 2 * xy : 418 + 2 * xy, :]
        behind = next_ref[2 * xy : 2 * xy + 2, :]
        window_ref[xy] = jnp.concatenate(
            [
                jnp.where(odd == 1, behind, near),
                pair_ref[2 * xy : 2 * xy + 2, :],
                jnp.where(odd == 1, near, behind),
                jnp.zeros((2, 128), F32),
            ],
            axis=0,
        )
    lanes = lax.broadcasted_iota(jnp.int32, (8, 128), 0)
    near = (lanes >= 1 + odd) & (lanes <= 3 + odd)
    for xy in range(49):
        for ref, table, masked in ((tin_ref, in_ref, True), (tout_ref, out_ref, False)):
            rows = table[2, xy * 7 : xy * 7 + 7, :]
            tile = jnp.where(odd == 1, rows[0:6], rows[1:7])
            tile = jnp.concatenate([tile, jnp.zeros((2, 128), F32)], axis=0)
            if masked and 2 <= xy // 7 <= 4 and 2 <= xy % 7 <= 4:
                tile = jnp.where(near, 0.0, tile)
            ref[xy] = tile
    for qx in range(6):
        for qy in range(6):
            source = window_ref[qx * 6 + qy]
            tiles = []
            for pair in range(4):
                cx, cy = pair // 2, pair % 2
                tiles.append(source * tin_ref[(qx + 1 - cx) * 7 + qy + 1 - cy])
            start = (qx * 6 + qy) * 32
            operand_ref[start : start + 32, :] = jnp.concatenate(tiles, axis=0).astype(BF16)
    totals = [jnp.zeros((8, 128), F32) for _ in range(4)]
    for qx in range(6):
        image = dot(operand_ref[qx * 192 : qx * 192 + 192, :], core_ref[2])
        for qy in range(6):
            for pair in range(4):
                cx, cy = pair // 2, pair % 2
                scale = tout_ref[(qx + 1 - cx) * 7 + qy + 1 - cy]
                start = qy * 32 + pair * 8
                totals[pair] = totals[pair] + scale * image[start : start + 8]
    local_top = jnp.concatenate(
        [jnp.sum(total, axis=0, keepdims=True) for total in totals] + [jnp.zeros((4, 128), F32)],
        axis=0,
    ).astype(BF16)
    for child in range(8):
        cx, cy, cz = child // 4, child // 2 % 2, child % 2
        rows = far1_ref[child * 4 : child * 4 + 4, :] + dot(local_top, down_ref[1, child])[0:4]
        for parent in range(4):
            row = ((2 * (parent // 2) + cx) * 2 + cz) * 4 + 2 * (parent % 2) + cy
            mid_ref[row : row + 1, :] = rows[parent : parent + 1]
    local_mid = mid_ref[...].astype(BF16)
    for child in range(8):
        cx, cy, cz = child // 4, child // 2 % 2, child % 2
        rows = far0_ref[child] + dot(local_mid, down_ref[0, child])
        for x in range(4):
            for z in range(2):
                start = (x * 2 + z) * 4
                local_ref[2 * x + cx, 2 * z + cz, pl.ds(cy, 4, stride=2), :] = rows[start : start + 4]

    lane_box = lax.broadcasted_iota(jnp.int32, (8, 128), 1) // 32
    row_y = lax.broadcasted_iota(jnp.int32, (8, 128), 0)
    base_x = lax.axis_index("gx") * 8
    base_y = lax.axis_index("gy") * 8
    base_z = lax.axis_index("gz") * 4
    place_y0 = (base_y + row_y).astype(F32)
    place_z0 = (base_z + lane_box).astype(F32)

    def one_plane(x, sums):
        local = local_ref[x].reshape(32, 128)
        weights = jnp.concatenate([local * wave_ref[d : d + 1, :] for d in range(3)], axis=0)
        high = weights.astype(BF16)
        low = (weights - high.astype(F32)).astype(BF16)
        sines = sin_ref[x]
        product = dot(
            jnp.concatenate([high, low], axis=1), jnp.concatenate([sines, sines], axis=0)
        )
        charge = charge_ref[x]
        found = []
        for d in range(3):
            picked = jnp.zeros((8, 128), F32)
            for z in range(4):
                start = (d * 4 + z) * 8
                for y in range(8):
                    picked = jnp.where(
                        (row_y == y) & (lane_box == z),
                        product[start : start + 8, y * 128 : y * 128 + 128],
                        picked,
                    )
            picked = picked * charge
            forces_ref[d, x] = picked
            found.append(picked)
        places = (
            ((base_x + x).astype(F32) + pos_ref[0, x]) * (1.0 / 32),
            (place_y0 + pos_ref[1, x]) * (1.0 / 64),
            (place_z0 + pos_ref[2, x]) * (1.0 / 64),
        )
        return tuple(
            sums[d * 3 + e] + places[d] * found[e] for d in range(3) for e in range(3)
        )

    sums = lax.fori_loop(0, 8, one_plane, (jnp.zeros((8, 128), F32),) * 9)
    lane = lax.broadcasted_iota(jnp.int32, (8, 128), 1)
    row = jnp.zeros((8, 128), F32)
    for i in range(9):
        row = jnp.where(lane == i, jnp.sum(sums[i]), row)
    share_ref[...] = jnp.broadcast_to(row[0:1], (64, 128))


def run_forces(far0, far1, pair, near, following, in_scale, out_scale, transfer, downward, charge, sines, positions, wave):
    return pl.pallas_call(
        force_kernel,
        in_specs=[VMEM] * 13,
        out_specs=[VMEM] * 2,
        out_shape=[
            jax.ShapeDtypeStruct((3, 8, 8, 128), F32),
            jax.ShapeDtypeStruct((64, 128), F32),
        ],
        scratch_shapes=[
            pltpu.VMEM((36, 8, 128), F32),
            pltpu.VMEM((49, 8, 128), F32),
            pltpu.VMEM((49, 8, 128), F32),
            pltpu.VMEM((1152, 128), BF16),
            pltpu.VMEM((32, 128), F32),
            pltpu.VMEM((8, 4, 8, 128), F32),
        ],
        compiler_params=pltpu.CompilerParams(vmem_limit_bytes=24 << 20),
        name="forces",
    )(far0, far1, pair, near, following, in_scale, out_scale, transfer, downward, charge, sines, positions, wave)


def fold_kernel(rows_ref, share_ref):
    share_ref[...] = jnp.broadcast_to(jnp.sum(rows_ref[...], axis=0, keepdims=True), (8, 128))


def fold(rows):
    return pl.pallas_call(
        fold_kernel,
        in_specs=[VMEM],
        out_specs=VMEM,
        out_shape=jax.ShapeDtypeStruct((8, 128), F32),
        compiler_params=pltpu.CompilerParams(vmem_limit_bytes=8 << 20),
        name="fold",
    )(rows)


def virial_kernel(scale, rows_ref, virial_ref):
    row = jnp.sum(rows_ref[...], axis=0, keepdims=True) * scale
    for d in range(3):
        virial_ref[d : d + 1, :] = row[:, d * 3 : d * 3 + 3]


def run_virial(rows, scale):
    return pl.pallas_call(
        lambda rows_ref, virial_ref: virial_kernel(scale, rows_ref, virial_ref),
        in_specs=[VMEM],
        out_specs=VMEM,
        out_shape=jax.ShapeDtypeStruct((3, 3), F32),
        compiler_params=pltpu.CompilerParams(vmem_limit_bytes=8 << 20),
        name="virial",
    )(rows)


def swapped(value, axis, kind):
    count = lax.axis_size(axis)
    pairs = []
    for i in range(count):
        hop = (1, -1, 3)[kind]
        pairs.append((i, (i + hop) % count if i % 2 == 0 else (i - hop) % count))
    return lax.ppermute(value, axis, pairs)


def shards(
    features, positions, box_counts, w_hidden, w_charge, wave_numbers, phases,
    upward, downward, transfer, out_scale, in_scale,
):
    charge, sines, own, send = run_atoms(
        features, positions, box_counts.transpose(0, 2, 1), w_hidden, w_charge.reshape(1, 128),
        wave_numbers, phases.reshape(1, 128), upward,
    )
    leaf, mid, top, xa, xb = glue_z(swapped(send, "gz", 0), own)
    ra, rb = swapped(xa, "gx", 0), swapped(xb, "gx", 1)
    leaf, mid, top, ya, yb = glue_x(ra, rb, leaf, mid, top)
    ra, rb = swapped(ya, "gy", 0), swapped(yb, "gy", 1)
    leaf, mid, pair, side = glue_y(ra, rb, leaf, mid, top)
    near, following = swapped(side, "gz", 1), swapped(pair, "gz", 2)
    far0, far1 = run_far(leaf, mid, near, in_scale, out_scale, transfer)
    forces, share = run_forces(
        far0, far1, pair, near, following, in_scale, out_scale, transfer, downward, charge, sines,
        positions, wave_numbers,
    )
    rows = fold(lax.all_to_all(share, ("gx", "gz"), 0, 0, tiled=True))
    rows = lax.all_to_all(rows, "gy", 0, 0, tiled=True)
    return forces, run_virial(rows, 1.0 / math.sqrt(4194304))


def solution(mesh):
    in_specs = (
        P("gx", "gy", "gz", None),
        P(None, "gx", "gy", "gz"),
        P("gx", "gy", "gz"),
    ) + (P(),) * 9
    out_specs = (P(None, "gx", "gy", "gz"), P())
    return jax.shard_map(shards, mesh=mesh, in_specs=in_specs, out_specs=out_specs, check_vma=False)
```

```python
import functools
import math

import jax
import jax.numpy as jnp
import numpy as np
from jax import lax
from jax.experimental import pallas as pl
from jax.experimental.pallas import tpu as pltpu
from jax.sharding import PartitionSpec as P

F32 = jnp.float32
BF16 = jnp.bfloat16
TURN = 1.0 / (2.0 * math.pi)
SIN_HALF = (4.4428679, -7.30744342, 3.59478808, -0.78437403)
COS_HALF = (1.4142135, -6.97885099, 5.73946117, -1.88356299, 0.31069819)
NT = (((1,), (1,)), ((), ()))
VMEM = pl.BlockSpec(memory_space=pltpu.VMEM)


def dot(a, b):
    return jnp.dot(a, b, preferred_element_type=F32)


def split(value):
    high = value.astype(BF16).astype(F32)
    rest = value - high
    middle = rest.astype(BF16).astype(F32)
    return high, middle, rest - middle


def wave_table(wave_ref, ph_ref, table_ref):
    blocks = []
    for d in range(3):
        high, middle, low = split(wave_ref[d : d + 1, :] * TURN)
        for part in (high, middle, low, high, middle, high):
            blocks.append(jnp.broadcast_to(part, (8, 128)))
    blocks += list(split(ph_ref[...] * TURN)) + [jnp.zeros((109, 128), F32)]
    table_ref[...] = jnp.concatenate(blocks, axis=0).T.astype(BF16)


def turns_of(step, pos_ref, table_ref):
    row_y = lax.broadcasted_iota(jnp.int32, (8, 128), 0)
    blocks = []
    for d in range(3):
        spread = []
        for part in split(pos_ref[d, step] - 0.5):
            spread.append(
                jnp.concatenate([jnp.where(row_y == y, part, 0.0) for y in range(8)], axis=1)
            )
        blocks += [spread[0]] * 3 + [spread[1]] * 2 + [spread[2]]
    blocks += [jnp.ones((8, 1024), F32), jnp.zeros((8, 1024), F32)]
    return dot(table_ref[:, 0:160], jnp.concatenate(blocks, axis=0).astype(BF16))


def poly(coefs, u):
    value = coefs[-1]
    for coef in coefs[-2::-1]:
        value = value * u + coef
    return value


def sines_kernel(start, pos_ref, wave_ref, ph_ref, _, sin_ref, table_ref):
    wave_table(wave_ref, ph_ref, table_ref)

    @pl.loop(0, sin_ref.shape[0])
    def _(x):
        turns = turns_of(start + x, pos_ref, table_ref)
        for y in range(8):
            t = turns[:, y * 128 : (y + 1) * 128]
            r = t - jnp.round(t)
            u = r * r
            sin_ref[x, :, y * 128 : (y + 1) * 128] = (
                poly(SIN_HALF, u) * r * poly(COS_HALF, u)
            ).astype(BF16)


def run_sines(positions, wave, phases, after, start, planes):
    return pl.pallas_call(
        functools.partial(sines_kernel, start),
        in_specs=[VMEM] * 4,
        out_specs=VMEM,
        out_shape=jax.ShapeDtypeStruct((planes, 128, 1024), BF16),
        scratch_shapes=[pltpu.VMEM((128, 256), BF16)],
        cost_estimate=pl.CostEstimate(flops=1 << 30, bytes_accessed=6 << 20, transcendentals=0),
        compiler_params=pltpu.CompilerParams(vmem_limit_bytes=16 << 20),
        name="sines",
    )(positions, wave, phases, after)


def atoms_kernel(
    feat_hbm, pos_hbm, cnt_ref, wh_hbm, wc_ref, wave_ref, ph_ref, up_hbm,
    charge_ref, own_ref, sa_ref, sb_ref,
    feat_ref, pos_ref, wh_ref, up_ref, table_ref, cos_ref, low_ref, leaf_ref, mid_ref,
    plane_sems, sems,
):
    def plane(x):
        return pltpu.make_async_copy(feat_hbm.at[x], feat_ref.at[x], plane_sems.at[x])

    others = [
        pltpu.make_async_copy(wh_hbm, wh_ref, sems.at[0]),
        pltpu.make_async_copy(pos_hbm, pos_ref, sems.at[1]),
        pltpu.make_async_copy(up_hbm, up_ref, sems.at[2]),
    ]
    plane(0).start()
    others[0].start()
    others[1].start()
    for x in range(1, 8):
        plane(x).start()
    others[2].start()
    wave_table(wave_ref, ph_ref, table_ref)
    others[0].wait()
    others[1].wait()

    @pl.loop(0, 8)
    def _(x):
        plane(x).wait()
        atoms_plane(
            x, feat_ref, pos_ref, cnt_ref, wh_ref, wc_ref, charge_ref, leaf_ref, table_ref,
            cos_ref, low_ref,
        )

    others[2].wait()
    atoms_lift(leaf_ref, up_ref, mid_ref, own_ref, sa_ref, sb_ref)


def atoms_plane(
    step, feat_ref, pos_ref, cnt_ref, wh_ref, wc_ref, charge_ref, leaf_ref, table_ref,
    cos_ref, low_ref,
):
    lane_box = lax.broadcasted_iota(jnp.int32, (8, 128), 1) // 32
    lane_slot = lax.broadcasted_iota(jnp.int32, (8, 128), 1) % 32
    row_y = lax.broadcasted_iota(jnp.int32, (8, 128), 0)
    counts = jnp.zeros((8, 128), jnp.int32)
    columns = cnt_ref[step].T
    for z in range(4):
        counts = jnp.where(
            lane_box == z, jnp.broadcast_to(columns[:, z : z + 1], (8, 128)), counts
        )
    live = jnp.where(lane_slot < counts, 1.0, 0.0).astype(F32)

    hidden = dot(feat_ref[step].reshape(1024, 128), wh_ref[...])
    half = hidden * 0.5
    hidden = (half + half * jnp.tanh(half)).astype(BF16)
    wc = jnp.broadcast_to(wc_ref[...], (8, 128))
    raw = lax.dot_general(wc, hidden, NT, preferred_element_type=F32)
    charge = jnp.zeros((8, 128), F32)
    for y in range(8):
        charge = jnp.where(row_y == y, raw[:, y * 128 : (y + 1) * 128], charge)
    charge = charge * live
    charge_ref[step] = charge

    spread = []
    for z in range(4):
        spread.append(
            jnp.concatenate(
                [
                    jnp.where((row_y == y) & (lane_box == z), charge, 0.0)
                    for y in range(8)
                ],
                axis=1,
            )
        )
    spread = jnp.concatenate(spread, axis=0)
    spread_high = spread.astype(BF16)
    spread_low = (spread - spread_high.astype(F32)).astype(BF16)

    turns = turns_of(step, pos_ref, table_ref)
    for y in range(8):
        t = turns[:, y * 128 : (y + 1) * 128]
        r = t - jnp.round(t)
        s = poly(SIN_HALF, r * r) * r
        cosine = 1.0 - s * s
        cosine_high = cosine.astype(BF16)
        cos_ref[:, y * 128 : (y + 1) * 128] = cosine_high
        low_ref[:, y * 128 : (y + 1) * 128] = (cosine - cosine_high.astype(F32)).astype(BF16)
    moments = lax.dot_general(
        jnp.concatenate([spread_high, spread_low], axis=0), cos_ref[...], NT,
        preferred_element_type=F32,
    )
    fine = lax.dot_general(spread_high, low_ref[...], NT, preferred_element_type=F32)
    moments = moments[0:32] + (moments[32:64] + fine)
    for z in range(4):
        leaf_ref[step, z] = moments[z * 8 : (z + 1) * 8]


def atoms_lift(leaf_ref, up_ref, mid_ref, own_ref, sa_ref, sb_ref):
    total = jnp.zeros((32, 128), F32)
    for child in range(8):
        cx, cy, cz = child // 4, child // 2 % 2, child % 2
        rows = jnp.concatenate(
            [
                leaf_ref[2 * x + cx, 2 * z + cz, pl.ds(cy, 4, stride=2), :]
                for x in range(4)
                for z in range(2)
            ],
            axis=0,
        )
        total = total + dot(rows.astype(BF16), up_ref[0, child])
    for x in range(4):
        for z in range(2):
            for y in range(4):
                row = (x * 2 + z) * 4 + y
                mid_ref[x, y, z : z + 1, :] = total[row : row + 1]
    crown = jnp.zeros((8, 128), F32)
    for child in range(8):
        cx, cy, cz = child // 4, child // 2 % 2, child % 2
        rows = jnp.concatenate(
            [
                mid_ref[2 * x + cx, 2 * y + cy, cz : cz + 1, :]
                for x in range(2)
                for y in range(2)
            ]
            + [jnp.zeros((4, 128), F32)],
            axis=0,
        )
        crown = crown + dot(rows.astype(BF16), up_ref[1, child])
    own_ref[0:256, :] = leaf_ref[...].reshape(256, 128)
    for x in range(4):
        for y in range(4):
            row = 256 + (x * 4 + y) * 2
            own_ref[row : row + 2, :] = mid_ref[x, y]
    own_ref[288:296, :] = crown
    odd = lax.axis_index("gx") % 2
    for ref, high in ((sa_ref, 1 - odd), (sb_ref, odd)):
        for x in range(2):
            for z in range(4):
                row = (x * 4 + z) * 8
                ref[row : row + 8, :] = leaf_ref[high * 6 + x, z]
            for y in range(4):
                row = 64 + (x * 4 + y) * 2
                ref[row : row + 2, :] = mid_ref[high * 2 + x, y]
        ref[80:84, :] = crown[0:4]
        ref[84:88, :] = jnp.zeros((4, 128), F32)


def run_atoms(features, positions, box_counts, w_hidden, w_charge, wave, phases, upward):
    hbm = pl.BlockSpec(memory_space=pltpu.HBM)
    return pl.pallas_call(
        atoms_kernel,
        in_specs=[hbm, hbm, VMEM, hbm, VMEM, VMEM, VMEM, hbm],
        out_specs=[VMEM] * 4,
        out_shape=[
            jax.ShapeDtypeStruct((8, 8, 128), F32),
            jax.ShapeDtypeStruct((296, 128), F32),
            jax.ShapeDtypeStruct((88, 128), F32),
            jax.ShapeDtypeStruct((88, 128), F32),
        ],
        scratch_shapes=[
            pltpu.VMEM((8, 8, 128, 128), BF16),
            pltpu.VMEM((3, 8, 8, 128), F32),
            pltpu.VMEM((128, 128), BF16),
            pltpu.VMEM((2, 8, 128, 128), BF16),
            pltpu.VMEM((128, 256), BF16),
            pltpu.VMEM((128, 1024), BF16),
            pltpu.VMEM((128, 1024), BF16),
            pltpu.VMEM((8, 4, 8, 128), F32),
            pltpu.VMEM((4, 4, 2, 128), F32),
            pltpu.SemaphoreType.DMA((8,)),
            pltpu.SemaphoreType.DMA((3,)),
        ],
        compiler_params=pltpu.CompilerParams(vmem_limit_bytes=58 << 20),
        name="atoms",
    )(features, positions, box_counts, w_hidden, w_charge, wave, phases, upward)


def glue_x_kernel(ra_ref, rb_ref, own_ref, _, leafx_ref, midx_ref, topx_ref, ya_ref, yb_ref):
    odd = lax.axis_index("gx") % 2
    leafx_ref[2:10] = own_ref[0:256, :].reshape(8, 4, 8, 128)
    for x in range(4):
        for y in range(4):
            row = 256 + (x * 4 + y) * 2
            midx_ref[2 + x, y] = own_ref[row : row + 2, :]
    for ref, high in ((ra_ref, 1 - odd), (rb_ref, odd)):
        for x in range(2):
            for z in range(4):
                row = (x * 4 + z) * 8
                leafx_ref[high * 10 + x, z] = ref[row : row + 8, :]
            for y in range(4):
                row = 64 + (x * 4 + y) * 2
                midx_ref[high * 6 + x, y] = ref[row : row + 2, :]
    ta, tb = ra_ref[80:84, :], rb_ref[80:84, :]
    topx_ref[...] = jnp.concatenate(
        [
            jnp.where(odd == 1, ta, tb),
            own_ref[288:292, :],
            jnp.where(odd == 1, tb, ta),
            jnp.zeros((4, 128), F32),
        ],
        axis=0,
    )
    odd_y = lax.axis_index("gy") % 2
    for x in range(12):
        for z in range(4):
            tile = leafx_ref[x, z]
            low, high = tile[0:2], tile[6:8]
            row = (x * 4 + z) * 2
            ya_ref[row : row + 2, :] = jnp.where(odd_y == 1, low, high)
            yb_ref[row : row + 2, :] = jnp.where(odd_y == 1, high, low)
    for ref, side in ((ya_ref, 1 - odd_y), (yb_ref, odd_y)):
        for x in range(8):
            for y in range(2):
                row = 96 + (x * 2 + y) * 2
                ref[row : row + 2, :] = midx_ref[x, side * 2 + y]
        ref[128:144, :] = topx_ref[...]


def glue_x(ra, rb, own, front):
    return pl.pallas_call(
        glue_x_kernel,
        in_specs=[VMEM] * 3 + [pl.BlockSpec(memory_space=pl.ANY)],
        out_specs=[VMEM] * 5,
        out_shape=[
            jax.ShapeDtypeStruct((12, 4, 8, 128), F32),
            jax.ShapeDtypeStruct((8, 4, 2, 128), F32),
            jax.ShapeDtypeStruct((16, 128), F32),
            jax.ShapeDtypeStruct((144, 128), F32),
            jax.ShapeDtypeStruct((144, 128), F32),
        ],
        compiler_params=pltpu.CompilerParams(vmem_limit_bytes=8 << 20),
        name="glue_x",
    )(ra, rb, own, front)


def glue_y_kernel(ra_ref, rb_ref, leafx_ref, midx_ref, topx_ref, _, leafxy_ref, midxy_ref, topxy_ref, za_ref, zb_ref):
    odd = lax.axis_index("gy") % 2
    for x in range(12):
        for z in range(4):
            row = (x * 4 + z) * 2
            a, b = ra_ref[row : row + 2, :], rb_ref[row : row + 2, :]
            leafxy_ref[x, z, 0:2, :] = jnp.where(odd == 1, a, b)
            leafxy_ref[x, z, 2:10, :] = leafx_ref[x, z]
            leafxy_ref[x, z, 10:12, :] = jnp.where(odd == 1, b, a)
    for x in range(8):
        midxy_ref[x, 2:6] = midx_ref[x]
        for ref, high in ((ra_ref, 1 - odd), (rb_ref, odd)):
            for y in range(2):
                row = 96 + (x * 2 + y) * 2
                midxy_ref[x, high * 6 + y] = ref[row : row + 2, :]
    for x in range(6):
        row = 128 + x * 2
        a, b = ra_ref[row : row + 2, :], rb_ref[row : row + 2, :]
        topxy_ref[x * 6 : x * 6 + 2, :] = jnp.where(odd == 1, a, b)
        topxy_ref[x * 6 + 2 : x * 6 + 4, :] = topx_ref[x * 2 : x * 2 + 2, :]
        topxy_ref[x * 6 + 4 : x * 6 + 6, :] = jnp.where(odd == 1, b, a)
    topxy_ref[36:40, :] = jnp.zeros((4, 128), F32)
    odd_z = lax.axis_index("gz") % 2
    for ref, side in ((za_ref, 1 - odd_z), (zb_ref, odd_z)):
        for x in range(12):
            for z in range(2):
                row = (x * 2 + z) * 12
                ref[row : row + 12, :] = leafxy_ref[x, side * 2 + z]
        for x in range(8):
            for y in range(8):
                row = 288 + (x * 8 + y) * 2
                ref[row : row + 2, :] = midxy_ref[x, y]
    za_ref[416:456, :] = topxy_ref[...]


def glue_y(ra, rb, leafx, midx, topx, back):
    return pl.pallas_call(
        glue_y_kernel,
        in_specs=[VMEM] * 5 + [pl.BlockSpec(memory_space=pl.ANY)],
        out_specs=[VMEM] * 5,
        out_shape=[
            jax.ShapeDtypeStruct((12, 4, 12, 128), F32),
            jax.ShapeDtypeStruct((8, 8, 2, 128), F32),
            jax.ShapeDtypeStruct((40, 128), F32),
            jax.ShapeDtypeStruct((456, 128), F32),
            jax.ShapeDtypeStruct((416, 128), F32),
        ],
        compiler_params=pltpu.CompilerParams(vmem_limit_bytes=8 << 20),
        name="glue_y",
    )(ra, rb, leafx, midx, topx, back)


def glue_z_kernel(ra_ref, topxy_ref, pair_ref):
    odd = lax.axis_index("gz") % 2
    mine, other = topxy_ref[0:36, :], ra_ref[416:452, :]
    pair_ref[...] = jnp.concatenate(
        [jnp.where(odd == 1, other, mine), jnp.where(odd == 1, mine, other)], axis=0
    )


def glue_z(ra, topxy):
    return pl.pallas_call(
        glue_z_kernel,
        in_specs=[VMEM] * 2,
        out_specs=VMEM,
        out_shape=jax.ShapeDtypeStruct((72, 128), F32),
        compiler_params=pltpu.CompilerParams(vmem_limit_bytes=8 << 20),
        name="glue_z",
    )(ra, topxy)


def offset_tiles(out_ref, table, cz, masked):
    zero = jnp.zeros((2, 128), F32)
    keep_rows = lax.broadcasted_iota(jnp.int32, (8, 128), 0)
    near = (keep_rows >= 1 + cz) & (keep_rows <= 3 + cz)
    for xy in range(49):
        start = xy * 7 + 1 - cz
        tile = jnp.concatenate([table[start : start + 6, :], zero], axis=0)
        if masked and 2 <= xy // 7 <= 4 and 2 <= xy % 7 <= 4:
            tile = jnp.where(near, 0.0, tile)
        out_ref[xy] = tile


def far_kernel(
    leafxy_ref, midxy_ref, ra_ref, rb_ref, in_ref, out_ref, core_ref,
    far0_ref, far1_ref,
    leaf_ref, mid_ref, scale_ref, tin_ref, tout_ref, acc_ref, even_ref, odd_ref,
):
    odd = lax.axis_index("gz") % 2
    leaf_ref[:, 2:6] = leafxy_ref[...]
    for ref, high in ((ra_ref, 1 - odd), (rb_ref, odd)):
        for x in range(12):
            for z in range(2):
                row = (x * 2 + z) * 12
                leaf_ref[x, high * 6 + z] = ref[row : row + 12, :]
    for x in range(8):
        for y in range(8):
            row = 288 + (x * 8 + y) * 2
            a, b = ra_ref[row : row + 2, :], rb_ref[row : row + 2, :]
            mid_ref[x, y] = jnp.concatenate(
                [
                    jnp.where(odd == 1, a, b),
                    midxy_ref[x, y],
                    jnp.where(odd == 1, b, a),
                    jnp.zeros((2, 128), F32),
                ],
                axis=0,
            )
    scale_ref[...] = in_ref[0]
    for x in range(2, 5):
        for y in range(2, 5):
            row = x * 49 + y * 7 + 2
            scale_ref[row : row + 3, :] = jnp.zeros((3, 128), F32)
    for cz in range(2):
        offset_tiles(tin_ref.at[cz], in_ref.at[1], cz, True)
        offset_tiles(tout_ref.at[cz], out_ref.at[1], cz, False)

    far0_ref[...] = jnp.zeros((8, 32, 128), F32)
    core0 = core_ref[0]

    def row_of(qx, qy, qz, pair, cz):
        return (qx + 1 - pair // 2) * 49 + (qy + 1 - pair % 2) * 7 + qz + 1 - cz

    def build_leaf(step, operand_ref):
        qx, qz = step // 6, step % 6
        for qy in range(6):
            tiles = []
            for x in range(4):
                for z in range(2):
                    tiles.append(leaf_ref[2 * x + qx, 2 * z + qz, pl.ds(qy, 4, stride=2), :])
            source = jnp.concatenate(tiles, axis=0)
            for pair in range(4):
                for cz in range(2):
                    start = ((pair * 2 + cz) * 6 + qy) * 32
                    row = row_of(qx, qy, qz, pair, cz)
                    scale = jnp.broadcast_to(scale_ref[pl.ds(row, 1), :], (32, 128))
                    operand_ref[start : start + 32, :] = (source * scale).astype(BF16)

    def apply_leaf(step, image):
        qx, qz = step // 6, step % 6
        for pair in range(4):
            for cz in range(2):
                total = far0_ref[pair * 2 + cz]
                for qy in range(6):
                    row = row_of(qx, qy, qz, pair, cz)
                    scale = jnp.broadcast_to(out_ref[0, pl.ds(row, 1), :], (32, 128))
                    start = ((pair * 2 + cz) * 6 + qy) * 32
                    total = total + scale * image[start : start + 32]
                far0_ref[pair * 2 + cz] = total

    build_leaf(0, even_ref)

    @pl.loop(0, 18)
    def _(turn):
        image = dot(even_ref[...], core0)
        build_leaf(2 * turn + 1, odd_ref)
        apply_leaf(2 * turn, image)
        image = dot(odd_ref[...], core0)
        build_leaf(jnp.minimum(2 * turn + 2, 35), even_ref)
        apply_leaf(2 * turn + 1, image)

    acc_ref[...] = jnp.zeros((8, 32, 128), F32)
    core1 = core_ref[1]

    def build_mid(qx, operand_ref):
        for qy in range(6):
            tiles = [mid_ref[2 * x + qx, 2 * y + qy] for x in range(2) for y in range(2)]
            for pair in range(4):
                xy = (qx + 1 - pair // 2) * 7 + qy + 1 - pair % 2
                for cz in range(2):
                    scale = tin_ref[cz, xy]
                    start = ((pair * 2 + cz) * 6 + qy) * 32
                    operand_ref[start : start + 32, :] = jnp.concatenate(
                        [tile * scale for tile in tiles], axis=0
                    ).astype(BF16)

    def apply_mid(qx, image):
        for pair in range(4):
            for cz in range(2):
                total = acc_ref[pair * 2 + cz]
                for qy in range(6):
                    scale = tout_ref[cz, (qx + 1 - pair // 2) * 7 + qy + 1 - pair % 2]
                    scale = jnp.concatenate([scale] * 4, axis=0)
                    start = ((pair * 2 + cz) * 6 + qy) * 32
                    total = total + scale * image[start : start + 32]
                acc_ref[pair * 2 + cz] = total

    build_mid(0, even_ref)

    @pl.loop(0, 3)
    def _(turn):
        image = dot(even_ref[...], core1)
        build_mid(2 * turn + 1, odd_ref)
        apply_mid(2 * turn, image)
        image = dot(odd_ref[...], core1)
        build_mid(jnp.minimum(2 * turn + 2, 5), even_ref)
        apply_mid(2 * turn + 1, image)

    for child in range(8):
        for parent in range(4):
            tile = acc_ref[child, parent * 8 : parent * 8 + 8, :]
            far1_ref[child * 4 + parent : child * 4 + parent + 1, :] = jnp.sum(
                tile, axis=0, keepdims=True
            )


def run_far(leafxy, midxy, ra, rb, in_scale, out_scale, transfer):
    return pl.pallas_call(
        far_kernel,
        in_specs=[VMEM] * 7,
        out_specs=[VMEM] * 2,
        out_shape=[
            jax.ShapeDtypeStruct((8, 32, 128), F32),
            jax.ShapeDtypeStruct((32, 128), F32),
        ],
        scratch_shapes=[
            pltpu.VMEM((12, 8, 12, 128), F32),
            pltpu.VMEM((8, 8, 8, 128), F32),
            pltpu.VMEM((343, 128), F32),
            pltpu.VMEM((2, 49, 8, 128), F32),
            pltpu.VMEM((2, 49, 8, 128), F32),
            pltpu.VMEM((8, 32, 128), F32),
            pltpu.VMEM((1536, 128), BF16),
            pltpu.VMEM((1536, 128), BF16),
        ],
        cost_estimate=pl.CostEstimate(flops=4 << 30, bytes_accessed=4 << 20, transcendentals=0),
        compiler_params=pltpu.CompilerParams(vmem_limit_bytes=24 << 20),
        name="far",
    )(leafxy, midxy, ra, rb, in_scale, out_scale, transfer)


def force_kernel(
    far0_ref, far1_ref, pair_ref, near_ref, next_ref, in_ref, out_ref, core_ref, down_ref,
    charge_ref, front_ref, back_ref, pos_ref, wave_ref,
    forces_ref, share_ref,
    window_ref, tin_ref, tout_ref, operand_ref, mid_ref, local_ref,
):
    odd = lax.axis_index("gz") % 2
    for xy in range(36):
        rows = [
            (ref[xy : xy + 1, :], ref[36 + xy : 37 + xy, :]) for ref in (near_ref, next_ref)
        ]
        low = [jnp.where(odd == 1, rows[1][z], rows[0][z]) for z in range(2)]
        high = [jnp.where(odd == 1, rows[0][z], rows[1][z]) for z in range(2)]
        window_ref[xy] = jnp.concatenate(
            low
            + [pair_ref[xy : xy + 1, :], pair_ref[36 + xy : 37 + xy, :]]
            + high
            + [jnp.zeros((2, 128), F32)],
            axis=0,
        )
    lanes = lax.broadcasted_iota(jnp.int32, (8, 128), 0)
    near = (lanes >= 1 + odd) & (lanes <= 3 + odd)
    for xy in range(49):
        for ref, table, masked in ((tin_ref, in_ref, True), (tout_ref, out_ref, False)):
            rows = table[2, xy * 7 : xy * 7 + 7, :]
            tile = jnp.where(odd == 1, rows[0:6], rows[1:7])
            tile = jnp.concatenate([tile, jnp.zeros((2, 128), F32)], axis=0)
            if masked and 2 <= xy // 7 <= 4 and 2 <= xy % 7 <= 4:
                tile = jnp.where(near, 0.0, tile)
            ref[xy] = tile
    for qx in range(6):
        for qy in range(6):
            source = window_ref[qx * 6 + qy]
            tiles = []
            for pair in range(4):
                cx, cy = pair // 2, pair % 2
                tiles.append(source * tin_ref[(qx + 1 - cx) * 7 + qy + 1 - cy])
            start = (qx * 6 + qy) * 32
            operand_ref[start : start + 32, :] = jnp.concatenate(tiles, axis=0).astype(BF16)
    totals = [jnp.zeros((8, 128), F32) for _ in range(4)]
    for qx in range(6):
        image = dot(operand_ref[qx * 192 : qx * 192 + 192, :], core_ref[2])
        for qy in range(6):
            for pair in range(4):
                cx, cy = pair // 2, pair % 2
                scale = tout_ref[(qx + 1 - cx) * 7 + qy + 1 - cy]
                start = qy * 32 + pair * 8
                totals[pair] = totals[pair] + scale * image[start : start + 8]
    local_top = jnp.concatenate(
        [jnp.sum(total, axis=0, keepdims=True) for total in totals] + [jnp.zeros((4, 128), F32)],
        axis=0,
    ).astype(BF16)
    for child in range(8):
        cx, cy, cz = child // 4, child // 2 % 2, child % 2
        rows = far1_ref[child * 4 : child * 4 + 4, :] + dot(local_top, down_ref[1, child])[0:4]
        for parent in range(4):
            row = ((2 * (parent // 2) + cx) * 2 + cz) * 4 + 2 * (parent % 2) + cy
            mid_ref[row : row + 1, :] = rows[parent : parent + 1]
    local_mid = mid_ref[...].astype(BF16)
    for child in range(8):
        cx, cy, cz = child // 4, child // 2 % 2, child % 2
        rows = far0_ref[child] + dot(local_mid, down_ref[0, child])
        for x in range(4):
            for z in range(2):
                start = (x * 2 + z) * 4
                local_ref[2 * x + cx, 2 * z + cz, pl.ds(cy, 4, stride=2), :] = rows[start : start + 4]

    lane_box = lax.broadcasted_iota(jnp.int32, (8, 128), 1) // 32
    row_y = lax.broadcasted_iota(jnp.int32, (8, 128), 0)
    base_x = lax.axis_index("gx") * 8
    base_y = lax.axis_index("gy") * 8
    base_z = lax.axis_index("gz") * 4
    place_y0 = (base_y + row_y).astype(F32)
    place_z0 = (base_z + lane_box).astype(F32)

    def one_plane(x, sums, sines):
        local = local_ref[x].reshape(32, 128)
        weights = jnp.concatenate([local * wave_ref[d : d + 1, :] for d in range(3)], axis=0)
        high = weights.astype(BF16)
        low = (weights - high.astype(F32)).astype(BF16)
        product = dot(
            jnp.concatenate([high, low], axis=1), jnp.concatenate([sines, sines], axis=0)
        )
        charge = charge_ref[x]
        found = []
        for d in range(3):
            picked = jnp.zeros((8, 128), F32)
            for z in range(4):
                start = (d * 4 + z) * 8
                for y in range(8):
                    picked = jnp.where(
                        (row_y == y) & (lane_box == z),
                        product[start : start + 8, y * 128 : y * 128 + 128],
                        picked,
                    )
            picked = picked * charge
            forces_ref[d, x] = picked
            found.append(picked)
        places = (
            ((base_x + x).astype(F32) + pos_ref[0, x]) * (1.0 / 32),
            (place_y0 + pos_ref[1, x]) * (1.0 / 64),
            (place_z0 + pos_ref[2, x]) * (1.0 / 64),
        )
        return tuple(
            sums[d * 3 + e] + places[d] * found[e] for d in range(3) for e in range(3)
        )

    sums = (jnp.zeros((8, 128), F32),) * 9
    sums = lax.fori_loop(0, 4, lambda x, sums: one_plane(x, sums, front_ref[x]), sums)
    sums = lax.fori_loop(0, 4, lambda x, sums: one_plane(x + 4, sums, back_ref[x]), sums)
    lane = lax.broadcasted_iota(jnp.int32, (8, 128), 1)
    row = jnp.zeros((8, 128), F32)
    for i in range(9):
        row = jnp.where(lane == i, jnp.sum(sums[i]), row)
    share_ref[...] = jnp.broadcast_to(row[0:1], (512, 128))


def run_forces(far0, far1, pair, near, following, in_scale, out_scale, transfer, downward, charge, front, back, positions, wave):
    return pl.pallas_call(
        force_kernel,
        in_specs=[VMEM] * 14,
        out_specs=[VMEM] * 2,
        out_shape=[
            jax.ShapeDtypeStruct((3, 8, 8, 128), F32),
            jax.ShapeDtypeStruct((512, 128), F32),
        ],
        scratch_shapes=[
            pltpu.VMEM((36, 8, 128), F32),
            pltpu.VMEM((49, 8, 128), F32),
            pltpu.VMEM((49, 8, 128), F32),
            pltpu.VMEM((1152, 128), BF16),
            pltpu.VMEM((32, 128), F32),
            pltpu.VMEM((8, 4, 8, 128), F32),
        ],
        compiler_params=pltpu.CompilerParams(vmem_limit_bytes=24 << 20),
        name="forces",
    )(far0, far1, pair, near, following, in_scale, out_scale, transfer, downward, charge, front, back, positions, wave)


def virial_kernel(scale, rows_ref, virial_ref):
    row = jnp.sum(rows_ref[...], axis=0, keepdims=True) * scale
    for d in range(3):
        virial_ref[d : d + 1, :] = row[:, d * 3 : d * 3 + 3]


def run_virial(rows, scale):
    return pl.pallas_call(
        lambda rows_ref, virial_ref: virial_kernel(scale, rows_ref, virial_ref),
        in_specs=[VMEM],
        out_specs=VMEM,
        out_shape=jax.ShapeDtypeStruct((3, 3), F32),
        compiler_params=pltpu.CompilerParams(vmem_limit_bytes=8 << 20),
        name="virial",
    )(rows)


def swapped(value, axis, kind):
    count = lax.axis_size(axis)
    pairs = []
    for i in range(count):
        hop = (1, -1, 3)[kind]
        pairs.append((i, (i + hop) % count if i % 2 == 0 else (i - hop) % count))
    return lax.ppermute(value, axis, pairs)


def shards(
    features, positions, box_counts, w_hidden, w_charge, wave_numbers, phases,
    upward, downward, transfer, out_scale, in_scale,
):
    phases = phases.reshape(1, 128)
    charge, own, xa, xb = run_atoms(
        features, positions, box_counts.transpose(0, 2, 1), w_hidden, w_charge.reshape(1, 128),
        wave_numbers, phases, upward,
    )
    front = run_sines(positions, wave_numbers, phases, own, 0, 4)
    ra, rb = swapped(xa, "gx", 0), swapped(xb, "gx", 1)
    leaf, mid, top, ya, yb = glue_x(ra, rb, own, front)
    back = run_sines(positions, wave_numbers, phases, top, 4, 4)
    ra, rb = swapped(ya, "gy", 0), swapped(yb, "gy", 1)
    leaf, mid, top, za, zb = glue_y(ra, rb, leaf, mid, top, back)
    ra, rb = swapped(za, "gz", 0), swapped(zb, "gz", 1)
    pair = glue_z(ra, top)
    near, following = swapped(pair, "gz", 1), swapped(pair, "gz", 2)
    far0, far1 = run_far(leaf, mid, ra, rb, in_scale, out_scale, transfer)
    forces, share = run_forces(
        far0, far1, pair, near, following, in_scale, out_scale, transfer, downward, charge, front, back,
        positions, wave_numbers,
    )
    rows = lax.all_to_all(share, ("gx", "gy", "gz"), 0, 0, tiled=True)
    return forces, run_virial(rows, 1.0 / math.sqrt(4194304))


def solution(mesh):
    in_specs = (
        P("gx", "gy", "gz", None),
        P(None, "gx", "gy", "gz"),
        P("gx", "gy", "gz"),
    ) + (P(),) * 9
    out_specs = (P(None, "gx", "gy", "gz"), P())
    return jax.shard_map(shards, mesh=mesh, in_specs=in_specs, out_specs=out_specs, check_vma=False)
```

```python
import functools
import math

import jax
import jax.numpy as jnp
import numpy as np
from jax import lax
from jax.experimental import pallas as pl
from jax.experimental.pallas import tpu as pltpu
from jax.sharding import PartitionSpec as P

F32 = jnp.float32
BF16 = jnp.bfloat16
TURN = 1.0 / (2.0 * math.pi)
SIN_HALF = (4.4428679, -7.30744342, 3.59478808, -0.78437403)
COS_HALF = (1.4142135, -6.97885099, 5.73946117, -1.88356299, 0.31069819)
NT = (((1,), (1,)), ((), ()))
VMEM = pl.BlockSpec(memory_space=pltpu.VMEM)


def dot(a, b):
    return jnp.dot(a, b, preferred_element_type=F32)


def split(value):
    high = value.astype(BF16).astype(F32)
    rest = value - high
    middle = rest.astype(BF16).astype(F32)
    return high, middle, rest - middle


def wave_table(wave_ref, ph_ref, table_ref):
    blocks = []
    for d in range(3):
        high, middle, low = split(wave_ref[d : d + 1, :] * TURN)
        for part in (high, middle, low, high, middle, high):
            blocks.append(jnp.broadcast_to(part, (8, 128)))
    blocks += list(split(ph_ref[...] * TURN)) + [jnp.zeros((109, 128), F32)]
    table_ref[...] = jnp.concatenate(blocks, axis=0).T.astype(BF16)


def turns_of(step, pos_ref, table_ref):
    row_y = lax.broadcasted_iota(jnp.int32, (8, 128), 0)
    blocks = []
    for d in range(3):
        spread = []
        for part in split(pos_ref[d, step] - 0.5):
            spread.append(
                jnp.concatenate([jnp.where(row_y == y, part, 0.0) for y in range(8)], axis=1)
            )
        blocks += [spread[0]] * 3 + [spread[1]] * 2 + [spread[2]]
    blocks += [jnp.ones((8, 1024), F32), jnp.zeros((8, 1024), F32)]
    return dot(table_ref[:, 0:160], jnp.concatenate(blocks, axis=0).astype(BF16))


def poly(coefs, u):
    value = coefs[-1]
    for coef in coefs[-2::-1]:
        value = value * u + coef
    return value


def sines_kernel(start, pos_ref, wave_ref, ph_ref, _, sin_ref, table_ref):
    wave_table(wave_ref, ph_ref, table_ref)

    @pl.loop(0, sin_ref.shape[0])
    def _(x):
        turns = turns_of(start + x, pos_ref, table_ref)
        for y in range(8):
            t = turns[:, y * 128 : (y + 1) * 128]
            r = t - jnp.round(t)
            u = r * r
            sin_ref[x, :, y * 128 : (y + 1) * 128] = (
                poly(SIN_HALF, u) * r * poly(COS_HALF, u)
            ).astype(BF16)


def run_sines(positions, wave, phases, after, start, planes):
    return pl.pallas_call(
        functools.partial(sines_kernel, start),
        in_specs=[VMEM] * 4,
        out_specs=VMEM,
        out_shape=jax.ShapeDtypeStruct((planes, 128, 1024), BF16),
        scratch_shapes=[pltpu.VMEM((128, 256), BF16)],
        cost_estimate=pl.CostEstimate(flops=1 << 30, bytes_accessed=6 << 20, transcendentals=0),
        compiler_params=pltpu.CompilerParams(vmem_limit_bytes=16 << 20),
        name="sines",
    )(positions, wave, phases, after)


def atoms_kernel(
    feat_hbm, pos_hbm, cnt_hbm, wh_hbm, wc_hbm, wave_hbm, ph_hbm, up_hbm,
    charge_ref, own_ref, sa_ref, sb_ref,
    feat_ref, pos_ref, cnt_ref, wh_ref, wc_ref, wave_ref, ph_ref, up_ref, parts_ref, leaf_ref, mid_ref,
    plane_sems, sems,
):
    def plane(x):
        return pltpu.make_async_copy(feat_hbm.at[x], feat_ref.at[x], plane_sems.at[x])

    others = [
        pltpu.make_async_copy(source, target, sems.at[i])
        for i, (source, target) in enumerate(
            (
                (wave_hbm, wave_ref),
                (ph_hbm, ph_ref),
                (wc_hbm, wc_ref),
                (pos_hbm, pos_ref),
                (wh_hbm, wh_ref),
                (cnt_hbm, cnt_ref),
                (up_hbm, up_ref),
            )
        )
    ]
    for copy in others[:3]:
        copy.start()
    plane(0).start()
    for copy in others[3:6]:
        copy.start()
    for x in range(1, 8):
        plane(x).start()
    others[6].start()
    for copy in others[:3]:
        copy.wait()
    rows = []
    for d in range(3):
        high, middle, low = split(wave_ref[d : d + 1, :] * TURN)
        rows += [high, middle, low, high, middle, high]
    rows += list(split(ph_ref[...] * TURN)) + [jnp.zeros((11, 128), F32)]
    table = jnp.concatenate(rows, axis=0).astype(BF16)
    for row in range(18, 32):
        parts_ref[row * 8 : row * 8 + 8, :] = jnp.full((8, 128), 1.0 if row < 21 else 0.0, F32)
    column = jnp.broadcast_to(wc_ref[...].astype(F32), (128, 128)).T.astype(BF16)
    for copy in others[3:6]:
        copy.wait()

    @pl.loop(0, 8)
    def _(x):
        plane(x).wait()
        atoms_plane(
            x, feat_ref, pos_ref, cnt_ref, wh_ref, wc_ref, charge_ref, leaf_ref, table, column,
            parts_ref,
        )

    others[6].wait()
    atoms_lift(leaf_ref, up_ref, mid_ref, own_ref, sa_ref, sb_ref)


def atoms_plane(
    step, feat_ref, pos_ref, cnt_ref, wh_ref, wc_ref, charge_ref, leaf_ref, table, column,
    parts_ref,
):
    lane_box = lax.broadcasted_iota(jnp.int32, (8, 128), 1) // 32
    lane_slot = lax.broadcasted_iota(jnp.int32, (8, 128), 1) % 32
    row_y = lax.broadcasted_iota(jnp.int32, (8, 128), 0)
    slot = lax.broadcasted_iota(jnp.int32, (32, 128), 0)
    for d in range(3):
        high, middle, low = split(pos_ref[d, step] - 0.5)
        for i, part in enumerate((high, high, high, middle, middle, low)):
            row = (d * 6 + i) * 8
            parts_ref[row : row + 8, :] = part
    lines = [parts_ref[pl.ds(y, 32, stride=8), :].T.astype(BF16) for y in range(8)]
    turns = dot(jnp.concatenate(lines, axis=0), table)

    hidden = dot(feat_ref[step].reshape(1024, 128), wh_ref[...])
    half = hidden * 0.5
    hidden = (half + half * jnp.tanh(half)).astype(BF16)
    broad = dot(hidden, column)
    wc = jnp.broadcast_to(wc_ref[...], (8, 128))
    raw = lax.dot_general(wc, hidden, NT, preferred_element_type=F32)
    counts = jnp.zeros((8, 128), jnp.int32)
    charge = jnp.zeros((8, 128), F32)
    for y in range(8):
        charge = jnp.where(row_y == y, raw[:, y * 128 : (y + 1) * 128], charge)
        for z in range(4):
            count = cnt_ref[step, z, y]
            counts = jnp.where((row_y == y) & (lane_box == z), count, counts)
            start = y * 128 + z * 32
            t = turns[start : start + 32]
            r = t - jnp.round(t)
            s = poly(SIN_HALF, r * r) * r
            terms = jnp.where(slot < count, broad[start : start + 32], 0.0) * (1.0 - s * s)
            leaf_ref[step, z, y : y + 1, :] = jnp.sum(terms, axis=0, keepdims=True)
    charge_ref[step] = jnp.where(lane_slot < counts, charge, 0.0)


def atoms_lift(leaf_ref, up_ref, mid_ref, own_ref, sa_ref, sb_ref):
    total = jnp.zeros((32, 128), F32)
    for child in range(8):
        cx, cy, cz = child // 4, child // 2 % 2, child % 2
        rows = jnp.concatenate(
            [
                leaf_ref[2 * x + cx, 2 * z + cz, pl.ds(cy, 4, stride=2), :]
                for x in range(4)
                for z in range(2)
            ],
            axis=0,
        )
        total = total + dot(rows.astype(BF16), up_ref[0, child])
    for x in range(4):
        for z in range(2):
            for y in range(4):
                row = (x * 2 + z) * 4 + y
                mid_ref[x, y, z : z + 1, :] = total[row : row + 1]
    crown = jnp.zeros((8, 128), F32)
    for child in range(8):
        cx, cy, cz = child // 4, child // 2 % 2, child % 2
        rows = jnp.concatenate(
            [
                mid_ref[2 * x + cx, 2 * y + cy, cz : cz + 1, :]
                for x in range(2)
                for y in range(2)
            ]
            + [jnp.zeros((4, 128), F32)],
            axis=0,
        )
        crown = crown + dot(rows.astype(BF16), up_ref[1, child])
    own_ref[0:256, :] = leaf_ref[...].reshape(256, 128)
    for x in range(4):
        for y in range(4):
            row = 256 + (x * 4 + y) * 2
            own_ref[row : row + 2, :] = mid_ref[x, y]
    own_ref[288:296, :] = crown
    odd = lax.axis_index("gx") % 2
    for ref, high in ((sa_ref, 1 - odd), (sb_ref, odd)):
        for x in range(2):
            for z in range(4):
                row = (x * 4 + z) * 8
                ref[row : row + 8, :] = leaf_ref[high * 6 + x, z]
            for y in range(4):
                row = 64 + (x * 4 + y) * 2
                ref[row : row + 2, :] = mid_ref[high * 2 + x, y]
        ref[80:84, :] = crown[0:4]
        ref[84:88, :] = jnp.zeros((4, 128), F32)


def run_atoms(features, positions, box_counts, w_hidden, w_charge, wave, phases, upward):
    hbm = pl.BlockSpec(memory_space=pltpu.HBM)
    return pl.pallas_call(
        atoms_kernel,
        in_specs=[hbm] * 8,
        out_specs=[VMEM] * 4,
        out_shape=[
            jax.ShapeDtypeStruct((8, 8, 128), F32),
            jax.ShapeDtypeStruct((296, 128), F32),
            jax.ShapeDtypeStruct((88, 128), F32),
            jax.ShapeDtypeStruct((88, 128), F32),
        ],
        scratch_shapes=[
            pltpu.VMEM((8, 8, 128, 128), BF16),
            pltpu.VMEM((3, 8, 8, 128), F32),
            pltpu.SMEM((8, 4, 8), jnp.int32),
            pltpu.VMEM((128, 128), BF16),
            pltpu.VMEM((1, 128), BF16),
            pltpu.VMEM((3, 128), F32),
            pltpu.VMEM((1, 128), F32),
            pltpu.VMEM((2, 8, 128, 128), BF16),
            pltpu.VMEM((256, 128), F32),
            pltpu.VMEM((8, 4, 8, 128), F32),
            pltpu.VMEM((4, 4, 2, 128), F32),
            pltpu.SemaphoreType.DMA((8,)),
            pltpu.SemaphoreType.DMA((7,)),
        ],
        compiler_params=pltpu.CompilerParams(vmem_limit_bytes=58 << 20),
        name="atoms",
    )(features, positions, box_counts, w_hidden, w_charge, wave, phases, upward)


def glue_x_kernel(ra_ref, rb_ref, own_ref, _, __, leafx_ref, midx_ref, topx_ref, ya_ref, yb_ref):
    odd = lax.axis_index("gx") % 2
    leafx_ref[2:10] = own_ref[0:256, :].reshape(8, 4, 8, 128)
    for x in range(4):
        for y in range(4):
            row = 256 + (x * 4 + y) * 2
            midx_ref[2 + x, y] = own_ref[row : row + 2, :]
    for ref, high in ((ra_ref, 1 - odd), (rb_ref, odd)):
        for x in range(2):
            for z in range(4):
                row = (x * 4 + z) * 8
                leafx_ref[high * 10 + x, z] = ref[row : row + 8, :]
            for y in range(4):
                row = 64 + (x * 4 + y) * 2
                midx_ref[high * 6 + x, y] = ref[row : row + 2, :]
    ta, tb = ra_ref[80:84, :], rb_ref[80:84, :]
    topx_ref[...] = jnp.concatenate(
        [
            jnp.where(odd == 1, ta, tb),
            own_ref[288:292, :],
            jnp.where(odd == 1, tb, ta),
            jnp.zeros((4, 128), F32),
        ],
        axis=0,
    )
    odd_y = lax.axis_index("gy") % 2
    for x in range(12):
        for z in range(4):
            tile = leafx_ref[x, z]
            low, high = tile[0:2], tile[6:8]
            row = (x * 4 + z) * 2
            ya_ref[row : row + 2, :] = jnp.where(odd_y == 1, low, high)
            yb_ref[row : row + 2, :] = jnp.where(odd_y == 1, high, low)
    for ref, side in ((ya_ref, 1 - odd_y), (yb_ref, odd_y)):
        for x in range(8):
            for y in range(2):
                row = 96 + (x * 2 + y) * 2
                ref[row : row + 2, :] = midx_ref[x, side * 2 + y]
        ref[128:144, :] = topx_ref[...]


def glue_x(ra, rb, own, front, scale):
    return pl.pallas_call(
        glue_x_kernel,
        in_specs=[VMEM] * 3 + [pl.BlockSpec(memory_space=pl.ANY)] * 2,
        out_specs=[VMEM] * 5,
        out_shape=[
            jax.ShapeDtypeStruct((12, 4, 8, 128), F32),
            jax.ShapeDtypeStruct((8, 4, 2, 128), F32),
            jax.ShapeDtypeStruct((16, 128), F32),
            jax.ShapeDtypeStruct((144, 128), F32),
            jax.ShapeDtypeStruct((144, 128), F32),
        ],
        compiler_params=pltpu.CompilerParams(vmem_limit_bytes=8 << 20),
        name="glue_x",
    )(ra, rb, own, front, scale)


def glue_y_kernel(ra_ref, rb_ref, leafx_ref, midx_ref, topx_ref, _, leafxy_ref, midxy_ref, topxy_ref, za_ref, zb_ref):
    odd = lax.axis_index("gy") % 2
    for x in range(12):
        for z in range(4):
            row = (x * 4 + z) * 2
            a, b = ra_ref[row : row + 2, :], rb_ref[row : row + 2, :]
            leafxy_ref[x, z, 0:2, :] = jnp.where(odd == 1, a, b)
            leafxy_ref[x, z, 2:10, :] = leafx_ref[x, z]
            leafxy_ref[x, z, 10:12, :] = jnp.where(odd == 1, b, a)
    for x in range(8):
        midxy_ref[x, 2:6] = midx_ref[x]
        for ref, high in ((ra_ref, 1 - odd), (rb_ref, odd)):
            for y in range(2):
                row = 96 + (x * 2 + y) * 2
                midxy_ref[x, high * 6 + y] = ref[row : row + 2, :]
    for x in range(6):
        row = 128 + x * 2
        a, b = ra_ref[row : row + 2, :], rb_ref[row : row + 2, :]
        topxy_ref[x * 6 : x * 6 + 2, :] = jnp.where(odd == 1, a, b)
        topxy_ref[x * 6 + 2 : x * 6 + 4, :] = topx_ref[x * 2 : x * 2 + 2, :]
        topxy_ref[x * 6 + 4 : x * 6 + 6, :] = jnp.where(odd == 1, b, a)
    topxy_ref[36:40, :] = jnp.zeros((4, 128), F32)
    odd_z = lax.axis_index("gz") % 2
    for ref, side in ((za_ref, 1 - odd_z), (zb_ref, odd_z)):
        for x in range(12):
            for z in range(2):
                row = (x * 2 + z) * 12
                ref[row : row + 12, :] = leafxy_ref[x, side * 2 + z]
        for x in range(8):
            for y in range(8):
                row = 288 + (x * 8 + y) * 2
                ref[row : row + 2, :] = midxy_ref[x, y]
    za_ref[416:456, :] = topxy_ref[...]


def glue_y(ra, rb, leafx, midx, topx, back):
    return pl.pallas_call(
        glue_y_kernel,
        in_specs=[VMEM] * 5 + [pl.BlockSpec(memory_space=pl.ANY)],
        out_specs=[VMEM] * 5,
        out_shape=[
            jax.ShapeDtypeStruct((12, 4, 12, 128), F32),
            jax.ShapeDtypeStruct((8, 8, 2, 128), F32),
            jax.ShapeDtypeStruct((40, 128), F32),
            jax.ShapeDtypeStruct((456, 128), F32),
            jax.ShapeDtypeStruct((416, 128), F32),
        ],
        compiler_params=pltpu.CompilerParams(vmem_limit_bytes=8 << 20),
        name="glue_y",
    )(ra, rb, leafx, midx, topx, back)


def glue_z_kernel(ra_ref, topxy_ref, pair_ref):
    odd = lax.axis_index("gz") % 2
    mine, other = topxy_ref[0:36, :], ra_ref[416:452, :]
    pair_ref[...] = jnp.concatenate(
        [jnp.where(odd == 1, other, mine), jnp.where(odd == 1, mine, other)], axis=0
    )


def glue_z(ra, topxy):
    return pl.pallas_call(
        glue_z_kernel,
        in_specs=[VMEM] * 2,
        out_specs=VMEM,
        out_shape=jax.ShapeDtypeStruct((72, 128), F32),
        compiler_params=pltpu.CompilerParams(vmem_limit_bytes=8 << 20),
        name="glue_z",
    )(ra, topxy)


def offset_tiles(out_ref, table, cz, masked):
    zero = jnp.zeros((2, 128), F32)
    keep_rows = lax.broadcasted_iota(jnp.int32, (8, 128), 0)
    near = (keep_rows >= 1 + cz) & (keep_rows <= 3 + cz)
    for xy in range(49):
        start = xy * 7 + 1 - cz
        tile = jnp.concatenate([table[start : start + 6, :], zero], axis=0)
        if masked and 2 <= xy // 7 <= 4 and 2 <= xy % 7 <= 4:
            tile = jnp.where(near, 0.0, tile)
        out_ref[xy] = tile


def tables_kernel(in_ref, out_ref, _, scale_ref, tin_ref, tout_ref, top_in_ref, top_out_ref):
    scale_ref[...] = in_ref[0]
    for x in range(2, 5):
        for y in range(2, 5):
            row = x * 49 + y * 7 + 2
            scale_ref[row : row + 3, :] = jnp.zeros((3, 128), F32)
    for cz in range(2):
        offset_tiles(tin_ref.at[cz], in_ref.at[1], cz, True)
        offset_tiles(tout_ref.at[cz], out_ref.at[1], cz, False)
    odd = lax.axis_index("gz") % 2
    lanes = lax.broadcasted_iota(jnp.int32, (8, 128), 0)
    near = (lanes >= 1 + odd) & (lanes <= 3 + odd)
    for xy in range(49):
        for ref, table, masked in ((top_in_ref, in_ref, True), (top_out_ref, out_ref, False)):
            rows = table[2, xy * 7 : xy * 7 + 7, :]
            tile = jnp.where(odd == 1, rows[0:6], rows[1:7])
            tile = jnp.concatenate([tile, jnp.zeros((2, 128), F32)], axis=0)
            if masked and 2 <= xy // 7 <= 4 and 2 <= xy % 7 <= 4:
                tile = jnp.where(near, 0.0, tile)
            ref[xy] = tile


def run_tables(in_scale, out_scale, after):
    return pl.pallas_call(
        tables_kernel,
        in_specs=[VMEM] * 2 + [pl.BlockSpec(memory_space=pl.ANY)],
        out_specs=[VMEM] * 5,
        out_shape=[
            jax.ShapeDtypeStruct((343, 128), F32),
            jax.ShapeDtypeStruct((2, 49, 8, 128), F32),
            jax.ShapeDtypeStruct((2, 49, 8, 128), F32),
            jax.ShapeDtypeStruct((49, 8, 128), F32),
            jax.ShapeDtypeStruct((49, 8, 128), F32),
        ],
        cost_estimate=pl.CostEstimate(flops=1 << 28, bytes_accessed=3 << 20, transcendentals=0),
        compiler_params=pltpu.CompilerParams(vmem_limit_bytes=8 << 20),
        name="tables",
    )(in_scale, out_scale, after)


def far_kernel(
    leafxy_ref, midxy_ref, ra_ref, rb_ref, scale_ref, tin_ref, tout_ref, out_ref, core_ref,
    far0_ref, far1_ref,
    leaf_ref, mid_ref, acc_ref, even_ref, odd_ref,
):
    odd = lax.axis_index("gz") % 2
    leaf_ref[:, 2:6] = leafxy_ref[...]
    for ref, high in ((ra_ref, 1 - odd), (rb_ref, odd)):
        for x in range(12):
            for z in range(2):
                row = (x * 2 + z) * 12
                leaf_ref[x, high * 6 + z] = ref[row : row + 12, :]
    for x in range(8):
        for y in range(8):
            row = 288 + (x * 8 + y) * 2
            a, b = ra_ref[row : row + 2, :], rb_ref[row : row + 2, :]
            mid_ref[x, y] = jnp.concatenate(
                [
                    jnp.where(odd == 1, a, b),
                    midxy_ref[x, y],
                    jnp.where(odd == 1, b, a),
                    jnp.zeros((2, 128), F32),
                ],
                axis=0,
            )
    far0_ref[...] = jnp.zeros((8, 32, 128), F32)
    core0 = core_ref[0]

    def row_of(qx, qy, qz, pair, cz):
        return (qx + 1 - pair // 2) * 49 + (qy + 1 - pair % 2) * 7 + qz + 1 - cz

    def build_leaf(step, operand_ref):
        qx, qz = step // 6, step % 6
        for qy in range(6):
            tiles = []
            for x in range(4):
                for z in range(2):
                    tiles.append(leaf_ref[2 * x + qx, 2 * z + qz, pl.ds(qy, 4, stride=2), :])
            source = jnp.concatenate(tiles, axis=0)
            for pair in range(4):
                for cz in range(2):
                    start = ((pair * 2 + cz) * 6 + qy) * 32
                    row = row_of(qx, qy, qz, pair, cz)
                    scale = jnp.broadcast_to(scale_ref[pl.ds(row, 1), :], (32, 128))
                    operand_ref[start : start + 32, :] = (source * scale).astype(BF16)

    def apply_leaf(step, image):
        qx, qz = step // 6, step % 6
        for pair in range(4):
            for cz in range(2):
                total = far0_ref[pair * 2 + cz]
                for qy in range(6):
                    row = row_of(qx, qy, qz, pair, cz)
                    scale = jnp.broadcast_to(out_ref[0, pl.ds(row, 1), :], (32, 128))
                    start = ((pair * 2 + cz) * 6 + qy) * 32
                    total = total + scale * image[start : start + 32]
                far0_ref[pair * 2 + cz] = total

    build_leaf(0, even_ref)

    @pl.loop(0, 18)
    def _(turn):
        image = dot(even_ref[...], core0)
        build_leaf(2 * turn + 1, odd_ref)
        apply_leaf(2 * turn, image)
        image = dot(odd_ref[...], core0)
        build_leaf(jnp.minimum(2 * turn + 2, 35), even_ref)
        apply_leaf(2 * turn + 1, image)

    acc_ref[...] = jnp.zeros((8, 32, 128), F32)
    core1 = core_ref[1]

    def build_mid(qx, operand_ref):
        for qy in range(6):
            tiles = [mid_ref[2 * x + qx, 2 * y + qy] for x in range(2) for y in range(2)]
            for pair in range(4):
                xy = (qx + 1 - pair // 2) * 7 + qy + 1 - pair % 2
                for cz in range(2):
                    scale = tin_ref[cz, xy]
                    start = ((pair * 2 + cz) * 6 + qy) * 32
                    operand_ref[start : start + 32, :] = jnp.concatenate(
                        [tile * scale for tile in tiles], axis=0
                    ).astype(BF16)

    def apply_mid(qx, image):
        for pair in range(4):
            for cz in range(2):
                total = acc_ref[pair * 2 + cz]
                for qy in range(6):
                    scale = tout_ref[cz, (qx + 1 - pair // 2) * 7 + qy + 1 - pair % 2]
                    scale = jnp.concatenate([scale] * 4, axis=0)
                    start = ((pair * 2 + cz) * 6 + qy) * 32
                    total = total + scale * image[start : start + 32]
                acc_ref[pair * 2 + cz] = total

    build_mid(0, even_ref)

    @pl.loop(0, 3)
    def _(turn):
        image = dot(even_ref[...], core1)
        build_mid(2 * turn + 1, odd_ref)
        apply_mid(2 * turn, image)
        image = dot(odd_ref[...], core1)
        build_mid(jnp.minimum(2 * turn + 2, 5), even_ref)
        apply_mid(2 * turn + 1, image)

    for child in range(8):
        for parent in range(4):
            tile = acc_ref[child, parent * 8 : parent * 8 + 8, :]
            far1_ref[child * 4 + parent : child * 4 + parent + 1, :] = jnp.sum(
                tile, axis=0, keepdims=True
            )


def run_far(leafxy, midxy, ra, rb, scale, tin, tout, out_scale, transfer):
    return pl.pallas_call(
        far_kernel,
        in_specs=[VMEM] * 9,
        out_specs=[VMEM] * 2,
        out_shape=[
            jax.ShapeDtypeStruct((8, 32, 128), F32),
            jax.ShapeDtypeStruct((32, 128), F32),
        ],
        scratch_shapes=[
            pltpu.VMEM((12, 8, 12, 128), F32),
            pltpu.VMEM((8, 8, 8, 128), F32),
            pltpu.VMEM((8, 32, 128), F32),
            pltpu.VMEM((1536, 128), BF16),
            pltpu.VMEM((1536, 128), BF16),
        ],
        cost_estimate=pl.CostEstimate(flops=4 << 30, bytes_accessed=4 << 20, transcendentals=0),
        compiler_params=pltpu.CompilerParams(vmem_limit_bytes=24 << 20),
        name="far",
    )(leafxy, midxy, ra, rb, scale, tin, tout, out_scale, transfer)


def force_kernel(
    far0_ref, far1_ref, pair_ref, near_ref, next_ref, tin_ref, tout_ref, core_ref, down_ref,
    charge_ref, front_ref, back_ref, pos_ref, wave_ref,
    forces_ref, share_ref,
    window_ref, operand_ref, mid_ref, local_ref,
):
    odd = lax.axis_index("gz") % 2
    for xy in range(36):
        rows = [
            (ref[xy : xy + 1, :], ref[36 + xy : 37 + xy, :]) for ref in (near_ref, next_ref)
        ]
        low = [jnp.where(odd == 1, rows[1][z], rows[0][z]) for z in range(2)]
        high = [jnp.where(odd == 1, rows[0][z], rows[1][z]) for z in range(2)]
        window_ref[xy] = jnp.concatenate(
            low
            + [pair_ref[xy : xy + 1, :], pair_ref[36 + xy : 37 + xy, :]]
            + high
            + [jnp.zeros((2, 128), F32)],
            axis=0,
        )
    for qx in range(6):
        for qy in range(6):
            source = window_ref[qx * 6 + qy]
            tiles = []
            for pair in range(4):
                cx, cy = pair // 2, pair % 2
                tiles.append(source * tin_ref[(qx + 1 - cx) * 7 + qy + 1 - cy])
            start = (qx * 6 + qy) * 32
            operand_ref[start : start + 32, :] = jnp.concatenate(tiles, axis=0).astype(BF16)
    totals = [jnp.zeros((8, 128), F32) for _ in range(4)]
    for qx in range(6):
        image = dot(operand_ref[qx * 192 : qx * 192 + 192, :], core_ref[2])
        for qy in range(6):
            for pair in range(4):
                cx, cy = pair // 2, pair % 2
                scale = tout_ref[(qx + 1 - cx) * 7 + qy + 1 - cy]
                start = qy * 32 + pair * 8
                totals[pair] = totals[pair] + scale * image[start : start + 8]
    local_top = jnp.concatenate(
        [jnp.sum(total, axis=0, keepdims=True) for total in totals] + [jnp.zeros((4, 128), F32)],
        axis=0,
    ).astype(BF16)
    for child in range(8):
        cx, cy, cz = child // 4, child // 2 % 2, child % 2
        rows = far1_ref[child * 4 : child * 4 + 4, :] + dot(local_top, down_ref[1, child])[0:4]
        for parent in range(4):
            row = ((2 * (parent // 2) + cx) * 2 + cz) * 4 + 2 * (parent % 2) + cy
            mid_ref[row : row + 1, :] = rows[parent : parent + 1]
    local_mid = mid_ref[...].astype(BF16)
    for child in range(8):
        cx, cy, cz = child // 4, child // 2 % 2, child % 2
        rows = far0_ref[child] + dot(local_mid, down_ref[0, child])
        for x in range(4):
            for z in range(2):
                start = (x * 2 + z) * 4
                local_ref[2 * x + cx, 2 * z + cz, pl.ds(cy, 4, stride=2), :] = rows[start : start + 4]

    lane_box = lax.broadcasted_iota(jnp.int32, (8, 128), 1) // 32
    row_y = lax.broadcasted_iota(jnp.int32, (8, 128), 0)
    base_x = lax.axis_index("gx") * 8
    base_y = lax.axis_index("gy") * 8
    base_z = lax.axis_index("gz") * 4
    place_y0 = (base_y + row_y).astype(F32)
    place_z0 = (base_z + lane_box).astype(F32)

    def one_plane(x, sums, sines):
        local = local_ref[x].reshape(32, 128)
        weights = jnp.concatenate([local * wave_ref[d : d + 1, :] for d in range(3)], axis=0)
        high = weights.astype(BF16)
        low = (weights - high.astype(F32)).astype(BF16)
        product = dot(
            jnp.concatenate([high, low], axis=1), jnp.concatenate([sines, sines], axis=0)
        )
        charge = charge_ref[x]
        found = []
        for d in range(3):
            picked = jnp.zeros((8, 128), F32)
            for z in range(4):
                start = (d * 4 + z) * 8
                for y in range(8):
                    picked = jnp.where(
                        (row_y == y) & (lane_box == z),
                        product[start : start + 8, y * 128 : y * 128 + 128],
                        picked,
                    )
            picked = picked * charge
            forces_ref[d, x] = picked
            found.append(picked)
        places = (
            ((base_x + x).astype(F32) + pos_ref[0, x]) * (1.0 / 32),
            (place_y0 + pos_ref[1, x]) * (1.0 / 64),
            (place_z0 + pos_ref[2, x]) * (1.0 / 64),
        )
        return tuple(
            sums[d * 3 + e] + places[d] * found[e] for d in range(3) for e in range(3)
        )

    sums = (jnp.zeros((8, 128), F32),) * 9
    sums = lax.fori_loop(0, 4, lambda x, sums: one_plane(x, sums, front_ref[x]), sums)
    sums = lax.fori_loop(0, 4, lambda x, sums: one_plane(x + 4, sums, back_ref[x]), sums)
    lane = lax.broadcasted_iota(jnp.int32, (8, 128), 1)
    row = jnp.zeros((8, 128), F32)
    for i in range(9):
        row = jnp.where(lane == i, jnp.sum(sums[i]), row)
    share_ref[...] = jnp.broadcast_to(row[0:1], (512, 128))


def run_forces(far0, far1, pair, near, following, top_in, top_out, transfer, downward, charge, front, back, positions, wave):
    return pl.pallas_call(
        force_kernel,
        in_specs=[VMEM] * 14,
        out_specs=[VMEM] * 2,
        out_shape=[
            jax.ShapeDtypeStruct((3, 8, 8, 128), F32),
            jax.ShapeDtypeStruct((512, 128), F32),
        ],
        scratch_shapes=[
            pltpu.VMEM((36, 8, 128), F32),
            pltpu.VMEM((1152, 128), BF16),
            pltpu.VMEM((32, 128), F32),
            pltpu.VMEM((8, 4, 8, 128), F32),
        ],
        compiler_params=pltpu.CompilerParams(vmem_limit_bytes=24 << 20),
        name="forces",
    )(far0, far1, pair, near, following, top_in, top_out, transfer, downward, charge, front, back, positions, wave)


def virial_kernel(scale, rows_ref, virial_ref):
    row = jnp.sum(rows_ref[...], axis=0, keepdims=True) * scale
    for d in range(3):
        virial_ref[d : d + 1, :] = row[:, d * 3 : d * 3 + 3]


def run_virial(rows, scale):
    return pl.pallas_call(
        lambda rows_ref, virial_ref: virial_kernel(scale, rows_ref, virial_ref),
        in_specs=[VMEM],
        out_specs=VMEM,
        out_shape=jax.ShapeDtypeStruct((3, 3), F32),
        compiler_params=pltpu.CompilerParams(vmem_limit_bytes=8 << 20),
        name="virial",
    )(rows)


def swapped(value, axis, kind):
    count = lax.axis_size(axis)
    pairs = []
    for i in range(count):
        hop = (1, -1, 3)[kind]
        pairs.append((i, (i + hop) % count if i % 2 == 0 else (i - hop) % count))
    return lax.ppermute(value, axis, pairs)


def shards(
    features, positions, box_counts, w_hidden, w_charge, wave_numbers, phases,
    upward, downward, transfer, out_scale, in_scale,
):
    phases = phases.reshape(1, 128)
    charge, own, xa, xb = run_atoms(
        features, positions, box_counts.transpose(0, 2, 1), w_hidden, w_charge.reshape(1, 128),
        wave_numbers, phases, upward,
    )
    front = run_sines(positions, wave_numbers, phases, own, 0, 4)
    scale, tin, tout, top_in, top_out = run_tables(in_scale, out_scale, own)
    ra, rb = swapped(xa, "gx", 0), swapped(xb, "gx", 1)
    leaf, mid, top, ya, yb = glue_x(ra, rb, own, front, scale)
    back = run_sines(positions, wave_numbers, phases, top, 4, 4)
    ra, rb = swapped(ya, "gy", 0), swapped(yb, "gy", 1)
    leaf, mid, top, za, zb = glue_y(ra, rb, leaf, mid, top, back)
    ra, rb = swapped(za, "gz", 0), swapped(zb, "gz", 1)
    pair = glue_z(ra, top)
    near, following = swapped(pair, "gz", 1), swapped(pair, "gz", 2)
    far0, far1 = run_far(leaf, mid, ra, rb, scale, tin, tout, out_scale, transfer)
    forces, share = run_forces(
        far0, far1, pair, near, following, top_in, top_out, transfer, downward, charge, front, back,
        positions, wave_numbers,
    )
    rows = lax.all_to_all(share, ("gx", "gy", "gz"), 0, 0, tiled=True)
    return forces, run_virial(rows, 1.0 / math.sqrt(4194304))


def solution(mesh):
    in_specs = (
        P("gx", "gy", "gz", None),
        P(None, "gx", "gy", "gz"),
        P("gx", "gy", "gz"),
    ) + (P(),) * 9
    out_specs = (P(None, "gx", "gy", "gz"), P())
    return jax.shard_map(shards, mesh=mesh, in_specs=in_specs, out_specs=out_specs, check_vma=False)
```

```python
import functools
import math

import jax
import jax.numpy as jnp
import numpy as np
from jax import lax
from jax.experimental import pallas as pl
from jax.experimental.pallas import tpu as pltpu
from jax.sharding import PartitionSpec as P

F32 = jnp.float32
BF16 = jnp.bfloat16
TURN = 1.0 / (2.0 * math.pi)
SIN_HALF = (4.4428679, -7.30744342, 3.59478808, -0.78437403)
COS_HALF = (1.4142135, -6.97885099, 5.73946117, -1.88356299, 0.31069819)
NT = (((1,), (1,)), ((), ()))
VMEM = pl.BlockSpec(memory_space=pltpu.VMEM)


def dot(a, b):
    return jnp.dot(a, b, preferred_element_type=F32)


def split(value):
    high = value.astype(BF16).astype(F32)
    rest = value - high
    middle = rest.astype(BF16).astype(F32)
    return high, middle, rest - middle


def wave_table(wave_ref, ph_ref, table_ref):
    blocks = []
    for d in range(3):
        high, middle, low = split(wave_ref[d : d + 1, :] * TURN)
        for part in (high, middle, low, high, middle, high):
            blocks.append(jnp.broadcast_to(part, (8, 128)))
    blocks += list(split(ph_ref[...] * TURN)) + [jnp.zeros((109, 128), F32)]
    table_ref[...] = jnp.concatenate(blocks, axis=0).T.astype(BF16)


def turns_of(step, pos_ref, table_ref):
    row_y = lax.broadcasted_iota(jnp.int32, (8, 128), 0)
    blocks = []
    for d in range(3):
        spread = []
        for part in split(pos_ref[d, step] - 0.5):
            spread.append(
                jnp.concatenate([jnp.where(row_y == y, part, 0.0) for y in range(8)], axis=1)
            )
        blocks += [spread[0]] * 3 + [spread[1]] * 2 + [spread[2]]
    blocks += [jnp.ones((8, 1024), F32), jnp.zeros((8, 1024), F32)]
    return dot(table_ref[:, 0:160], jnp.concatenate(blocks, axis=0).astype(BF16))


def poly(coefs, u):
    value = coefs[-1]
    for coef in coefs[-2::-1]:
        value = value * u + coef
    return value


def sines_kernel(start, pos_ref, wave_ref, ph_ref, _, sin_ref, table_ref):
    wave_table(wave_ref, ph_ref, table_ref)

    @pl.loop(0, sin_ref.shape[0])
    def _(x):
        turns = turns_of(start + x, pos_ref, table_ref)
        for y in range(8):
            t = turns[:, y * 128 : (y + 1) * 128]
            r = t - jnp.round(t)
            u = r * r
            sin_ref[x, :, y * 128 : (y + 1) * 128] = (
                poly(SIN_HALF, u) * r * poly(COS_HALF, u)
            ).astype(BF16)


def front_kernel(pos_ref, wave_ref, ph_ref, own_ref, sin_ref, send_ref, table_ref):
    side = 1 - lax.axis_index("gx") % 2
    send_ref[0:64, :] = own_ref[pl.ds(pl.multiple_of(side * 192, 8), 64), :]
    send_ref[64:80, :] = own_ref[pl.ds(pl.multiple_of(256 + side * 16, 8), 16), :]
    send_ref[80:88, :] = own_ref[288:296, :]
    sines_kernel(0, pos_ref, wave_ref, ph_ref, None, sin_ref, table_ref)


def run_front(positions, wave, phases, own, planes):
    return pl.pallas_call(
        front_kernel,
        in_specs=[VMEM] * 4,
        out_specs=[VMEM] * 2,
        out_shape=[
            jax.ShapeDtypeStruct((planes, 128, 1024), BF16),
            jax.ShapeDtypeStruct((88, 128), F32),
        ],
        scratch_shapes=[pltpu.VMEM((128, 256), BF16)],
        cost_estimate=pl.CostEstimate(flops=1 << 30, bytes_accessed=6 << 20, transcendentals=0),
        compiler_params=pltpu.CompilerParams(vmem_limit_bytes=16 << 20),
        name="front",
    )(positions, wave, phases, own)


def run_sines(positions, wave, phases, after, start, planes):
    return pl.pallas_call(
        functools.partial(sines_kernel, start),
        in_specs=[VMEM] * 4,
        out_specs=VMEM,
        out_shape=jax.ShapeDtypeStruct((planes, 128, 1024), BF16),
        scratch_shapes=[pltpu.VMEM((128, 256), BF16)],
        cost_estimate=pl.CostEstimate(flops=1 << 30, bytes_accessed=6 << 20, transcendentals=0),
        compiler_params=pltpu.CompilerParams(vmem_limit_bytes=16 << 20),
        name="sines",
    )(positions, wave, phases, after)


def atoms_kernel(
    feat_hbm, pos_hbm, cnt_hbm, wh_hbm, wc_hbm, wave_hbm, ph_hbm, up_hbm,
    charge_ref, own_ref, sb_ref,
    feat_ref, pos_ref, cnt_ref, wh_ref, wc_ref, wave_ref, ph_ref, up_ref, parts_ref, leaf_ref, mid_ref,
    plane_sems, sems,
):
    def plane(x):
        return pltpu.make_async_copy(feat_hbm.at[x], feat_ref.at[x], plane_sems.at[x])

    others = [
        pltpu.make_async_copy(source, target, sems.at[i])
        for i, (source, target) in enumerate(
            (
                (wave_hbm, wave_ref),
                (ph_hbm, ph_ref),
                (wc_hbm, wc_ref),
                (pos_hbm, pos_ref),
                (wh_hbm, wh_ref),
                (cnt_hbm, cnt_ref),
                (up_hbm, up_ref),
            )
        )
    ]
    for copy in others[:3]:
        copy.start()
    plane(0).start()
    for copy in others[3:6]:
        copy.start()
    for x in range(1, 8):
        plane(x).start()
    others[6].start()
    for copy in others[:3]:
        copy.wait()
    rows = []
    for d in range(3):
        high, middle, low = split(wave_ref[d : d + 1, :] * TURN)
        rows += [high, middle, low, high, middle, high]
    rows += list(split(ph_ref[...] * TURN)) + [jnp.zeros((11, 128), F32)]
    table = jnp.concatenate(rows, axis=0).astype(BF16)
    for row in range(18, 32):
        parts_ref[row * 8 : row * 8 + 8, :] = jnp.full((8, 128), 1.0 if row < 21 else 0.0, F32)
    column = jnp.broadcast_to(wc_ref[...].astype(F32), (128, 128)).T.astype(BF16)
    for copy in others[3:6]:
        copy.wait()

    @pl.loop(0, 8)
    def _(x):
        plane(x).wait()
        atoms_plane(
            x, feat_ref, pos_ref, cnt_ref, wh_ref, wc_ref, charge_ref, leaf_ref, table, column,
            parts_ref,
        )

    others[6].wait()
    atoms_lift(leaf_ref, up_ref, mid_ref, own_ref, sb_ref)


def atoms_plane(
    step, feat_ref, pos_ref, cnt_ref, wh_ref, wc_ref, charge_ref, leaf_ref, table, column,
    parts_ref,
):
    lane_box = lax.broadcasted_iota(jnp.int32, (8, 128), 1) // 32
    lane_slot = lax.broadcasted_iota(jnp.int32, (8, 128), 1) % 32
    row_y = lax.broadcasted_iota(jnp.int32, (8, 128), 0)
    slot = lax.broadcasted_iota(jnp.int32, (32, 128), 0)
    for d in range(3):
        high, middle, low = split(pos_ref[d, step] - 0.5)
        for i, part in enumerate((high, high, high, middle, middle, low)):
            row = (d * 6 + i) * 8
            parts_ref[row : row + 8, :] = part
    lines = [parts_ref[pl.ds(y, 32, stride=8), :].T.astype(BF16) for y in range(8)]
    turns = dot(jnp.concatenate(lines, axis=0), table)

    hidden = dot(feat_ref[step].reshape(1024, 128), wh_ref[...])
    half = hidden * 0.5
    hidden = (half + half * jnp.tanh(half)).astype(BF16)
    broad = dot(hidden, column)
    wc = jnp.broadcast_to(wc_ref[...], (8, 128))
    raw = lax.dot_general(wc, hidden, NT, preferred_element_type=F32)
    counts = jnp.zeros((8, 128), jnp.int32)
    charge = jnp.zeros((8, 128), F32)
    for y in range(8):
        charge = jnp.where(row_y == y, raw[:, y * 128 : (y + 1) * 128], charge)
        for z in range(4):
            count = cnt_ref[step, z, y]
            counts = jnp.where((row_y == y) & (lane_box == z), count, counts)
            start = y * 128 + z * 32
            t = turns[start : start + 32]
            r = t - jnp.round(t)
            s = poly(SIN_HALF, r * r) * r
            terms = jnp.where(slot < count, broad[start : start + 32], 0.0) * (1.0 - s * s)
            leaf_ref[step, z, y : y + 1, :] = jnp.sum(terms, axis=0, keepdims=True)
    charge_ref[step] = jnp.where(lane_slot < counts, charge, 0.0)


def atoms_lift(leaf_ref, up_ref, mid_ref, own_ref, sb_ref):
    total = jnp.zeros((32, 128), F32)
    for child in range(8):
        cx, cy, cz = child // 4, child // 2 % 2, child % 2
        rows = jnp.concatenate(
            [
                leaf_ref[2 * x + cx, 2 * z + cz, pl.ds(cy, 4, stride=2), :]
                for x in range(4)
                for z in range(2)
            ],
            axis=0,
        )
        total = total + dot(rows.astype(BF16), up_ref[0, child])
    for x in range(4):
        for z in range(2):
            for y in range(4):
                row = (x * 2 + z) * 4 + y
                mid_ref[x, y, z : z + 1, :] = total[row : row + 1]
    crown = jnp.zeros((8, 128), F32)
    for child in range(8):
        cx, cy, cz = child // 4, child // 2 % 2, child % 2
        rows = jnp.concatenate(
            [
                mid_ref[2 * x + cx, 2 * y + cy, cz : cz + 1, :]
                for x in range(2)
                for y in range(2)
            ]
            + [jnp.zeros((4, 128), F32)],
            axis=0,
        )
        crown = crown + dot(rows.astype(BF16), up_ref[1, child])
    own_ref[0:256, :] = leaf_ref[...].reshape(256, 128)
    for x in range(4):
        for y in range(4):
            row = 256 + (x * 4 + y) * 2
            own_ref[row : row + 2, :] = mid_ref[x, y]
    own_ref[288:296, :] = crown
    odd = lax.axis_index("gx") % 2
    for ref, high in ((sb_ref, odd),):
        for x in range(2):
            for z in range(4):
                row = (x * 4 + z) * 8
                ref[row : row + 8, :] = leaf_ref[high * 6 + x, z]
            for y in range(4):
                row = 64 + (x * 4 + y) * 2
                ref[row : row + 2, :] = mid_ref[high * 2 + x, y]
        ref[80:84, :] = crown[0:4]
        ref[84:88, :] = jnp.zeros((4, 128), F32)


def run_atoms(features, positions, box_counts, w_hidden, w_charge, wave, phases, upward):
    hbm = pl.BlockSpec(memory_space=pltpu.HBM)
    return pl.pallas_call(
        atoms_kernel,
        in_specs=[hbm] * 8,
        out_specs=[VMEM] * 3,
        out_shape=[
            jax.ShapeDtypeStruct((8, 8, 128), F32),
            jax.ShapeDtypeStruct((296, 128), F32),
            jax.ShapeDtypeStruct((88, 128), F32),
        ],
        scratch_shapes=[
            pltpu.VMEM((8, 8, 128, 128), BF16),
            pltpu.VMEM((3, 8, 8, 128), F32),
            pltpu.SMEM((8, 4, 8), jnp.int32),
            pltpu.VMEM((128, 128), BF16),
            pltpu.VMEM((1, 128), BF16),
            pltpu.VMEM((3, 128), F32),
            pltpu.VMEM((1, 128), F32),
            pltpu.VMEM((2, 8, 128, 128), BF16),
            pltpu.VMEM((256, 128), F32),
            pltpu.VMEM((8, 4, 8, 128), F32),
            pltpu.VMEM((4, 4, 2, 128), F32),
            pltpu.SemaphoreType.DMA((8,)),
            pltpu.SemaphoreType.DMA((7,)),
        ],
        compiler_params=pltpu.CompilerParams(vmem_limit_bytes=58 << 20),
        name="atoms",
    )(features, positions, box_counts, w_hidden, w_charge, wave, phases, upward)


def glue_x_kernel(ra_ref, rb_ref, own_ref, _, __, leafx_ref, midx_ref, topx_ref, ya_ref, yb_ref):
    odd = lax.axis_index("gx") % 2
    leafx_ref[2:10] = own_ref[0:256, :].reshape(8, 4, 8, 128)
    for x in range(4):
        for y in range(4):
            row = 256 + (x * 4 + y) * 2
            midx_ref[2 + x, y] = own_ref[row : row + 2, :]
    for ref, high in ((ra_ref, 1 - odd), (rb_ref, odd)):
        for x in range(2):
            for z in range(4):
                row = (x * 4 + z) * 8
                leafx_ref[high * 10 + x, z] = ref[row : row + 8, :]
            for y in range(4):
                row = 64 + (x * 4 + y) * 2
                midx_ref[high * 6 + x, y] = ref[row : row + 2, :]
    ta, tb = ra_ref[80:84, :], rb_ref[80:84, :]
    topx_ref[...] = jnp.concatenate(
        [
            jnp.where(odd == 1, ta, tb),
            own_ref[288:292, :],
            jnp.where(odd == 1, tb, ta),
            jnp.zeros((4, 128), F32),
        ],
        axis=0,
    )
    odd_y = lax.axis_index("gy") % 2
    for x in range(12):
        for z in range(4):
            tile = leafx_ref[x, z]
            low, high = tile[0:2], tile[6:8]
            row = (x * 4 + z) * 2
            ya_ref[row : row + 2, :] = jnp.where(odd_y == 1, low, high)
            yb_ref[row : row + 2, :] = jnp.where(odd_y == 1, high, low)
    for ref, side in ((ya_ref, 1 - odd_y), (yb_ref, odd_y)):
        for x in range(8):
            for y in range(2):
                row = 96 + (x * 2 + y) * 2
                ref[row : row + 2, :] = midx_ref[x, side * 2 + y]
        ref[128:144, :] = topx_ref[...]


def glue_x(ra, rb, own, front, scale):
    return pl.pallas_call(
        glue_x_kernel,
        in_specs=[VMEM] * 3 + [pl.BlockSpec(memory_space=pl.ANY)] * 2,
        out_specs=[VMEM] * 5,
        out_shape=[
            jax.ShapeDtypeStruct((12, 4, 8, 128), F32),
            jax.ShapeDtypeStruct((8, 4, 2, 128), F32),
            jax.ShapeDtypeStruct((16, 128), F32),
            jax.ShapeDtypeStruct((144, 128), F32),
            jax.ShapeDtypeStruct((144, 128), F32),
        ],
        compiler_params=pltpu.CompilerParams(vmem_limit_bytes=8 << 20),
        name="glue_x",
    )(ra, rb, own, front, scale)


def glue_y_kernel(ra_ref, rb_ref, leafx_ref, midx_ref, topx_ref, _, leafxy_ref, midxy_ref, topxy_ref, za_ref, zb_ref):
    odd = lax.axis_index("gy") % 2
    for x in range(12):
        for z in range(4):
            row = (x * 4 + z) * 2
            a, b = ra_ref[row : row + 2, :], rb_ref[row : row + 2, :]
            leafxy_ref[x, z, 0:2, :] = jnp.where(odd == 1, a, b)
            leafxy_ref[x, z, 2:10, :] = leafx_ref[x, z]
            leafxy_ref[x, z, 10:12, :] = jnp.where(odd == 1, b, a)
    for x in range(8):
        midxy_ref[x, 2:6] = midx_ref[x]
        for ref, high in ((ra_ref, 1 - odd), (rb_ref, odd)):
            for y in range(2):
                row = 96 + (x * 2 + y) * 2
                midxy_ref[x, high * 6 + y] = ref[row : row + 2, :]
    for x in range(6):
        row = 128 + x * 2
        a, b = ra_ref[row : row + 2, :], rb_ref[row : row + 2, :]
        topxy_ref[x * 6 : x * 6 + 2, :] = jnp.where(odd == 1, a, b)
        topxy_ref[x * 6 + 2 : x * 6 + 4, :] = topx_ref[x * 2 : x * 2 + 2, :]
        topxy_ref[x * 6 + 4 : x * 6 + 6, :] = jnp.where(odd == 1, b, a)
    topxy_ref[36:40, :] = jnp.zeros((4, 128), F32)
    odd_z = lax.axis_index("gz") % 2
    for ref, side in ((za_ref, 1 - odd_z), (zb_ref, odd_z)):
        for x in range(12):
            for z in range(2):
                row = (x * 2 + z) * 12
                ref[row : row + 12, :] = leafxy_ref[x, side * 2 + z]
        for x in range(8):
            for y in range(8):
                row = 288 + (x * 8 + y) * 2
                ref[row : row + 2, :] = midxy_ref[x, y]
    za_ref[416:456, :] = topxy_ref[...]


def glue_y(ra, rb, leafx, midx, topx, back):
    return pl.pallas_call(
        glue_y_kernel,
        in_specs=[VMEM] * 5 + [pl.BlockSpec(memory_space=pl.ANY)],
        out_specs=[VMEM] * 5,
        out_shape=[
            jax.ShapeDtypeStruct((12, 4, 12, 128), F32),
            jax.ShapeDtypeStruct((8, 8, 2, 128), F32),
            jax.ShapeDtypeStruct((40, 128), F32),
            jax.ShapeDtypeStruct((456, 128), F32),
            jax.ShapeDtypeStruct((416, 128), F32),
        ],
        compiler_params=pltpu.CompilerParams(vmem_limit_bytes=8 << 20),
        name="glue_y",
    )(ra, rb, leafx, midx, topx, back)


def glue_z_kernel(ra_ref, topxy_ref, pair_ref):
    odd = lax.axis_index("gz") % 2
    mine, other = topxy_ref[0:36, :], ra_ref[416:452, :]
    pair_ref[...] = jnp.concatenate(
        [jnp.where(odd == 1, other, mine), jnp.where(odd == 1, mine, other)], axis=0
    )


def glue_z(ra, topxy):
    return pl.pallas_call(
        glue_z_kernel,
        in_specs=[VMEM] * 2,
        out_specs=VMEM,
        out_shape=jax.ShapeDtypeStruct((72, 128), F32),
        compiler_params=pltpu.CompilerParams(vmem_limit_bytes=8 << 20),
        name="glue_z",
    )(ra, topxy)


def offset_tiles(out_ref, table, cz, masked):
    zero = jnp.zeros((2, 128), F32)
    keep_rows = lax.broadcasted_iota(jnp.int32, (8, 128), 0)
    near = (keep_rows >= 1 + cz) & (keep_rows <= 3 + cz)
    for xy in range(49):
        start = xy * 7 + 1 - cz
        tile = jnp.concatenate([table[start : start + 6, :], zero], axis=0)
        if masked and 2 <= xy // 7 <= 4 and 2 <= xy % 7 <= 4:
            tile = jnp.where(near, 0.0, tile)
        out_ref[xy] = tile


def tables_kernel(in_ref, out_ref, _, scale_ref, tin_ref, tout_ref, top_in_ref, top_out_ref):
    scale_ref[...] = in_ref[0]
    for x in range(2, 5):
        for y in range(2, 5):
            row = x * 49 + y * 7 + 2
            scale_ref[row : row + 3, :] = jnp.zeros((3, 128), F32)
    for cz in range(2):
        offset_tiles(tin_ref.at[cz], in_ref.at[1], cz, True)
        offset_tiles(tout_ref.at[cz], out_ref.at[1], cz, False)
    odd = lax.axis_index("gz") % 2
    lanes = lax.broadcasted_iota(jnp.int32, (8, 128), 0)
    near = (lanes >= 1 + odd) & (lanes <= 3 + odd)
    for xy in range(49):
        for ref, table, masked in ((top_in_ref, in_ref, True), (top_out_ref, out_ref, False)):
            rows = table[2, xy * 7 : xy * 7 + 7, :]
            tile = jnp.where(odd == 1, rows[0:6], rows[1:7])
            tile = jnp.concatenate([tile, jnp.zeros((2, 128), F32)], axis=0)
            if masked and 2 <= xy // 7 <= 4 and 2 <= xy % 7 <= 4:
                tile = jnp.where(near, 0.0, tile)
            ref[xy] = tile


def run_tables(in_scale, out_scale, after):
    return pl.pallas_call(
        tables_kernel,
        in_specs=[VMEM] * 2 + [pl.BlockSpec(memory_space=pl.ANY)],
        out_specs=[VMEM] * 5,
        out_shape=[
            jax.ShapeDtypeStruct((343, 128), F32),
            jax.ShapeDtypeStruct((2, 49, 8, 128), F32),
            jax.ShapeDtypeStruct((2, 49, 8, 128), F32),
            jax.ShapeDtypeStruct((49, 8, 128), F32),
            jax.ShapeDtypeStruct((49, 8, 128), F32),
        ],
        cost_estimate=pl.CostEstimate(flops=1 << 28, bytes_accessed=3 << 20, transcendentals=0),
        compiler_params=pltpu.CompilerParams(vmem_limit_bytes=8 << 20),
        name="tables",
    )(in_scale, out_scale, after)


def far_kernel(
    leafxy_ref, midxy_ref, ra_ref, rb_ref, scale_ref, tin_ref, tout_ref, out_ref, core_ref,
    far0_ref, far1_ref,
    leaf_ref, mid_ref, acc_ref, even_ref, odd_ref,
):
    odd = lax.axis_index("gz") % 2
    leaf_ref[:, 2:6] = leafxy_ref[...]
    for ref, high in ((ra_ref, 1 - odd), (rb_ref, odd)):
        for x in range(12):
            for z in range(2):
                row = (x * 2 + z) * 12
                leaf_ref[x, high * 6 + z] = ref[row : row + 12, :]
    for x in range(8):
        for y in range(8):
            row = 288 + (x * 8 + y) * 2
            a, b = ra_ref[row : row + 2, :], rb_ref[row : row + 2, :]
            mid_ref[x, y] = jnp.concatenate(
                [
                    jnp.where(odd == 1, a, b),
                    midxy_ref[x, y],
                    jnp.where(odd == 1, b, a),
                    jnp.zeros((2, 128), F32),
                ],
                axis=0,
            )
    far0_ref[...] = jnp.zeros((8, 32, 128), F32)
    core0 = core_ref[0]

    def row_of(qx, qy, qz, pair, cz):
        return (qx + 1 - pair // 2) * 49 + (qy + 1 - pair % 2) * 7 + qz + 1 - cz

    def build_leaf(step, operand_ref):
        qx, qz = step // 6, step % 6
        for qy in range(6):
            tiles = []
            for x in range(4):
                for z in range(2):
                    tiles.append(leaf_ref[2 * x + qx, 2 * z + qz, pl.ds(qy, 4, stride=2), :])
            source = jnp.concatenate(tiles, axis=0)
            for pair in range(4):
                for cz in range(2):
                    start = ((pair * 2 + cz) * 6 + qy) * 32
                    row = row_of(qx, qy, qz, pair, cz)
                    scale = jnp.broadcast_to(scale_ref[pl.ds(row, 1), :], (32, 128))
                    operand_ref[start : start + 32, :] = (source * scale).astype(BF16)

    def apply_leaf(step, image):
        qx, qz = step // 6, step % 6
        for pair in range(4):
            for cz in range(2):
                total = far0_ref[pair * 2 + cz]
                for qy in range(6):
                    row = row_of(qx, qy, qz, pair, cz)
                    scale = jnp.broadcast_to(out_ref[0, pl.ds(row, 1), :], (32, 128))
                    start = ((pair * 2 + cz) * 6 + qy) * 32
                    total = total + scale * image[start : start + 32]
                far0_ref[pair * 2 + cz] = total

    build_leaf(0, even_ref)

    @pl.loop(0, 18)
    def _(turn):
        image = dot(even_ref[...], core0)
        build_leaf(2 * turn + 1, odd_ref)
        apply_leaf(2 * turn, image)
        image = dot(odd_ref[...], core0)
        build_leaf(jnp.minimum(2 * turn + 2, 35), even_ref)
        apply_leaf(2 * turn + 1, image)

    acc_ref[...] = jnp.zeros((8, 32, 128), F32)
    core1 = core_ref[1]

    def build_mid(qx, operand_ref):
        for qy in range(6):
            tiles = [mid_ref[2 * x + qx, 2 * y + qy] for x in range(2) for y in range(2)]
            for pair in range(4):
                xy = (qx + 1 - pair // 2) * 7 + qy + 1 - pair % 2
                for cz in range(2):
                    scale = tin_ref[cz, xy]
                    start = ((pair * 2 + cz) * 6 + qy) * 32
                    operand_ref[start : start + 32, :] = jnp.concatenate(
                        [tile * scale for tile in tiles], axis=0
                    ).astype(BF16)

    def apply_mid(qx, image):
        for pair in range(4):
            for cz in range(2):
                total = acc_ref[pair * 2 + cz]
                for qy in range(6):
                    scale = tout_ref[cz, (qx + 1 - pair // 2) * 7 + qy + 1 - pair % 2]
                    scale = jnp.concatenate([scale] * 4, axis=0)
                    start = ((pair * 2 + cz) * 6 + qy) * 32
                    total = total + scale * image[start : start + 32]
                acc_ref[pair * 2 + cz] = total

    build_mid(0, even_ref)

    @pl.loop(0, 3)
    def _(turn):
        image = dot(even_ref[...], core1)
        build_mid(2 * turn + 1, odd_ref)
        apply_mid(2 * turn, image)
        image = dot(odd_ref[...], core1)
        build_mid(jnp.minimum(2 * turn + 2, 5), even_ref)
        apply_mid(2 * turn + 1, image)

    for child in range(8):
        for parent in range(4):
            tile = acc_ref[child, parent * 8 : parent * 8 + 8, :]
            far1_ref[child * 4 + parent : child * 4 + parent + 1, :] = jnp.sum(
                tile, axis=0, keepdims=True
            )


def run_far(leafxy, midxy, ra, rb, scale, tin, tout, out_scale, transfer):
    return pl.pallas_call(
        far_kernel,
        in_specs=[VMEM] * 9,
        out_specs=[VMEM] * 2,
        out_shape=[
            jax.ShapeDtypeStruct((8, 32, 128), F32),
            jax.ShapeDtypeStruct((32, 128), F32),
        ],
        scratch_shapes=[
            pltpu.VMEM((12, 8, 12, 128), F32),
            pltpu.VMEM((8, 8, 8, 128), F32),
            pltpu.VMEM((8, 32, 128), F32),
            pltpu.VMEM((1536, 128), BF16),
            pltpu.VMEM((1536, 128), BF16),
        ],
        cost_estimate=pl.CostEstimate(flops=4 << 30, bytes_accessed=4 << 20, transcendentals=0),
        compiler_params=pltpu.CompilerParams(vmem_limit_bytes=24 << 20),
        name="far",
    )(leafxy, midxy, ra, rb, scale, tin, tout, out_scale, transfer)


def force_kernel(
    far0_ref, far1_ref, pair_ref, near_ref, next_ref, tin_ref, tout_ref, core_ref, down_ref,
    charge_ref, front_ref, back_ref, pos_ref, wave_ref,
    forces_ref, share_ref,
    window_ref, operand_ref, mid_ref, local_ref,
):
    odd = lax.axis_index("gz") % 2
    for xy in range(36):
        rows = [
            (ref[xy : xy + 1, :], ref[36 + xy : 37 + xy, :]) for ref in (near_ref, next_ref)
        ]
        low = [jnp.where(odd == 1, rows[1][z], rows[0][z]) for z in range(2)]
        high = [jnp.where(odd == 1, rows[0][z], rows[1][z]) for z in range(2)]
        window_ref[xy] = jnp.concatenate(
            low
            + [pair_ref[xy : xy + 1, :], pair_ref[36 + xy : 37 + xy, :]]
            + high
            + [jnp.zeros((2, 128), F32)],
            axis=0,
        )
    for qx in range(6):
        for qy in range(6):
            source = window_ref[qx * 6 + qy]
            tiles = []
            for pair in range(4):
                cx, cy = pair // 2, pair % 2
                tiles.append(source * tin_ref[(qx + 1 - cx) * 7 + qy + 1 - cy])
            start = (qx * 6 + qy) * 32
            operand_ref[start : start + 32, :] = jnp.concatenate(tiles, axis=0).astype(BF16)
    totals = [jnp.zeros((8, 128), F32) for _ in range(4)]
    for qx in range(6):
        image = dot(operand_ref[qx * 192 : qx * 192 + 192, :], core_ref[2])
        for qy in range(6):
            for pair in range(4):
                cx, cy = pair // 2, pair % 2
                scale = tout_ref[(qx + 1 - cx) * 7 + qy + 1 - cy]
                start = qy * 32 + pair * 8
                totals[pair] = totals[pair] + scale * image[start : start + 8]
    local_top = jnp.concatenate(
        [jnp.sum(total, axis=0, keepdims=True) for total in totals] + [jnp.zeros((4, 128), F32)],
        axis=0,
    ).astype(BF16)
    for child in range(8):
        cx, cy, cz = child // 4, child // 2 % 2, child % 2
        rows = far1_ref[child * 4 : child * 4 + 4, :] + dot(local_top, down_ref[1, child])[0:4]
        for parent in range(4):
            row = ((2 * (parent // 2) + cx) * 2 + cz) * 4 + 2 * (parent % 2) + cy
            mid_ref[row : row + 1, :] = rows[parent : parent + 1]
    local_mid = mid_ref[...].astype(BF16)
    for child in range(8):
        cx, cy, cz = child // 4, child // 2 % 2, child % 2
        rows = far0_ref[child] + dot(local_mid, down_ref[0, child])
        for x in range(4):
            for z in range(2):
                start = (x * 2 + z) * 4
                local_ref[2 * x + cx, 2 * z + cz, pl.ds(cy, 4, stride=2), :] = rows[start : start + 4]

    lane_box = lax.broadcasted_iota(jnp.int32, (8, 128), 1) // 32
    row_y = lax.broadcasted_iota(jnp.int32, (8, 128), 0)
    base_x = lax.axis_index("gx") * 8
    base_y = lax.axis_index("gy") * 8
    base_z = lax.axis_index("gz") * 4
    place_y0 = (base_y + row_y).astype(F32)
    place_z0 = (base_z + lane_box).astype(F32)

    def one_plane(x, sums, sines):
        local = local_ref[x].reshape(32, 128)
        weights = jnp.concatenate([local * wave_ref[d : d + 1, :] for d in range(3)], axis=0)
        high = weights.astype(BF16)
        low = (weights - high.astype(F32)).astype(BF16)
        product = dot(
            jnp.concatenate([high, low], axis=1), jnp.concatenate([sines, sines], axis=0)
        )
        charge = charge_ref[x]
        found = []
        for d in range(3):
            picked = jnp.zeros((8, 128), F32)
            for z in range(4):
                start = (d * 4 + z) * 8
                for y in range(8):
                    picked = jnp.where(
                        (row_y == y) & (lane_box == z),
                        product[start : start + 8, y * 128 : y * 128 + 128],
                        picked,
                    )
            picked = picked * charge
            forces_ref[d, x] = picked
            found.append(picked)
        places = (
            ((base_x + x).astype(F32) + pos_ref[0, x]) * (1.0 / 32),
            (place_y0 + pos_ref[1, x]) * (1.0 / 64),
            (place_z0 + pos_ref[2, x]) * (1.0 / 64),
        )
        return tuple(
            sums[d * 3 + e] + places[d] * found[e] for d in range(3) for e in range(3)
        )

    sums = (jnp.zeros((8, 128), F32),) * 9
    sums = lax.fori_loop(0, 4, lambda x, sums: one_plane(x, sums, front_ref[x]), sums)
    sums = lax.fori_loop(0, 4, lambda x, sums: one_plane(x + 4, sums, back_ref[x]), sums)
    lane = lax.broadcasted_iota(jnp.int32, (8, 128), 1)
    row = jnp.zeros((8, 128), F32)
    for i in range(9):
        row = jnp.where(lane == i, jnp.sum(sums[i]), row)
    share_ref[...] = jnp.broadcast_to(row[0:1], (512, 128))


def run_forces(far0, far1, pair, near, following, top_in, top_out, transfer, downward, charge, front, back, positions, wave):
    return pl.pallas_call(
        force_kernel,
        in_specs=[VMEM] * 14,
        out_specs=[VMEM] * 2,
        out_shape=[
            jax.ShapeDtypeStruct((3, 8, 8, 128), F32),
            jax.ShapeDtypeStruct((512, 128), F32),
        ],
        scratch_shapes=[
            pltpu.VMEM((36, 8, 128), F32),
            pltpu.VMEM((1152, 128), BF16),
            pltpu.VMEM((32, 128), F32),
            pltpu.VMEM((8, 4, 8, 128), F32),
        ],
        compiler_params=pltpu.CompilerParams(vmem_limit_bytes=24 << 20),
        name="forces",
    )(far0, far1, pair, near, following, top_in, top_out, transfer, downward, charge, front, back, positions, wave)


def virial_kernel(scale, rows_ref, virial_ref):
    row = jnp.sum(rows_ref[...], axis=0, keepdims=True) * scale
    for d in range(3):
        virial_ref[d : d + 1, :] = row[:, d * 3 : d * 3 + 3]


def run_virial(rows, scale):
    return pl.pallas_call(
        lambda rows_ref, virial_ref: virial_kernel(scale, rows_ref, virial_ref),
        in_specs=[VMEM],
        out_specs=VMEM,
        out_shape=jax.ShapeDtypeStruct((3, 3), F32),
        compiler_params=pltpu.CompilerParams(vmem_limit_bytes=8 << 20),
        name="virial",
    )(rows)


def swapped(value, axis, kind):
    count = lax.axis_size(axis)
    pairs = []
    for i in range(count):
        hop = (1, -1, 3)[kind]
        pairs.append((i, (i + hop) % count if i % 2 == 0 else (i - hop) % count))
    return lax.ppermute(value, axis, pairs)


def shards(
    features, positions, box_counts, w_hidden, w_charge, wave_numbers, phases,
    upward, downward, transfer, out_scale, in_scale,
):
    phases = phases.reshape(1, 128)
    charge, own, xb = run_atoms(
        features, positions, box_counts.transpose(0, 2, 1), w_hidden, w_charge.reshape(1, 128),
        wave_numbers, phases, upward,
    )
    rb = swapped(xb, "gx", 1)
    front, xa = run_front(positions, wave_numbers, phases, own, 4)
    scale, tin, tout, top_in, top_out = run_tables(in_scale, out_scale, own)
    ra = swapped(xa, "gx", 0)
    leaf, mid, top, ya, yb = glue_x(ra, rb, own, front, scale)
    back = run_sines(positions, wave_numbers, phases, top, 4, 4)
    ra, rb = swapped(ya, "gy", 0), swapped(yb, "gy", 1)
    leaf, mid, top, za, zb = glue_y(ra, rb, leaf, mid, top, back)
    ra, rb = swapped(za, "gz", 0), swapped(zb, "gz", 1)
    pair = glue_z(ra, top)
    near, following = swapped(pair, "gz", 1), swapped(pair, "gz", 2)
    far0, far1 = run_far(leaf, mid, ra, rb, scale, tin, tout, out_scale, transfer)
    forces, share = run_forces(
        far0, far1, pair, near, following, top_in, top_out, transfer, downward, charge, front, back,
        positions, wave_numbers,
    )
    rows = lax.all_to_all(share, ("gx", "gy", "gz"), 0, 0, tiled=True)
    return forces, run_virial(rows, 1.0 / math.sqrt(4194304))


def solution(mesh):
    in_specs = (
        P("gx", "gy", "gz", None),
        P(None, "gx", "gy", "gz"),
        P("gx", "gy", "gz"),
    ) + (P(),) * 9
    out_specs = (P(None, "gx", "gy", "gz"), P())
    return jax.shard_map(shards, mesh=mesh, in_specs=in_specs, out_specs=out_specs, check_vma=False)
```

```python
import functools
import math

import jax
import jax.numpy as jnp
import numpy as np
from jax import lax
from jax.experimental import pallas as pl
from jax.experimental.pallas import tpu as pltpu
from jax.sharding import PartitionSpec as P

F32 = jnp.float32
BF16 = jnp.bfloat16
TURN = 1.0 / (2.0 * math.pi)
SIN_HALF = (4.4428679, -7.30744342, 3.59478808, -0.78437403)
COS_HALF = (1.4142135, -6.97885099, 5.73946117, -1.88356299, 0.31069819)
NT = (((1,), (1,)), ((), ()))
VMEM = pl.BlockSpec(memory_space=pltpu.VMEM)


def dot(a, b):
    return jnp.dot(a, b, preferred_element_type=F32)


def split(value):
    high = value.astype(BF16).astype(F32)
    rest = value - high
    middle = rest.astype(BF16).astype(F32)
    return high, middle, rest - middle


def wave_table(wave_ref, ph_ref, table_ref):
    blocks = []
    for d in range(3):
        high, middle, low = split(wave_ref[d : d + 1, :] * TURN)
        for part in (high, middle, low, high, middle, high):
            blocks.append(jnp.broadcast_to(part, (8, 128)))
    blocks += list(split(ph_ref[...] * TURN)) + [jnp.zeros((109, 128), F32)]
    table_ref[...] = jnp.concatenate(blocks, axis=0).T.astype(BF16)


def turns_of(step, pos_ref, table_ref):
    row_y = lax.broadcasted_iota(jnp.int32, (8, 128), 0)
    blocks = []
    for d in range(3):
        spread = []
        for part in split(pos_ref[d, step] - 0.5):
            spread.append(
                jnp.concatenate([jnp.where(row_y == y, part, 0.0) for y in range(8)], axis=1)
            )
        blocks += [spread[0]] * 3 + [spread[1]] * 2 + [spread[2]]
    blocks += [jnp.ones((8, 1024), F32), jnp.zeros((8, 1024), F32)]
    return dot(table_ref[:, 0:160], jnp.concatenate(blocks, axis=0).astype(BF16))


def poly(coefs, u):
    value = coefs[-1]
    for coef in coefs[-2::-1]:
        value = value * u + coef
    return value


def sines_kernel(start, pos_ref, wave_ref, ph_ref, _, sin_ref, table_ref):
    wave_table(wave_ref, ph_ref, table_ref)

    @pl.loop(0, sin_ref.shape[0])
    def _(x):
        turns = turns_of(start + x, pos_ref, table_ref)
        for y in range(8):
            t = turns[:, y * 128 : (y + 1) * 128]
            r = t - jnp.round(t)
            u = r * r
            sin_ref[x, :, y * 128 : (y + 1) * 128] = (
                poly(SIN_HALF, u) * r * poly(COS_HALF, u)
            ).astype(BF16)


def front_kernel(pos_ref, wave_ref, ph_ref, own_ref, sin_ref, send_ref, table_ref):
    side = 1 - lax.axis_index("gx") % 2
    send_ref[0:64, :] = own_ref[pl.ds(pl.multiple_of(side * 192, 8), 64), :]
    send_ref[64:80, :] = own_ref[pl.ds(pl.multiple_of(256 + side * 16, 8), 16), :]
    send_ref[80:88, :] = own_ref[288:296, :]
    sines_kernel(0, pos_ref, wave_ref, ph_ref, None, sin_ref, table_ref)


def run_front(positions, wave, phases, own, planes):
    return pl.pallas_call(
        front_kernel,
        in_specs=[VMEM] * 4,
        out_specs=[VMEM] * 2,
        out_shape=[
            jax.ShapeDtypeStruct((planes, 128, 1024), BF16),
            jax.ShapeDtypeStruct((88, 128), F32),
        ],
        scratch_shapes=[pltpu.VMEM((128, 256), BF16)],
        cost_estimate=pl.CostEstimate(flops=1 << 30, bytes_accessed=6 << 20, transcendentals=0),
        compiler_params=pltpu.CompilerParams(vmem_limit_bytes=16 << 20),
        name="front",
    )(positions, wave, phases, own)


def run_sines(positions, wave, phases, after, start, planes):
    return pl.pallas_call(
        functools.partial(sines_kernel, start),
        in_specs=[VMEM] * 4,
        out_specs=VMEM,
        out_shape=jax.ShapeDtypeStruct((planes, 128, 1024), BF16),
        scratch_shapes=[pltpu.VMEM((128, 256), BF16)],
        cost_estimate=pl.CostEstimate(flops=1 << 30, bytes_accessed=6 << 20, transcendentals=0),
        compiler_params=pltpu.CompilerParams(vmem_limit_bytes=16 << 20),
        name="sines",
    )(positions, wave, phases, after)


def atoms_kernel(
    feat_hbm, pos_hbm, cnt_hbm, wh_hbm, wc_hbm, wave_hbm, ph_hbm, up_hbm,
    charge_ref, own_ref, sb_ref,
    feat_ref, pos_ref, cnt_ref, wh_ref, wc_ref, wave_ref, ph_ref, up_ref, parts_ref, leaf_ref, mid_ref,
    plane_sems, sems,
):
    def plane(x):
        return pltpu.make_async_copy(feat_hbm.at[x], feat_ref.at[x], plane_sems.at[x])

    others = [
        pltpu.make_async_copy(source, target, sems.at[i])
        for i, (source, target) in enumerate(
            (
                (wave_hbm, wave_ref),
                (ph_hbm, ph_ref),
                (wc_hbm, wc_ref),
                (pos_hbm, pos_ref),
                (wh_hbm, wh_ref),
                (cnt_hbm, cnt_ref),
                (up_hbm, up_ref),
            )
        )
    ]
    for copy in others[:3]:
        copy.start()
    plane(0).start()
    for copy in others[3:6]:
        copy.start()
    for x in range(1, 8):
        plane(x).start()
    others[6].start()
    for copy in others[:3]:
        copy.wait()
    rows = []
    for d in range(3):
        high, middle, low = split(wave_ref[d : d + 1, :] * TURN)
        rows += [high, middle, low, high, middle, high]
    rows += list(split(ph_ref[...] * TURN)) + [jnp.zeros((11, 128), F32)]
    table = jnp.concatenate(rows, axis=0).astype(BF16)
    for row in range(18, 32):
        parts_ref[row * 8 : row * 8 + 8, :] = jnp.full((8, 128), 1.0 if row < 21 else 0.0, F32)
    column = jnp.broadcast_to(wc_ref[...].astype(F32), (128, 128)).T.astype(BF16)
    for copy in others[3:6]:
        copy.wait()

    @pl.loop(0, 8)
    def _(x):
        plane(x).wait()
        atoms_plane(
            x, feat_ref, pos_ref, cnt_ref, wh_ref, wc_ref, charge_ref, leaf_ref, table, column,
            parts_ref,
        )

    others[6].wait()
    atoms_lift(leaf_ref, up_ref, mid_ref, own_ref, sb_ref)


def atoms_plane(
    step, feat_ref, pos_ref, cnt_ref, wh_ref, wc_ref, charge_ref, leaf_ref, table, column,
    parts_ref,
):
    lane_box = lax.broadcasted_iota(jnp.int32, (8, 128), 1) // 32
    lane_slot = lax.broadcasted_iota(jnp.int32, (8, 128), 1) % 32
    row_y = lax.broadcasted_iota(jnp.int32, (8, 128), 0)
    slot = lax.broadcasted_iota(jnp.int32, (32, 128), 0)
    for d in range(3):
        high, middle, low = split(pos_ref[d, step] - 0.5)
        for i, part in enumerate((high, high, high, middle, middle, low)):
            row = (d * 6 + i) * 8
            parts_ref[row : row + 8, :] = part
    lines = [parts_ref[pl.ds(y, 32, stride=8), :].T.astype(BF16) for y in range(8)]
    turns = dot(jnp.concatenate(lines, axis=0), table)

    hidden = dot(feat_ref[step].reshape(1024, 128), wh_ref[...])
    half = hidden * 0.5
    hidden = (half + half * jnp.tanh(half)).astype(BF16)
    broad = dot(hidden, column)
    wc = jnp.broadcast_to(wc_ref[...], (8, 128))
    raw = lax.dot_general(wc, hidden, NT, preferred_element_type=F32)
    counts = jnp.zeros((8, 128), jnp.int32)
    charge = jnp.zeros((8, 128), F32)
    for y in range(8):
        charge = jnp.where(row_y == y, raw[:, y * 128 : (y + 1) * 128], charge)
        for z in range(4):
            count = cnt_ref[step, z, y]
            counts = jnp.where((row_y == y) & (lane_box == z), count, counts)
            start = y * 128 + z * 32
            t = turns[start : start + 32]
            r = t - jnp.round(t)
            s = poly(SIN_HALF, r * r) * r
            terms = jnp.where(slot < count, broad[start : start + 32], 0.0) * (1.0 - s * s)
            leaf_ref[step, z, y : y + 1, :] = jnp.sum(terms, axis=0, keepdims=True)
    charge_ref[step] = jnp.where(lane_slot < counts, charge, 0.0)


def atoms_lift(leaf_ref, up_ref, mid_ref, own_ref, sb_ref):
    total = jnp.zeros((32, 128), F32)
    for child in range(8):
        cx, cy, cz = child // 4, child // 2 % 2, child % 2
        rows = jnp.concatenate(
            [
                leaf_ref[2 * x + cx, 2 * z + cz, pl.ds(cy, 4, stride=2), :]
                for x in range(4)
                for z in range(2)
            ],
            axis=0,
        )
        total = total + dot(rows.astype(BF16), up_ref[0, child])
    for x in range(4):
        for z in range(2):
            for y in range(4):
                row = (x * 2 + z) * 4 + y
                mid_ref[x, y, z : z + 1, :] = total[row : row + 1]
    crown = jnp.zeros((8, 128), F32)
    for child in range(8):
        cx, cy, cz = child // 4, child // 2 % 2, child % 2
        rows = jnp.concatenate(
            [
                mid_ref[2 * x + cx, 2 * y + cy, cz : cz + 1, :]
                for x in range(2)
                for y in range(2)
            ]
            + [jnp.zeros((4, 128), F32)],
            axis=0,
        )
        crown = crown + dot(rows.astype(BF16), up_ref[1, child])
    own_ref[0:256, :] = leaf_ref[...].reshape(256, 128)
    for x in range(4):
        for y in range(4):
            row = 256 + (x * 4 + y) * 2
            own_ref[row : row + 2, :] = mid_ref[x, y]
    own_ref[288:296, :] = crown
    odd = lax.axis_index("gx") % 2
    for ref, high in ((sb_ref, odd),):
        for x in range(2):
            for z in range(4):
                row = (x * 4 + z) * 8
                ref[row : row + 8, :] = leaf_ref[high * 6 + x, z]
            for y in range(4):
                row = 64 + (x * 4 + y) * 2
                ref[row : row + 2, :] = mid_ref[high * 2 + x, y]
        ref[80:84, :] = crown[0:4]
        ref[84:88, :] = jnp.zeros((4, 128), F32)


def run_atoms(features, positions, box_counts, w_hidden, w_charge, wave, phases, upward):
    hbm = pl.BlockSpec(memory_space=pltpu.HBM)
    return pl.pallas_call(
        atoms_kernel,
        in_specs=[hbm] * 8,
        out_specs=[VMEM] * 3,
        out_shape=[
            jax.ShapeDtypeStruct((8, 8, 128), F32),
            jax.ShapeDtypeStruct((296, 128), F32),
            jax.ShapeDtypeStruct((88, 128), F32),
        ],
        scratch_shapes=[
            pltpu.VMEM((8, 8, 128, 128), BF16),
            pltpu.VMEM((3, 8, 8, 128), F32),
            pltpu.SMEM((8, 4, 8), jnp.int32),
            pltpu.VMEM((128, 128), BF16),
            pltpu.VMEM((1, 128), BF16),
            pltpu.VMEM((3, 128), F32),
            pltpu.VMEM((1, 128), F32),
            pltpu.VMEM((2, 8, 128, 128), BF16),
            pltpu.VMEM((256, 128), F32),
            pltpu.VMEM((8, 4, 8, 128), F32),
            pltpu.VMEM((4, 4, 2, 128), F32),
            pltpu.SemaphoreType.DMA((8,)),
            pltpu.SemaphoreType.DMA((7,)),
        ],
        compiler_params=pltpu.CompilerParams(vmem_limit_bytes=58 << 20),
        name="atoms",
    )(features, positions, box_counts, w_hidden, w_charge, wave, phases, upward)


def glue_x_kernel(ra_ref, rb_ref, own_ref, _, __, leafx_ref, midx_ref, topx_ref, ya_ref, yb_ref):
    odd = lax.axis_index("gx") % 2
    leafx_ref[2:10] = own_ref[0:256, :].reshape(8, 4, 8, 128)
    for x in range(4):
        for y in range(4):
            row = 256 + (x * 4 + y) * 2
            midx_ref[2 + x, y] = own_ref[row : row + 2, :]
    for ref, high in ((ra_ref, 1 - odd), (rb_ref, odd)):
        for x in range(2):
            for z in range(4):
                row = (x * 4 + z) * 8
                leafx_ref[high * 10 + x, z] = ref[row : row + 8, :]
            for y in range(4):
                row = 64 + (x * 4 + y) * 2
                midx_ref[high * 6 + x, y] = ref[row : row + 2, :]
    ta, tb = ra_ref[80:84, :], rb_ref[80:84, :]
    topx_ref[...] = jnp.concatenate(
        [
            jnp.where(odd == 1, ta, tb),
            own_ref[288:292, :],
            jnp.where(odd == 1, tb, ta),
            jnp.zeros((4, 128), F32),
        ],
        axis=0,
    )
    odd_y = lax.axis_index("gy") % 2
    for x in range(12):
        for z in range(4):
            tile = leafx_ref[x, z]
            low, high = tile[0:2], tile[6:8]
            row = (x * 4 + z) * 2
            ya_ref[row : row + 2, :] = jnp.where(odd_y == 1, low, high)
            yb_ref[row : row + 2, :] = jnp.where(odd_y == 1, high, low)
    for ref, side in ((ya_ref, 1 - odd_y), (yb_ref, odd_y)):
        for x in range(8):
            for y in range(2):
                row = 96 + (x * 2 + y) * 2
                ref[row : row + 2, :] = midx_ref[x, side * 2 + y]
        ref[128:144, :] = topx_ref[...]


def glue_x(ra, rb, own, front, scale):
    return pl.pallas_call(
        glue_x_kernel,
        in_specs=[VMEM] * 3 + [pl.BlockSpec(memory_space=pl.ANY)] * 2,
        out_specs=[VMEM] * 5,
        out_shape=[
            jax.ShapeDtypeStruct((12, 4, 8, 128), F32),
            jax.ShapeDtypeStruct((8, 4, 2, 128), F32),
            jax.ShapeDtypeStruct((16, 128), F32),
            jax.ShapeDtypeStruct((144, 128), F32),
            jax.ShapeDtypeStruct((144, 128), F32),
        ],
        compiler_params=pltpu.CompilerParams(vmem_limit_bytes=8 << 20),
        name="glue_x",
    )(ra, rb, own, front, scale)


def glue_y_kernel(ra_ref, rb_ref, leafx_ref, midx_ref, topx_ref, _, leafxy_ref, midxy_ref, topxy_ref, za_ref, zb_ref):
    odd = lax.axis_index("gy") % 2
    for x in range(12):
        for z in range(4):
            row = (x * 4 + z) * 2
            a, b = ra_ref[row : row + 2, :], rb_ref[row : row + 2, :]
            leafxy_ref[x, z, 0:2, :] = jnp.where(odd == 1, a, b)
            leafxy_ref[x, z, 2:10, :] = leafx_ref[x, z]
            leafxy_ref[x, z, 10:12, :] = jnp.where(odd == 1, b, a)
    for x in range(8):
        midxy_ref[x, 2:6] = midx_ref[x]
        for ref, high in ((ra_ref, 1 - odd), (rb_ref, odd)):
            for y in range(2):
                row = 96 + (x * 2 + y) * 2
                midxy_ref[x, high * 6 + y] = ref[row : row + 2, :]
    for x in range(6):
        row = 128 + x * 2
        a, b = ra_ref[row : row + 2, :], rb_ref[row : row + 2, :]
        topxy_ref[x * 6 : x * 6 + 2, :] = jnp.where(odd == 1, a, b)
        topxy_ref[x * 6 + 2 : x * 6 + 4, :] = topx_ref[x * 2 : x * 2 + 2, :]
        topxy_ref[x * 6 + 4 : x * 6 + 6, :] = jnp.where(odd == 1, b, a)
    topxy_ref[36:40, :] = jnp.zeros((4, 128), F32)
    odd_z = lax.axis_index("gz") % 2
    for ref, side in ((za_ref, 1 - odd_z), (zb_ref, odd_z)):
        for x in range(12):
            for z in range(2):
                row = (x * 2 + z) * 12
                ref[row : row + 12, :] = leafxy_ref[x, side * 2 + z]
        for x in range(8):
            for y in range(8):
                row = 288 + (x * 8 + y) * 2
                ref[row : row + 2, :] = midxy_ref[x, y]
    za_ref[416:456, :] = topxy_ref[...]
    zb_ref[416:456, :] = topxy_ref[...]


def glue_y(ra, rb, leafx, midx, topx, back):
    return pl.pallas_call(
        glue_y_kernel,
        in_specs=[VMEM] * 5 + [pl.BlockSpec(memory_space=pl.ANY)],
        out_specs=[VMEM] * 5,
        out_shape=[
            jax.ShapeDtypeStruct((12, 4, 12, 128), F32),
            jax.ShapeDtypeStruct((8, 8, 2, 128), F32),
            jax.ShapeDtypeStruct((40, 128), F32),
            jax.ShapeDtypeStruct((456, 128), F32),
            jax.ShapeDtypeStruct((456, 128), F32),
        ],
        compiler_params=pltpu.CompilerParams(vmem_limit_bytes=8 << 20),
        name="glue_y",
    )(ra, rb, leafx, midx, topx, back)


def glue_z_kernel(ra_ref, topxy_ref, pair_ref):
    odd = lax.axis_index("gz") % 2
    mine, other = topxy_ref[0:36, :], ra_ref[416:452, :]
    pair_ref[...] = jnp.concatenate(
        [jnp.where(odd == 1, other, mine), jnp.where(odd == 1, mine, other)], axis=0
    )


def glue_z(ra, topxy):
    return pl.pallas_call(
        glue_z_kernel,
        in_specs=[VMEM] * 2,
        out_specs=VMEM,
        out_shape=jax.ShapeDtypeStruct((72, 128), F32),
        compiler_params=pltpu.CompilerParams(vmem_limit_bytes=8 << 20),
        name="glue_z",
    )(ra, topxy)


def offset_tiles(out_ref, table, cz, masked):
    zero = jnp.zeros((2, 128), F32)
    keep_rows = lax.broadcasted_iota(jnp.int32, (8, 128), 0)
    near = (keep_rows >= 1 + cz) & (keep_rows <= 3 + cz)
    for xy in range(49):
        start = xy * 7 + 1 - cz
        tile = jnp.concatenate([table[start : start + 6, :], zero], axis=0)
        if masked and 2 <= xy // 7 <= 4 and 2 <= xy % 7 <= 4:
            tile = jnp.where(near, 0.0, tile)
        out_ref[xy] = tile


def tables_kernel(in_ref, out_ref, _, scale_ref, tin_ref, tout_ref, top_in_ref, top_out_ref):
    scale_ref[...] = in_ref[0]
    for x in range(2, 5):
        for y in range(2, 5):
            row = x * 49 + y * 7 + 2
            scale_ref[row : row + 3, :] = jnp.zeros((3, 128), F32)
    for cz in range(2):
        offset_tiles(tin_ref.at[cz], in_ref.at[1], cz, True)
        offset_tiles(tout_ref.at[cz], out_ref.at[1], cz, False)
    odd = lax.axis_index("gz") % 2
    lanes = lax.broadcasted_iota(jnp.int32, (8, 128), 0)
    near = (lanes >= 1 + odd) & (lanes <= 3 + odd)
    for xy in range(49):
        for ref, table, masked in ((top_in_ref, in_ref, True), (top_out_ref, out_ref, False)):
            rows = table[2, xy * 7 : xy * 7 + 7, :]
            tile = jnp.where(odd == 1, rows[0:6], rows[1:7])
            tile = jnp.concatenate([tile, jnp.zeros((2, 128), F32)], axis=0)
            if masked and 2 <= xy // 7 <= 4 and 2 <= xy % 7 <= 4:
                tile = jnp.where(near, 0.0, tile)
            ref[xy] = tile


def run_tables(in_scale, out_scale, after):
    return pl.pallas_call(
        tables_kernel,
        in_specs=[VMEM] * 2 + [pl.BlockSpec(memory_space=pl.ANY)],
        out_specs=[VMEM] * 5,
        out_shape=[
            jax.ShapeDtypeStruct((343, 128), F32),
            jax.ShapeDtypeStruct((2, 49, 8, 128), F32),
            jax.ShapeDtypeStruct((2, 49, 8, 128), F32),
            jax.ShapeDtypeStruct((49, 8, 128), F32),
            jax.ShapeDtypeStruct((49, 8, 128), F32),
        ],
        cost_estimate=pl.CostEstimate(flops=1 << 28, bytes_accessed=3 << 20, transcendentals=0),
        compiler_params=pltpu.CompilerParams(vmem_limit_bytes=8 << 20),
        name="tables",
    )(in_scale, out_scale, after)


def far_kernel(
    leafxy_ref, midxy_ref, ra_ref, rb_ref, scale_ref, tin_ref, tout_ref, out_ref, core_ref,
    far0_ref, far1_ref,
    leaf_ref, mid_ref, acc_ref, even_ref, odd_ref,
):
    odd = lax.axis_index("gz") % 2
    leaf_ref[:, 2:6] = leafxy_ref[...]
    for ref, high in ((ra_ref, 1 - odd), (rb_ref, odd)):
        for x in range(12):
            for z in range(2):
                row = (x * 2 + z) * 12
                leaf_ref[x, high * 6 + z] = ref[row : row + 12, :]
    for x in range(8):
        for y in range(8):
            row = 288 + (x * 8 + y) * 2
            a, b = ra_ref[row : row + 2, :], rb_ref[row : row + 2, :]
            mid_ref[x, y] = jnp.concatenate(
                [
                    jnp.where(odd == 1, a, b),
                    midxy_ref[x, y],
                    jnp.where(odd == 1, b, a),
                    jnp.zeros((2, 128), F32),
                ],
                axis=0,
            )
    far0_ref[...] = jnp.zeros((8, 32, 128), F32)
    core0 = core_ref[0]

    def row_of(qx, qy, qz, pair, cz):
        return (qx + 1 - pair // 2) * 49 + (qy + 1 - pair % 2) * 7 + qz + 1 - cz

    def build_leaf(step, operand_ref):
        qx, qz = step // 6, step % 6
        for qy in range(6):
            tiles = []
            for x in range(4):
                for z in range(2):
                    tiles.append(leaf_ref[2 * x + qx, 2 * z + qz, pl.ds(qy, 4, stride=2), :])
            source = jnp.concatenate(tiles, axis=0)
            for pair in range(4):
                for cz in range(2):
                    start = ((pair * 2 + cz) * 6 + qy) * 32
                    row = row_of(qx, qy, qz, pair, cz)
                    scale = jnp.broadcast_to(scale_ref[pl.ds(row, 1), :], (32, 128))
                    operand_ref[start : start + 32, :] = (source * scale).astype(BF16)

    def apply_leaf(step, image):
        qx, qz = step // 6, step % 6
        for pair in range(4):
            for cz in range(2):
                total = far0_ref[pair * 2 + cz]
                for qy in range(6):
                    row = row_of(qx, qy, qz, pair, cz)
                    scale = jnp.broadcast_to(out_ref[0, pl.ds(row, 1), :], (32, 128))
                    start = ((pair * 2 + cz) * 6 + qy) * 32
                    total = total + scale * image[start : start + 32]
                far0_ref[pair * 2 + cz] = total

    build_leaf(0, even_ref)

    @pl.loop(0, 18)
    def _(turn):
        image = dot(even_ref[...], core0)
        build_leaf(2 * turn + 1, odd_ref)
        apply_leaf(2 * turn, image)
        image = dot(odd_ref[...], core0)
        build_leaf(jnp.minimum(2 * turn + 2, 35), even_ref)
        apply_leaf(2 * turn + 1, image)

    acc_ref[...] = jnp.zeros((8, 32, 128), F32)
    core1 = core_ref[1]

    def build_mid(qx, operand_ref):
        for qy in range(6):
            tiles = [mid_ref[2 * x + qx, 2 * y + qy] for x in range(2) for y in range(2)]
            for pair in range(4):
                xy = (qx + 1 - pair // 2) * 7 + qy + 1 - pair % 2
                for cz in range(2):
                    scale = tin_ref[cz, xy]
                    start = ((pair * 2 + cz) * 6 + qy) * 32
                    operand_ref[start : start + 32, :] = jnp.concatenate(
                        [tile * scale for tile in tiles], axis=0
                    ).astype(BF16)

    def apply_mid(qx, image):
        for pair in range(4):
            for cz in range(2):
                total = acc_ref[pair * 2 + cz]
                for qy in range(6):
                    scale = tout_ref[cz, (qx + 1 - pair // 2) * 7 + qy + 1 - pair % 2]
                    scale = jnp.concatenate([scale] * 4, axis=0)
                    start = ((pair * 2 + cz) * 6 + qy) * 32
                    total = total + scale * image[start : start + 32]
                acc_ref[pair * 2 + cz] = total

    build_mid(0, even_ref)

    @pl.loop(0, 3)
    def _(turn):
        image = dot(even_ref[...], core1)
        build_mid(2 * turn + 1, odd_ref)
        apply_mid(2 * turn, image)
        image = dot(odd_ref[...], core1)
        build_mid(jnp.minimum(2 * turn + 2, 5), even_ref)
        apply_mid(2 * turn + 1, image)

    for child in range(8):
        for parent in range(4):
            tile = acc_ref[child, parent * 8 : parent * 8 + 8, :]
            far1_ref[child * 4 + parent : child * 4 + parent + 1, :] = jnp.sum(
                tile, axis=0, keepdims=True
            )


def run_far(leafxy, midxy, ra, rb, scale, tin, tout, out_scale, transfer):
    return pl.pallas_call(
        far_kernel,
        in_specs=[VMEM] * 9,
        out_specs=[VMEM] * 2,
        out_shape=[
            jax.ShapeDtypeStruct((8, 32, 128), F32),
            jax.ShapeDtypeStruct((32, 128), F32),
        ],
        scratch_shapes=[
            pltpu.VMEM((12, 8, 12, 128), F32),
            pltpu.VMEM((8, 8, 8, 128), F32),
            pltpu.VMEM((8, 32, 128), F32),
            pltpu.VMEM((1536, 128), BF16),
            pltpu.VMEM((1536, 128), BF16),
        ],
        cost_estimate=pl.CostEstimate(flops=4 << 30, bytes_accessed=4 << 20, transcendentals=0),
        compiler_params=pltpu.CompilerParams(vmem_limit_bytes=24 << 20),
        name="far",
    )(leafxy, midxy, ra, rb, scale, tin, tout, out_scale, transfer)


def force_kernel(
    far0_ref, far1_ref, pair_ref, side_ref, far_ref, next_ref, tin_ref, tout_ref, core_ref, down_ref,
    charge_ref, front_ref, back_ref, pos_ref, wave_ref,
    forces_ref, share_ref,
    window_ref, operand_ref, mid_ref, local_ref,
):
    odd = lax.axis_index("gz") % 2
    near, beyond = side_ref[416:452, :], far_ref[0:36, :]
    first, second = next_ref[0:36, :], next_ref[36:72, :]
    lines = [
        jnp.where(odd == 1, first, beyond),
        jnp.where(odd == 1, second, near),
        pair_ref[0:36, :],
        pair_ref[36:72, :],
        jnp.where(odd == 1, near, first),
        jnp.where(odd == 1, beyond, second),
    ]
    for xy in range(36):
        window_ref[xy] = jnp.concatenate(
            [line[xy : xy + 1] for line in lines] + [jnp.zeros((2, 128), F32)], axis=0
        )
    for qx in range(6):
        for qy in range(6):
            source = window_ref[qx * 6 + qy]
            tiles = []
            for pair in range(4):
                cx, cy = pair // 2, pair % 2
                tiles.append(source * tin_ref[(qx + 1 - cx) * 7 + qy + 1 - cy])
            start = (qx * 6 + qy) * 32
            operand_ref[start : start + 32, :] = jnp.concatenate(tiles, axis=0).astype(BF16)
    totals = [jnp.zeros((8, 128), F32) for _ in range(4)]
    for qx in range(6):
        image = dot(operand_ref[qx * 192 : qx * 192 + 192, :], core_ref[2])
        for qy in range(6):
            for pair in range(4):
                cx, cy = pair // 2, pair % 2
                scale = tout_ref[(qx + 1 - cx) * 7 + qy + 1 - cy]
                start = qy * 32 + pair * 8
                totals[pair] = totals[pair] + scale * image[start : start + 8]
    local_top = jnp.concatenate(
        [jnp.sum(total, axis=0, keepdims=True) for total in totals] + [jnp.zeros((4, 128), F32)],
        axis=0,
    ).astype(BF16)
    for child in range(8):
        cx, cy, cz = child // 4, child // 2 % 2, child % 2
        rows = far1_ref[child * 4 : child * 4 + 4, :] + dot(local_top, down_ref[1, child])[0:4]
        for parent in range(4):
            row = ((2 * (parent // 2) + cx) * 2 + cz) * 4 + 2 * (parent % 2) + cy
            mid_ref[row : row + 1, :] = rows[parent : parent + 1]
    local_mid = mid_ref[...].astype(BF16)
    for child in range(8):
        cx, cy, cz = child // 4, child // 2 % 2, child % 2
        rows = far0_ref[child] + dot(local_mid, down_ref[0, child])
        for x in range(4):
            for z in range(2):
                start = (x * 2 + z) * 4
                local_ref[2 * x + cx, 2 * z + cz, pl.ds(cy, 4, stride=2), :] = rows[start : start + 4]

    lane_box = lax.broadcasted_iota(jnp.int32, (8, 128), 1) // 32
    row_y = lax.broadcasted_iota(jnp.int32, (8, 128), 0)
    base_x = lax.axis_index("gx") * 8
    base_y = lax.axis_index("gy") * 8
    base_z = lax.axis_index("gz") * 4
    place_y0 = (base_y + row_y).astype(F32)
    place_z0 = (base_z + lane_box).astype(F32)

    def one_plane(x, sums, sines):
        local = local_ref[x].reshape(32, 128)
        weights = jnp.concatenate([local * wave_ref[d : d + 1, :] for d in range(3)], axis=0)
        high = weights.astype(BF16)
        low = (weights - high.astype(F32)).astype(BF16)
        product = dot(
            jnp.concatenate([high, low], axis=1), jnp.concatenate([sines, sines], axis=0)
        )
        charge = charge_ref[x]
        found = []
        for d in range(3):
            picked = jnp.zeros((8, 128), F32)
            for z in range(4):
                start = (d * 4 + z) * 8
                for y in range(8):
                    picked = jnp.where(
                        (row_y == y) & (lane_box == z),
                        product[start : start + 8, y * 128 : y * 128 + 128],
                        picked,
                    )
            picked = picked * charge
            forces_ref[d, x] = picked
            found.append(picked)
        places = (
            ((base_x + x).astype(F32) + pos_ref[0, x]) * (1.0 / 32),
            (place_y0 + pos_ref[1, x]) * (1.0 / 64),
            (place_z0 + pos_ref[2, x]) * (1.0 / 64),
        )
        return tuple(
            sums[d * 3 + e] + places[d] * found[e] for d in range(3) for e in range(3)
        )

    sums = (jnp.zeros((8, 128), F32),) * 9
    sums = lax.fori_loop(0, 4, lambda x, sums: one_plane(x, sums, front_ref[x]), sums)
    sums = lax.fori_loop(0, 4, lambda x, sums: one_plane(x + 4, sums, back_ref[x]), sums)
    lane = lax.broadcasted_iota(jnp.int32, (8, 128), 1)
    row = jnp.zeros((8, 128), F32)
    for i in range(9):
        row = jnp.where(lane == i, jnp.sum(sums[i]), row)
    share_ref[...] = jnp.broadcast_to(row[0:1], (512, 128))


def run_forces(far0, far1, pair, side, beyond, following, top_in, top_out, transfer, downward, charge, front, back, positions, wave):
    return pl.pallas_call(
        force_kernel,
        in_specs=[VMEM] * 15,
        out_specs=[VMEM] * 2,
        out_shape=[
            jax.ShapeDtypeStruct((3, 8, 8, 128), F32),
            jax.ShapeDtypeStruct((512, 128), F32),
        ],
        scratch_shapes=[
            pltpu.VMEM((36, 8, 128), F32),
            pltpu.VMEM((1152, 128), BF16),
            pltpu.VMEM((32, 128), F32),
            pltpu.VMEM((8, 4, 8, 128), F32),
        ],
        compiler_params=pltpu.CompilerParams(vmem_limit_bytes=24 << 20),
        name="forces",
    )(far0, far1, pair, side, beyond, following, top_in, top_out, transfer, downward, charge, front, back, positions, wave)


def virial_kernel(scale, rows_ref, virial_ref):
    row = jnp.sum(rows_ref[...], axis=0, keepdims=True) * scale
    for d in range(3):
        virial_ref[d : d + 1, :] = row[:, d * 3 : d * 3 + 3]


def run_virial(rows, scale):
    return pl.pallas_call(
        lambda rows_ref, virial_ref: virial_kernel(scale, rows_ref, virial_ref),
        in_specs=[VMEM],
        out_specs=VMEM,
        out_shape=jax.ShapeDtypeStruct((3, 3), F32),
        compiler_params=pltpu.CompilerParams(vmem_limit_bytes=8 << 20),
        name="virial",
    )(rows)


def swapped(value, axis, kind):
    count = lax.axis_size(axis)
    pairs = []
    for i in range(count):
        hop = (1, -1, 3)[kind]
        pairs.append((i, (i + hop) % count if i % 2 == 0 else (i - hop) % count))
    return lax.ppermute(value, axis, pairs)


def shards(
    features, positions, box_counts, w_hidden, w_charge, wave_numbers, phases,
    upward, downward, transfer, out_scale, in_scale,
):
    phases = phases.reshape(1, 128)
    charge, own, xb = run_atoms(
        features, positions, box_counts.transpose(0, 2, 1), w_hidden, w_charge.reshape(1, 128),
        wave_numbers, phases, upward,
    )
    rb = swapped(xb, "gx", 1)
    front, xa = run_front(positions, wave_numbers, phases, own, 4)
    scale, tin, tout, top_in, top_out = run_tables(in_scale, out_scale, own)
    ra = swapped(xa, "gx", 0)
    leaf, mid, top, ya, yb = glue_x(ra, rb, own, front, scale)
    back = run_sines(positions, wave_numbers, phases, top, 4, 4)
    ra, rb = swapped(ya, "gy", 0), swapped(yb, "gy", 1)
    leaf, mid, top, za, zb = glue_y(ra, rb, leaf, mid, top, back)
    ra, rb = swapped(za, "gz", 0), swapped(zb, "gz", 1)
    beyond = lax.ppermute(
        top, "gz", [(i, (i + (-2 if i % 2 else 2)) % 16) for i in range(16)]
    )
    pair = glue_z(ra, top)
    following = swapped(pair, "gz", 2)
    far0, far1 = run_far(leaf, mid, ra, rb, scale, tin, tout, out_scale, transfer)
    forces, share = run_forces(
        far0, far1, pair, rb, beyond, following, top_in, top_out, transfer, downward, charge, front, back,
        positions, wave_numbers,
    )
    rows = lax.all_to_all(share, ("gx", "gy", "gz"), 0, 0, tiled=True)
    return forces, run_virial(rows, 1.0 / math.sqrt(4194304))


def solution(mesh):
    in_specs = (
        P("gx", "gy", "gz", None),
        P(None, "gx", "gy", "gz"),
        P("gx", "gy", "gz"),
    ) + (P(),) * 9
    out_specs = (P(None, "gx", "gy", "gz"), P())
    return jax.shard_map(shards, mesh=mesh, in_specs=in_specs, out_specs=out_specs, check_vma=False)
```

```python
import functools
import math

import jax
import jax.numpy as jnp
import numpy as np
from jax import lax
from jax.experimental import pallas as pl
from jax.experimental.pallas import tpu as pltpu
from jax.sharding import PartitionSpec as P

F32 = jnp.float32
BF16 = jnp.bfloat16
TURN = 1.0 / (2.0 * math.pi)
SIN_HALF = (4.4428679, -7.30744342, 3.59478808, -0.78437403)
COS_HALF = (1.4142135, -6.97885099, 5.73946117, -1.88356299, 0.31069819)
NT = (((1,), (1,)), ((), ()))
VMEM = pl.BlockSpec(memory_space=pltpu.VMEM)


def dot(a, b):
    return jnp.dot(a, b, preferred_element_type=F32)


def split(value):
    high = value.astype(BF16).astype(F32)
    rest = value - high
    middle = rest.astype(BF16).astype(F32)
    return high, middle, rest - middle


def wave_table(wave_ref, ph_ref, table_ref):
    blocks = []
    for d in range(3):
        high, middle, low = split(wave_ref[d : d + 1, :] * TURN)
        for part in (high, middle, low, high, middle, high):
            blocks.append(jnp.broadcast_to(part, (8, 128)))
    blocks += list(split(ph_ref[...] * TURN)) + [jnp.zeros((109, 128), F32)]
    table_ref[...] = jnp.concatenate(blocks, axis=0).T.astype(BF16)


def turns_of(step, pos_ref, table_ref):
    row_y = lax.broadcasted_iota(jnp.int32, (8, 128), 0)
    blocks = []
    for d in range(3):
        spread = []
        for part in split(pos_ref[d, step] - 0.5):
            spread.append(
                jnp.concatenate([jnp.where(row_y == y, part, 0.0) for y in range(8)], axis=1)
            )
        blocks += [spread[0]] * 3 + [spread[1]] * 2 + [spread[2]]
    blocks += [jnp.ones((8, 1024), F32), jnp.zeros((8, 1024), F32)]
    return dot(table_ref[:, 0:160], jnp.concatenate(blocks, axis=0).astype(BF16))


def poly(coefs, u):
    value = coefs[-1]
    for coef in coefs[-2::-1]:
        value = value * u + coef
    return value


def sines_kernel(start, pos_ref, wave_ref, ph_ref, _, sin_ref, table_ref):
    wave_table(wave_ref, ph_ref, table_ref)

    @pl.loop(0, sin_ref.shape[0])
    def _(x):
        turns = turns_of(start + x, pos_ref, table_ref)
        for y in range(8):
            t = turns[:, y * 128 : (y + 1) * 128]
            r = t - jnp.round(t)
            u = r * r
            sin_ref[x, :, y * 128 : (y + 1) * 128] = (
                poly(SIN_HALF, u) * r * poly(COS_HALF, u)
            ).astype(BF16)


def front_kernel(pos_ref, wave_ref, ph_ref, own_ref, sin_ref, send_ref, table_ref):
    side = 1 - lax.axis_index("gx") % 2
    send_ref[0:64, :] = own_ref[pl.ds(pl.multiple_of(side * 192, 8), 64), :]
    send_ref[64:80, :] = own_ref[pl.ds(pl.multiple_of(256 + side * 16, 8), 16), :]
    send_ref[80:88, :] = own_ref[288:296, :]
    sines_kernel(0, pos_ref, wave_ref, ph_ref, None, sin_ref, table_ref)


def run_front(positions, wave, phases, own, planes):
    return pl.pallas_call(
        front_kernel,
        in_specs=[VMEM] * 4,
        out_specs=[VMEM] * 2,
        out_shape=[
            jax.ShapeDtypeStruct((planes, 128, 1024), BF16),
            jax.ShapeDtypeStruct((88, 128), F32),
        ],
        scratch_shapes=[pltpu.VMEM((128, 256), BF16)],
        cost_estimate=pl.CostEstimate(flops=1 << 30, bytes_accessed=6 << 20, transcendentals=0),
        compiler_params=pltpu.CompilerParams(vmem_limit_bytes=16 << 20),
        name="front",
    )(positions, wave, phases, own)


def run_sines(positions, wave, phases, after, start, planes):
    return pl.pallas_call(
        functools.partial(sines_kernel, start),
        in_specs=[VMEM] * 4,
        out_specs=VMEM,
        out_shape=jax.ShapeDtypeStruct((planes, 128, 1024), BF16),
        scratch_shapes=[pltpu.VMEM((128, 256), BF16)],
        cost_estimate=pl.CostEstimate(flops=1 << 30, bytes_accessed=6 << 20, transcendentals=0),
        compiler_params=pltpu.CompilerParams(vmem_limit_bytes=16 << 20),
        name="sines",
    )(positions, wave, phases, after)


def atoms_kernel(
    feat_hbm, pos_hbm, cnt_hbm, wh_hbm, wc_hbm, wave_hbm, ph_hbm, up_hbm,
    charge_ref, own_ref, sb_ref,
    feat_ref, pos_ref, cnt_ref, wh_ref, wc_ref, wave_ref, ph_ref, up_ref, parts_ref, leaf_ref, mid_ref,
    plane_sems, sems,
):
    def plane(x):
        return pltpu.make_async_copy(feat_hbm.at[x], feat_ref.at[x], plane_sems.at[x])

    others = [
        pltpu.make_async_copy(source, target, sems.at[i])
        for i, (source, target) in enumerate(
            (
                (wave_hbm, wave_ref),
                (ph_hbm, ph_ref),
                (wc_hbm, wc_ref),
                (pos_hbm, pos_ref),
                (wh_hbm, wh_ref),
                (cnt_hbm, cnt_ref),
                (up_hbm, up_ref),
            )
        )
    ]
    for copy in others[:3]:
        copy.start()
    plane(0).start()
    for copy in others[3:6]:
        copy.start()
    for x in range(1, 8):
        plane(x).start()
    others[6].start()
    for copy in others[:3]:
        copy.wait()
    rows = []
    for d in range(3):
        high, middle, low = split(wave_ref[d : d + 1, :] * TURN)
        rows += [high, middle, low, high, middle, high]
    rows += list(split(ph_ref[...] * TURN)) + [jnp.zeros((11, 128), F32)]
    table = jnp.concatenate(rows, axis=0).astype(BF16)
    for row in range(18, 32):
        parts_ref[row * 8 : row * 8 + 8, :] = jnp.full((8, 128), 1.0 if row < 21 else 0.0, F32)
    column = jnp.broadcast_to(wc_ref[...].astype(F32), (128, 128)).T.astype(BF16)
    for copy in others[3:6]:
        copy.wait()

    @pl.loop(0, 8)
    def _(x):
        plane(x).wait()
        atoms_plane(
            x, feat_ref, pos_ref, cnt_ref, wh_ref, wc_ref, charge_ref, leaf_ref, table, column,
            parts_ref,
        )

    others[6].wait()
    atoms_lift(leaf_ref, up_ref, mid_ref, own_ref, sb_ref)


def atoms_plane(
    step, feat_ref, pos_ref, cnt_ref, wh_ref, wc_ref, charge_ref, leaf_ref, table, column,
    parts_ref,
):
    lane_box = lax.broadcasted_iota(jnp.int32, (8, 128), 1) // 32
    lane_slot = lax.broadcasted_iota(jnp.int32, (8, 128), 1) % 32
    row_y = lax.broadcasted_iota(jnp.int32, (8, 128), 0)
    slot = lax.broadcasted_iota(jnp.int32, (32, 128), 0)
    for d in range(3):
        high, middle, low = split(pos_ref[d, step] - 0.5)
        for i, part in enumerate((high, high, high, middle, middle, low)):
            row = (d * 6 + i) * 8
            parts_ref[row : row + 8, :] = part
    lines = [parts_ref[pl.ds(y, 32, stride=8), :].T.astype(BF16) for y in range(8)]
    turns = dot(jnp.concatenate(lines, axis=0), table)

    hidden = dot(feat_ref[step].reshape(1024, 128), wh_ref[...])
    half = hidden * 0.5
    hidden = (half + half * jnp.tanh(half)).astype(BF16)
    broad = dot(hidden, column)
    wc = jnp.broadcast_to(wc_ref[...], (8, 128))
    raw = lax.dot_general(wc, hidden, NT, preferred_element_type=F32)
    counts = jnp.zeros((8, 128), jnp.int32)
    charge = jnp.zeros((8, 128), F32)
    for y in range(8):
        charge = jnp.where(row_y == y, raw[:, y * 128 : (y + 1) * 128], charge)
        for z in range(4):
            count = cnt_ref[step, z, y]
            counts = jnp.where((row_y == y) & (lane_box == z), count, counts)
            start = y * 128 + z * 32
            t = turns[start : start + 32]
            r = t - jnp.round(t)
            s = poly(SIN_HALF, r * r) * r
            terms = jnp.where(slot < count, broad[start : start + 32], 0.0) * (1.0 - s * s)
            leaf_ref[step, z, y : y + 1, :] = jnp.sum(terms, axis=0, keepdims=True)
    charge_ref[step] = jnp.where(lane_slot < counts, charge, 0.0)


def atoms_lift(leaf_ref, up_ref, mid_ref, own_ref, sb_ref):
    total = jnp.zeros((32, 128), F32)
    for child in range(8):
        cx, cy, cz = child // 4, child // 2 % 2, child % 2
        rows = jnp.concatenate(
            [
                leaf_ref[2 * x + cx, 2 * z + cz, pl.ds(cy, 4, stride=2), :]
                for x in range(4)
                for z in range(2)
            ],
            axis=0,
        )
        total = total + dot(rows.astype(BF16), up_ref[0, child])
    for x in range(4):
        for z in range(2):
            for y in range(4):
                row = (x * 2 + z) * 4 + y
                mid_ref[x, y, z : z + 1, :] = total[row : row + 1]
    crown = jnp.zeros((8, 128), F32)
    for child in range(8):
        cx, cy, cz = child // 4, child // 2 % 2, child % 2
        rows = jnp.concatenate(
            [
                mid_ref[2 * x + cx, 2 * y + cy, cz : cz + 1, :]
                for x in range(2)
                for y in range(2)
            ]
            + [jnp.zeros((4, 128), F32)],
            axis=0,
        )
        crown = crown + dot(rows.astype(BF16), up_ref[1, child])
    own_ref[0:256, :] = leaf_ref[...].reshape(256, 128)
    for x in range(4):
        for y in range(4):
            row = 256 + (x * 4 + y) * 2
            own_ref[row : row + 2, :] = mid_ref[x, y]
    own_ref[288:296, :] = crown
    odd = lax.axis_index("gx") % 2
    for ref, high in ((sb_ref, odd),):
        for x in range(2):
            for z in range(4):
                row = (x * 4 + z) * 8
                ref[row : row + 8, :] = leaf_ref[high * 6 + x, z]
            for y in range(4):
                row = 64 + (x * 4 + y) * 2
                ref[row : row + 2, :] = mid_ref[high * 2 + x, y]
        ref[80:84, :] = crown[0:4]
        ref[84:88, :] = jnp.zeros((4, 128), F32)


def run_atoms(features, positions, box_counts, w_hidden, w_charge, wave, phases, upward):
    hbm = pl.BlockSpec(memory_space=pltpu.HBM)
    return pl.pallas_call(
        atoms_kernel,
        in_specs=[hbm] * 8,
        out_specs=[VMEM] * 3,
        out_shape=[
            jax.ShapeDtypeStruct((8, 8, 128), F32),
            jax.ShapeDtypeStruct((296, 128), F32),
            jax.ShapeDtypeStruct((88, 128), F32),
        ],
        scratch_shapes=[
            pltpu.VMEM((8, 8, 128, 128), BF16),
            pltpu.VMEM((3, 8, 8, 128), F32),
            pltpu.SMEM((8, 4, 8), jnp.int32),
            pltpu.VMEM((128, 128), BF16),
            pltpu.VMEM((1, 128), BF16),
            pltpu.VMEM((3, 128), F32),
            pltpu.VMEM((1, 128), F32),
            pltpu.VMEM((2, 8, 128, 128), BF16),
            pltpu.VMEM((256, 128), F32),
            pltpu.VMEM((8, 4, 8, 128), F32),
            pltpu.VMEM((4, 4, 2, 128), F32),
            pltpu.SemaphoreType.DMA((8,)),
            pltpu.SemaphoreType.DMA((7,)),
        ],
        compiler_params=pltpu.CompilerParams(vmem_limit_bytes=58 << 20),
        name="atoms",
    )(features, positions, box_counts, w_hidden, w_charge, wave, phases, upward)


def glue_x_kernel(ra_ref, rb_ref, own_ref, _, __, leafx_ref, midx_ref, topx_ref, ya_ref, yb_ref):
    odd = lax.axis_index("gx") % 2
    leafx_ref[2:10] = own_ref[0:256, :].reshape(8, 4, 8, 128)
    for x in range(4):
        for y in range(4):
            row = 256 + (x * 4 + y) * 2
            midx_ref[2 + x, y] = own_ref[row : row + 2, :]
    for ref, high in ((ra_ref, 1 - odd), (rb_ref, odd)):
        for x in range(2):
            for z in range(4):
                row = (x * 4 + z) * 8
                leafx_ref[high * 10 + x, z] = ref[row : row + 8, :]
            for y in range(4):
                row = 64 + (x * 4 + y) * 2
                midx_ref[high * 6 + x, y] = ref[row : row + 2, :]
    ta, tb = ra_ref[80:84, :], rb_ref[80:84, :]
    topx_ref[...] = jnp.concatenate(
        [
            jnp.where(odd == 1, ta, tb),
            own_ref[288:292, :],
            jnp.where(odd == 1, tb, ta),
            jnp.zeros((4, 128), F32),
        ],
        axis=0,
    )
    odd_y = lax.axis_index("gy") % 2
    for x in range(12):
        for z in range(4):
            tile = leafx_ref[x, z]
            low, high = tile[0:2], tile[6:8]
            row = (x * 4 + z) * 2
            ya_ref[row : row + 2, :] = jnp.where(odd_y == 1, low, high)
            yb_ref[row : row + 2, :] = jnp.where(odd_y == 1, high, low)
    for ref, side in ((ya_ref, 1 - odd_y), (yb_ref, odd_y)):
        for x in range(8):
            for y in range(2):
                row = 96 + (x * 2 + y) * 2
                ref[row : row + 2, :] = midx_ref[x, side * 2 + y]
        ref[128:144, :] = topx_ref[...]


def glue_x(ra, rb, own, front, scale):
    return pl.pallas_call(
        glue_x_kernel,
        in_specs=[VMEM] * 3 + [pl.BlockSpec(memory_space=pl.ANY)] * 2,
        out_specs=[VMEM] * 5,
        out_shape=[
            jax.ShapeDtypeStruct((12, 4, 8, 128), F32),
            jax.ShapeDtypeStruct((8, 4, 2, 128), F32),
            jax.ShapeDtypeStruct((16, 128), F32),
            jax.ShapeDtypeStruct((144, 128), F32),
            jax.ShapeDtypeStruct((144, 128), F32),
        ],
        compiler_params=pltpu.CompilerParams(vmem_limit_bytes=8 << 20),
        name="glue_x",
    )(ra, rb, own, front, scale)


def glue_y_kernel(ra_ref, rb_ref, leafx_ref, midx_ref, topx_ref, _, leafxy_ref, midxy_ref, topxy_ref, za_ref, zb_ref):
    odd = lax.axis_index("gy") % 2
    for x in range(12):
        for z in range(4):
            row = (x * 4 + z) * 2
            a, b = ra_ref[row : row + 2, :], rb_ref[row : row + 2, :]
            leafxy_ref[x, z, 0:2, :] = jnp.where(odd == 1, a, b)
            leafxy_ref[x, z, 2:10, :] = leafx_ref[x, z]
            leafxy_ref[x, z, 10:12, :] = jnp.where(odd == 1, b, a)
    for x in range(8):
        midxy_ref[x, 2:6] = midx_ref[x]
        for ref, high in ((ra_ref, 1 - odd), (rb_ref, odd)):
            for y in range(2):
                row = 96 + (x * 2 + y) * 2
                midxy_ref[x, high * 6 + y] = ref[row : row + 2, :]
    for x in range(6):
        row = 128 + x * 2
        a, b = ra_ref[row : row + 2, :], rb_ref[row : row + 2, :]
        topxy_ref[x * 6 : x * 6 + 2, :] = jnp.where(odd == 1, a, b)
        topxy_ref[x * 6 + 2 : x * 6 + 4, :] = topx_ref[x * 2 : x * 2 + 2, :]
        topxy_ref[x * 6 + 4 : x * 6 + 6, :] = jnp.where(odd == 1, b, a)
    topxy_ref[36:40, :] = jnp.zeros((4, 128), F32)
    odd_z = lax.axis_index("gz") % 2
    for ref, side in ((za_ref, 1 - odd_z), (zb_ref, odd_z)):
        for x in range(12):
            for z in range(2):
                row = (x * 2 + z) * 12
                ref[row : row + 12, :] = leafxy_ref[x, side * 2 + z]
        for x in range(8):
            for y in range(8):
                row = 288 + (x * 8 + y) * 2
                ref[row : row + 2, :] = midxy_ref[x, y]
    za_ref[416:456, :] = topxy_ref[...]
    zb_ref[416:456, :] = topxy_ref[...]


def glue_y(ra, rb, leafx, midx, topx, back):
    return pl.pallas_call(
        glue_y_kernel,
        in_specs=[VMEM] * 5 + [pl.BlockSpec(memory_space=pl.ANY)],
        out_specs=[VMEM] * 5,
        out_shape=[
            jax.ShapeDtypeStruct((12, 4, 12, 128), F32),
            jax.ShapeDtypeStruct((8, 8, 2, 128), F32),
            jax.ShapeDtypeStruct((40, 128), F32),
            jax.ShapeDtypeStruct((456, 128), F32),
            jax.ShapeDtypeStruct((456, 128), F32),
        ],
        compiler_params=pltpu.CompilerParams(vmem_limit_bytes=8 << 20),
        name="glue_y",
    )(ra, rb, leafx, midx, topx, back)


def glue_z_kernel(ra_ref, topxy_ref, pair_ref):
    odd = lax.axis_index("gz") % 2
    mine, other = topxy_ref[0:36, :], ra_ref[416:452, :]
    pair_ref[...] = jnp.concatenate(
        [jnp.where(odd == 1, other, mine), jnp.where(odd == 1, mine, other)], axis=0
    )


def glue_z(ra, topxy):
    return pl.pallas_call(
        glue_z_kernel,
        in_specs=[VMEM] * 2,
        out_specs=VMEM,
        out_shape=jax.ShapeDtypeStruct((72, 128), F32),
        compiler_params=pltpu.CompilerParams(vmem_limit_bytes=8 << 20),
        name="glue_z",
    )(ra, topxy)


def offset_tiles(out_ref, table, cz, masked):
    zero = jnp.zeros((2, 128), F32)
    keep_rows = lax.broadcasted_iota(jnp.int32, (8, 128), 0)
    near = (keep_rows >= 1 + cz) & (keep_rows <= 3 + cz)
    for xy in range(49):
        start = xy * 7 + 1 - cz
        tile = jnp.concatenate([table[start : start + 6, :], zero], axis=0)
        if masked and 2 <= xy // 7 <= 4 and 2 <= xy % 7 <= 4:
            tile = jnp.where(near, 0.0, tile)
        out_ref[xy] = tile


def tables_kernel(in_ref, out_ref, _, scale_ref, tin_ref, tout_ref, top_in_ref, top_out_ref):
    scale_ref[...] = in_ref[0]
    for x in range(2, 5):
        for y in range(2, 5):
            row = x * 49 + y * 7 + 2
            scale_ref[row : row + 3, :] = jnp.zeros((3, 128), F32)
    for cz in range(2):
        offset_tiles(tin_ref.at[cz], in_ref.at[1], cz, True)
        offset_tiles(tout_ref.at[cz], out_ref.at[1], cz, False)
    odd = lax.axis_index("gz") % 2
    lanes = lax.broadcasted_iota(jnp.int32, (8, 128), 0)
    near = (lanes >= 1 + odd) & (lanes <= 3 + odd)
    for xy in range(49):
        for ref, table, masked in ((top_in_ref, in_ref, True), (top_out_ref, out_ref, False)):
            rows = table[2, xy * 7 : xy * 7 + 7, :]
            tile = jnp.where(odd == 1, rows[0:6], rows[1:7])
            tile = jnp.concatenate([tile, jnp.zeros((2, 128), F32)], axis=0)
            if masked and 2 <= xy // 7 <= 4 and 2 <= xy % 7 <= 4:
                tile = jnp.where(near, 0.0, tile)
            ref[xy] = tile


def run_tables(in_scale, out_scale, after):
    return pl.pallas_call(
        tables_kernel,
        in_specs=[VMEM] * 2 + [pl.BlockSpec(memory_space=pl.ANY)],
        out_specs=[VMEM] * 5,
        out_shape=[
            jax.ShapeDtypeStruct((343, 128), F32),
            jax.ShapeDtypeStruct((2, 49, 8, 128), F32),
            jax.ShapeDtypeStruct((2, 49, 8, 128), F32),
            jax.ShapeDtypeStruct((49, 8, 128), F32),
            jax.ShapeDtypeStruct((49, 8, 128), F32),
        ],
        cost_estimate=pl.CostEstimate(flops=1 << 28, bytes_accessed=3 << 20, transcendentals=0),
        compiler_params=pltpu.CompilerParams(vmem_limit_bytes=8 << 20),
        name="tables",
    )(in_scale, out_scale, after)


def far_kernel(
    leafxy_ref, midxy_ref, ra_ref, rb_ref, scale_ref, tin_ref, tout_ref, out_ref, core_ref,
    far0_ref, far1_ref,
    leaf_ref, mid_ref, acc_ref, even_ref, odd_ref,
):
    odd = lax.axis_index("gz") % 2
    leaf_ref[:, 2:6] = leafxy_ref[...]
    for ref, high in ((ra_ref, 1 - odd), (rb_ref, odd)):
        for x in range(12):
            for z in range(2):
                row = (x * 2 + z) * 12
                leaf_ref[x, high * 6 + z] = ref[row : row + 12, :]
    for x in range(8):
        for y in range(8):
            row = 288 + (x * 8 + y) * 2
            a, b = ra_ref[row : row + 2, :], rb_ref[row : row + 2, :]
            mid_ref[x, y] = jnp.concatenate(
                [
                    jnp.where(odd == 1, a, b),
                    midxy_ref[x, y],
                    jnp.where(odd == 1, b, a),
                    jnp.zeros((2, 128), F32),
                ],
                axis=0,
            )
    def products(operand_ref, core):
        rows = 384
        return [dot(operand_ref[i * rows : i * rows + rows, :], core) for i in range(4)]

    far0_ref[...] = jnp.zeros((8, 32, 128), F32)
    core0 = core_ref[0]

    def row_of(qx, qy, qz, pair, cz):
        return (qx + 1 - pair // 2) * 49 + (qy + 1 - pair % 2) * 7 + qz + 1 - cz

    def build_leaf(step, operand_ref):
        qx, qz = step // 6, step % 6
        for qy in range(6):
            tiles = []
            for x in range(4):
                for z in range(2):
                    tiles.append(leaf_ref[2 * x + qx, 2 * z + qz, pl.ds(qy, 4, stride=2), :])
            source = jnp.concatenate(tiles, axis=0)
            for pair in range(4):
                for cz in range(2):
                    start = ((pair * 2 + cz) * 6 + qy) * 32
                    row = row_of(qx, qy, qz, pair, cz)
                    scale = jnp.broadcast_to(scale_ref[pl.ds(row, 1), :], (32, 128))
                    operand_ref[start : start + 32, :] = (source * scale).astype(BF16)

    def apply_leaf(step, image):
        qx, qz = step // 6, step % 6
        for pair in range(4):
            for cz in range(2):
                total = far0_ref[pair * 2 + cz]
                for qy in range(6):
                    row = row_of(qx, qy, qz, pair, cz)
                    scale = jnp.broadcast_to(out_ref[0, pl.ds(row, 1), :], (32, 128))
                    start = ((pair * 2 + cz) * 6 + qy) * 32
                    total = total + scale * image[start // 384][start % 384 : start % 384 + 32]
                far0_ref[pair * 2 + cz] = total

    build_leaf(0, even_ref)

    @pl.loop(0, 18)
    def _(turn):
        image = products(even_ref, core0)
        build_leaf(2 * turn + 1, odd_ref)
        apply_leaf(2 * turn, image)
        image = products(odd_ref, core0)
        build_leaf(jnp.minimum(2 * turn + 2, 35), even_ref)
        apply_leaf(2 * turn + 1, image)

    acc_ref[...] = jnp.zeros((8, 32, 128), F32)
    core1 = core_ref[1]

    def build_mid(qx, operand_ref):
        for qy in range(6):
            tiles = [mid_ref[2 * x + qx, 2 * y + qy] for x in range(2) for y in range(2)]
            for pair in range(4):
                xy = (qx + 1 - pair // 2) * 7 + qy + 1 - pair % 2
                for cz in range(2):
                    scale = tin_ref[cz, xy]
                    start = ((pair * 2 + cz) * 6 + qy) * 32
                    operand_ref[start : start + 32, :] = jnp.concatenate(
                        [tile * scale for tile in tiles], axis=0
                    ).astype(BF16)

    def apply_mid(qx, image):
        for pair in range(4):
            for cz in range(2):
                total = acc_ref[pair * 2 + cz]
                for qy in range(6):
                    scale = tout_ref[cz, (qx + 1 - pair // 2) * 7 + qy + 1 - pair % 2]
                    scale = jnp.concatenate([scale] * 4, axis=0)
                    start = ((pair * 2 + cz) * 6 + qy) * 32
                    total = total + scale * image[start // 384][start % 384 : start % 384 + 32]
                acc_ref[pair * 2 + cz] = total

    build_mid(0, even_ref)

    @pl.loop(0, 3)
    def _(turn):
        image = products(even_ref, core1)
        build_mid(2 * turn + 1, odd_ref)
        apply_mid(2 * turn, image)
        image = products(odd_ref, core1)
        build_mid(jnp.minimum(2 * turn + 2, 5), even_ref)
        apply_mid(2 * turn + 1, image)

    for child in range(8):
        for parent in range(4):
            tile = acc_ref[child, parent * 8 : parent * 8 + 8, :]
            far1_ref[child * 4 + parent : child * 4 + parent + 1, :] = jnp.sum(
                tile, axis=0, keepdims=True
            )


def run_far(leafxy, midxy, ra, rb, scale, tin, tout, out_scale, transfer):
    return pl.pallas_call(
        far_kernel,
        in_specs=[VMEM] * 9,
        out_specs=[VMEM] * 2,
        out_shape=[
            jax.ShapeDtypeStruct((8, 32, 128), F32),
            jax.ShapeDtypeStruct((32, 128), F32),
        ],
        scratch_shapes=[
            pltpu.VMEM((12, 8, 12, 128), F32),
            pltpu.VMEM((8, 8, 8, 128), F32),
            pltpu.VMEM((8, 32, 128), F32),
            pltpu.VMEM((1536, 128), BF16),
            pltpu.VMEM((1536, 128), BF16),
        ],
        cost_estimate=pl.CostEstimate(flops=4 << 30, bytes_accessed=4 << 20, transcendentals=0),
        compiler_params=pltpu.CompilerParams(vmem_limit_bytes=24 << 20),
        name="far",
    )(leafxy, midxy, ra, rb, scale, tin, tout, out_scale, transfer)


def force_kernel(
    far0_ref, far1_ref, pair_ref, side_ref, far_ref, next_ref, tin_ref, tout_ref, core_ref, down_ref,
    charge_ref, front_ref, back_ref, pos_ref, wave_ref,
    forces_ref, share_ref,
    window_ref, operand_ref, mid_ref, local_ref,
):
    odd = lax.axis_index("gz") % 2
    near, beyond = side_ref[416:452, :], far_ref[0:36, :]
    first, second = next_ref[0:36, :], next_ref[36:72, :]
    lines = [
        jnp.where(odd == 1, first, beyond),
        jnp.where(odd == 1, second, near),
        pair_ref[0:36, :],
        pair_ref[36:72, :],
        jnp.where(odd == 1, near, first),
        jnp.where(odd == 1, beyond, second),
    ]
    for xy in range(36):
        window_ref[xy] = jnp.concatenate(
            [line[xy : xy + 1] for line in lines] + [jnp.zeros((2, 128), F32)], axis=0
        )
    for qx in range(6):
        for qy in range(6):
            source = window_ref[qx * 6 + qy]
            tiles = []
            for pair in range(4):
                cx, cy = pair // 2, pair % 2
                tiles.append(source * tin_ref[(qx + 1 - cx) * 7 + qy + 1 - cy])
            start = (qx * 6 + qy) * 32
            operand_ref[start : start + 32, :] = jnp.concatenate(tiles, axis=0).astype(BF16)
    totals = [jnp.zeros((8, 128), F32) for _ in range(4)]
    for qx in range(6):
        image = dot(operand_ref[qx * 192 : qx * 192 + 192, :], core_ref[2])
        for qy in range(6):
            for pair in range(4):
                cx, cy = pair // 2, pair % 2
                scale = tout_ref[(qx + 1 - cx) * 7 + qy + 1 - cy]
                start = qy * 32 + pair * 8
                totals[pair] = totals[pair] + scale * image[start : start + 8]
    local_top = jnp.concatenate(
        [jnp.sum(total, axis=0, keepdims=True) for total in totals] + [jnp.zeros((4, 128), F32)],
        axis=0,
    ).astype(BF16)
    for child in range(8):
        cx, cy, cz = child // 4, child // 2 % 2, child % 2
        rows = far1_ref[child * 4 : child * 4 + 4, :] + dot(local_top, down_ref[1, child])[0:4]
        for parent in range(4):
            row = ((2 * (parent // 2) + cx) * 2 + cz) * 4 + 2 * (parent % 2) + cy
            mid_ref[row : row + 1, :] = rows[parent : parent + 1]
    local_mid = mid_ref[...].astype(BF16)
    for child in range(8):
        cx, cy, cz = child // 4, child // 2 % 2, child % 2
        rows = far0_ref[child] + dot(local_mid, down_ref[0, child])
        for x in range(4):
            for z in range(2):
                start = (x * 2 + z) * 4
                local_ref[2 * x + cx, 2 * z + cz, pl.ds(cy, 4, stride=2), :] = rows[start : start + 4]

    lane_box = lax.broadcasted_iota(jnp.int32, (8, 128), 1) // 32
    row_y = lax.broadcasted_iota(jnp.int32, (8, 128), 0)
    base_x = lax.axis_index("gx") * 8
    base_y = lax.axis_index("gy") * 8
    base_z = lax.axis_index("gz") * 4
    place_y0 = (base_y + row_y).astype(F32)
    place_z0 = (base_z + lane_box).astype(F32)

    def one_plane(x, sums, sines):
        local = local_ref[x].reshape(32, 128)
        weights = jnp.concatenate([local * wave_ref[d : d + 1, :] for d in range(3)], axis=0)
        high = weights.astype(BF16)
        low = (weights - high.astype(F32)).astype(BF16)
        product = dot(
            jnp.concatenate([high, low], axis=1), jnp.concatenate([sines, sines], axis=0)
        )
        charge = charge_ref[x]
        found = []
        for d in range(3):
            picked = jnp.zeros((8, 128), F32)
            for z in range(4):
                start = (d * 4 + z) * 8
                for y in range(8):
                    picked = jnp.where(
                        (row_y == y) & (lane_box == z),
                        product[start : start + 8, y * 128 : y * 128 + 128],
                        picked,
                    )
            picked = picked * charge
            forces_ref[d, x] = picked
            found.append(picked)
        places = (
            ((base_x + x).astype(F32) + pos_ref[0, x]) * (1.0 / 32),
            (place_y0 + pos_ref[1, x]) * (1.0 / 64),
            (place_z0 + pos_ref[2, x]) * (1.0 / 64),
        )
        return tuple(
            sums[d * 3 + e] + places[d] * found[e] for d in range(3) for e in range(3)
        )

    sums = (jnp.zeros((8, 128), F32),) * 9
    sums = lax.fori_loop(0, 4, lambda x, sums: one_plane(x, sums, front_ref[x]), sums)
    sums = lax.fori_loop(0, 4, lambda x, sums: one_plane(x + 4, sums, back_ref[x]), sums)
    lane = lax.broadcasted_iota(jnp.int32, (8, 128), 1)
    row = jnp.zeros((8, 128), F32)
    for i in range(9):
        row = jnp.where(lane == i, jnp.sum(sums[i]), row)
    share_ref[...] = jnp.broadcast_to(row[0:1], (512, 128))


def run_forces(far0, far1, pair, side, beyond, following, top_in, top_out, transfer, downward, charge, front, back, positions, wave):
    return pl.pallas_call(
        force_kernel,
        in_specs=[VMEM] * 15,
        out_specs=[VMEM] * 2,
        out_shape=[
            jax.ShapeDtypeStruct((3, 8, 8, 128), F32),
            jax.ShapeDtypeStruct((512, 128), F32),
        ],
        scratch_shapes=[
            pltpu.VMEM((36, 8, 128), F32),
            pltpu.VMEM((1152, 128), BF16),
            pltpu.VMEM((32, 128), F32),
            pltpu.VMEM((8, 4, 8, 128), F32),
        ],
        compiler_params=pltpu.CompilerParams(vmem_limit_bytes=24 << 20),
        name="forces",
    )(far0, far1, pair, side, beyond, following, top_in, top_out, transfer, downward, charge, front, back, positions, wave)


def virial_kernel(scale, rows_ref, virial_ref):
    row = jnp.sum(rows_ref[...], axis=0, keepdims=True) * scale
    for d in range(3):
        virial_ref[d : d + 1, :] = row[:, d * 3 : d * 3 + 3]


def run_virial(rows, scale):
    return pl.pallas_call(
        lambda rows_ref, virial_ref: virial_kernel(scale, rows_ref, virial_ref),
        in_specs=[VMEM],
        out_specs=VMEM,
        out_shape=jax.ShapeDtypeStruct((3, 3), F32),
        compiler_params=pltpu.CompilerParams(vmem_limit_bytes=8 << 20),
        name="virial",
    )(rows)


def swapped(value, axis, kind):
    count = lax.axis_size(axis)
    pairs = []
    for i in range(count):
        hop = (1, -1, 3)[kind]
        pairs.append((i, (i + hop) % count if i % 2 == 0 else (i - hop) % count))
    return lax.ppermute(value, axis, pairs)


def shards(
    features, positions, box_counts, w_hidden, w_charge, wave_numbers, phases,
    upward, downward, transfer, out_scale, in_scale,
):
    phases = phases.reshape(1, 128)
    charge, own, xb = run_atoms(
        features, positions, box_counts.transpose(0, 2, 1), w_hidden, w_charge.reshape(1, 128),
        wave_numbers, phases, upward,
    )
    rb = swapped(xb, "gx", 1)
    front, xa = run_front(positions, wave_numbers, phases, own, 4)
    scale, tin, tout, top_in, top_out = run_tables(in_scale, out_scale, own)
    ra = swapped(xa, "gx", 0)
    leaf, mid, top, ya, yb = glue_x(ra, rb, own, front, scale)
    back = run_sines(positions, wave_numbers, phases, top, 4, 4)
    ra, rb = swapped(ya, "gy", 0), swapped(yb, "gy", 1)
    leaf, mid, top, za, zb = glue_y(ra, rb, leaf, mid, top, back)
    ra, rb = swapped(za, "gz", 0), swapped(zb, "gz", 1)
    beyond = lax.ppermute(
        top, "gz", [(i, (i + (-2 if i % 2 else 2)) % 16) for i in range(16)]
    )
    pair = glue_z(ra, top)
    following = swapped(pair, "gz", 2)
    far0, far1 = run_far(leaf, mid, ra, rb, scale, tin, tout, out_scale, transfer)
    forces, share = run_forces(
        far0, far1, pair, rb, beyond, following, top_in, top_out, transfer, downward, charge, front, back,
        positions, wave_numbers,
    )
    rows = lax.all_to_all(share, ("gx", "gy", "gz"), 0, 0, tiled=True)
    return forces, run_virial(rows, 1.0 / math.sqrt(4194304))


def solution(mesh):
    in_specs = (
        P("gx", "gy", "gz", None),
        P(None, "gx", "gy", "gz"),
        P("gx", "gy", "gz"),
    ) + (P(),) * 9
    out_specs = (P(None, "gx", "gy", "gz"), P())
    return jax.shard_map(shards, mesh=mesh, in_specs=in_specs, out_specs=out_specs, check_vma=False)
```

```python
import functools
import math

import jax
import jax.numpy as jnp
import numpy as np
from jax import lax
from jax.experimental import pallas as pl
from jax.experimental.pallas import tpu as pltpu
from jax.sharding import PartitionSpec as P

F32 = jnp.float32
BF16 = jnp.bfloat16
TURN = 1.0 / (2.0 * math.pi)
SIN_HALF = (4.4428679, -7.30744342, 3.59478808, -0.78437403)
COS_HALF = (1.4142135, -6.97885099, 5.73946117, -1.88356299, 0.31069819)
NT = (((1,), (1,)), ((), ()))
VMEM = pl.BlockSpec(memory_space=pltpu.VMEM)


def dot(a, b):
    return jnp.dot(a, b, preferred_element_type=F32)


def split(value):
    high = value.astype(BF16).astype(F32)
    rest = value - high
    middle = rest.astype(BF16).astype(F32)
    return high, middle, rest - middle


def wave_table(wave_ref, ph_ref, table_ref):
    blocks = []
    for d in range(3):
        high, middle, low = split(wave_ref[d : d + 1, :] * TURN)
        for part in (high, middle, low, high, middle, high):
            blocks.append(jnp.broadcast_to(part, (8, 128)))
    blocks += list(split(ph_ref[...] * TURN)) + [jnp.zeros((109, 128), F32)]
    table_ref[...] = jnp.concatenate(blocks, axis=0).T.astype(BF16)


def turns_of(step, pos_ref, table_ref):
    row_y = lax.broadcasted_iota(jnp.int32, (8, 128), 0)
    blocks = []
    for d in range(3):
        spread = []
        for part in split(pos_ref[d, step] - 0.5):
            spread.append(
                jnp.concatenate([jnp.where(row_y == y, part, 0.0) for y in range(8)], axis=1)
            )
        blocks += [spread[0]] * 3 + [spread[1]] * 2 + [spread[2]]
    blocks += [jnp.ones((8, 1024), F32), jnp.zeros((8, 1024), F32)]
    return dot(table_ref[:, 0:160], jnp.concatenate(blocks, axis=0).astype(BF16))


def poly(coefs, u):
    value = coefs[-1]
    for coef in coefs[-2::-1]:
        value = value * u + coef
    return value


def sines_kernel(start, pos_ref, wave_ref, ph_ref, _, sin_ref, table_ref):
    wave_table(wave_ref, ph_ref, table_ref)

    @pl.loop(0, sin_ref.shape[0])
    def _(x):
        turns = turns_of(start + x, pos_ref, table_ref)
        for y in range(8):
            t = turns[:, y * 128 : (y + 1) * 128]
            r = t - jnp.round(t)
            u = r * r
            sin_ref[x, :, y * 128 : (y + 1) * 128] = (
                poly(SIN_HALF, u) * r * poly(COS_HALF, u)
            ).astype(BF16)


def front_kernel(pos_ref, wave_ref, ph_ref, own_ref, sin_ref, send_ref, table_ref):
    side = 1 - lax.axis_index("gx") % 2
    send_ref[0:64, :] = own_ref[pl.ds(pl.multiple_of(side * 192, 8), 64), :]
    send_ref[64:80, :] = own_ref[pl.ds(pl.multiple_of(256 + side * 16, 8), 16), :]
    send_ref[80:88, :] = own_ref[288:296, :]
    sines_kernel(0, pos_ref, wave_ref, ph_ref, None, sin_ref, table_ref)


def run_front(positions, wave, phases, own, planes):
    return pl.pallas_call(
        front_kernel,
        in_specs=[VMEM] * 4,
        out_specs=[VMEM] * 2,
        out_shape=[
            jax.ShapeDtypeStruct((planes, 128, 1024), BF16),
            jax.ShapeDtypeStruct((88, 128), F32),
        ],
        scratch_shapes=[pltpu.VMEM((128, 256), BF16)],
        cost_estimate=pl.CostEstimate(flops=1 << 30, bytes_accessed=6 << 20, transcendentals=0),
        compiler_params=pltpu.CompilerParams(vmem_limit_bytes=16 << 20),
        name="front",
    )(positions, wave, phases, own)


def run_sines(positions, wave, phases, after, start, planes):
    return pl.pallas_call(
        functools.partial(sines_kernel, start),
        in_specs=[VMEM] * 4,
        out_specs=VMEM,
        out_shape=jax.ShapeDtypeStruct((planes, 128, 1024), BF16),
        scratch_shapes=[pltpu.VMEM((128, 256), BF16)],
        cost_estimate=pl.CostEstimate(flops=1 << 30, bytes_accessed=6 << 20, transcendentals=0),
        compiler_params=pltpu.CompilerParams(vmem_limit_bytes=16 << 20),
        name="sines",
    )(positions, wave, phases, after)


def atoms_kernel(
    feat_hbm, pos_hbm, cnt_hbm, wh_hbm, wc_hbm, wave_hbm, ph_hbm, up_hbm,
    charge_ref, own_ref, sb_ref,
    feat_ref, pos_ref, cnt_ref, wh_ref, wc_ref, wave_ref, ph_ref, up_ref, parts_ref, leaf_ref, mid_ref,
    plane_sems, sems,
):
    def plane(x):
        return pltpu.make_async_copy(feat_hbm.at[x], feat_ref.at[x], plane_sems.at[x])

    others = [
        pltpu.make_async_copy(source, target, sems.at[i])
        for i, (source, target) in enumerate(
            (
                (wave_hbm, wave_ref),
                (ph_hbm, ph_ref),
                (wc_hbm, wc_ref),
                (pos_hbm, pos_ref),
                (wh_hbm, wh_ref),
                (cnt_hbm, cnt_ref),
                (up_hbm, up_ref),
            )
        )
    ]
    for copy in others[:3]:
        copy.start()
    plane(0).start()
    for copy in others[3:6]:
        copy.start()
    for x in range(1, 8):
        plane(x).start()
    others[6].start()
    for copy in others[:3]:
        copy.wait()
    rows = []
    for d in range(3):
        high, middle, low = split(wave_ref[d : d + 1, :] * TURN)
        rows += [high, middle, low, high, middle, high]
    rows += list(split(ph_ref[...] * TURN)) + [jnp.zeros((11, 128), F32)]
    table = jnp.concatenate(rows, axis=0).astype(BF16)
    for row in range(18, 32):
        parts_ref[row * 8 : row * 8 + 8, :] = jnp.full((8, 128), 1.0 if row < 21 else 0.0, F32)
    column = jnp.broadcast_to(wc_ref[...].astype(F32), (128, 128)).T.astype(BF16)
    for copy in others[3:6]:
        copy.wait()

    @pl.loop(0, 8)
    def _(x):
        plane(x).wait()
        atoms_plane(
            x, feat_ref, pos_ref, cnt_ref, wh_ref, wc_ref, charge_ref, leaf_ref, table, column,
            parts_ref,
        )

    others[6].wait()
    atoms_lift(leaf_ref, up_ref, mid_ref, own_ref, sb_ref)


def atoms_plane(
    step, feat_ref, pos_ref, cnt_ref, wh_ref, wc_ref, charge_ref, leaf_ref, table, column,
    parts_ref,
):
    lane_box = lax.broadcasted_iota(jnp.int32, (8, 128), 1) // 32
    lane_slot = lax.broadcasted_iota(jnp.int32, (8, 128), 1) % 32
    row_y = lax.broadcasted_iota(jnp.int32, (8, 128), 0)
    slot = lax.broadcasted_iota(jnp.int32, (32, 128), 0)
    for d in range(3):
        high, middle, low = split(pos_ref[d, step] - 0.5)
        for i, part in enumerate((high, high, high, middle, middle, low)):
            row = (d * 6 + i) * 8
            parts_ref[row : row + 8, :] = part
    lines = [parts_ref[pl.ds(y, 32, stride=8), :].T.astype(BF16) for y in range(8)]
    turns = dot(jnp.concatenate(lines, axis=0), table)

    hidden = dot(feat_ref[step].reshape(1024, 128), wh_ref[...])
    half = hidden * 0.5
    hidden = (half + half * jnp.tanh(half)).astype(BF16)
    broad = dot(hidden, column)
    wc = jnp.broadcast_to(wc_ref[...], (8, 128))
    raw = lax.dot_general(wc, hidden, NT, preferred_element_type=F32)
    counts = jnp.zeros((8, 128), jnp.int32)
    charge = jnp.zeros((8, 128), F32)
    for y in range(8):
        charge = jnp.where(row_y == y, raw[:, y * 128 : (y + 1) * 128], charge)
        for z in range(4):
            count = cnt_ref[step, z, y]
            counts = jnp.where((row_y == y) & (lane_box == z), count, counts)
            start = y * 128 + z * 32
            t = turns[start : start + 32]
            r = t - jnp.round(t)
            s = poly(SIN_HALF, r * r) * r
            terms = jnp.where(slot < count, broad[start : start + 32], 0.0) * (1.0 - s * s)
            leaf_ref[step, z, y : y + 1, :] = jnp.sum(terms, axis=0, keepdims=True)
    charge_ref[step] = jnp.where(lane_slot < counts, charge, 0.0)


def atoms_lift(leaf_ref, up_ref, mid_ref, own_ref, sb_ref):
    total = jnp.zeros((32, 128), F32)
    for child in range(8):
        cx, cy, cz = child // 4, child // 2 % 2, child % 2
        rows = jnp.concatenate(
            [
                leaf_ref[2 * x + cx, 2 * z + cz, pl.ds(cy, 4, stride=2), :]
                for x in range(4)
                for z in range(2)
            ],
            axis=0,
        )
        total = total + dot(rows.astype(BF16), up_ref[0, child])
    for x in range(4):
        for z in range(2):
            for y in range(4):
                row = (x * 2 + z) * 4 + y
                mid_ref[x, y, z : z + 1, :] = total[row : row + 1]
    crown = jnp.zeros((8, 128), F32)
    for child in range(8):
        cx, cy, cz = child // 4, child // 2 % 2, child % 2
        rows = jnp.concatenate(
            [
                mid_ref[2 * x + cx, 2 * y + cy, cz : cz + 1, :]
                for x in range(2)
                for y in range(2)
            ]
            + [jnp.zeros((4, 128), F32)],
            axis=0,
        )
        crown = crown + dot(rows.astype(BF16), up_ref[1, child])
    own_ref[0:256, :] = leaf_ref[...].reshape(256, 128)
    for x in range(4):
        for y in range(4):
            row = 256 + (x * 4 + y) * 2
            own_ref[row : row + 2, :] = mid_ref[x, y]
    own_ref[288:296, :] = crown
    odd = lax.axis_index("gx") % 2
    for ref, high in ((sb_ref, odd),):
        for x in range(2):
            for z in range(4):
                row = (x * 4 + z) * 8
                ref[row : row + 8, :] = leaf_ref[high * 6 + x, z]
            for y in range(4):
                row = 64 + (x * 4 + y) * 2
                ref[row : row + 2, :] = mid_ref[high * 2 + x, y]
        ref[80:84, :] = crown[0:4]
        ref[84:88, :] = jnp.zeros((4, 128), F32)


def run_atoms(features, positions, box_counts, w_hidden, w_charge, wave, phases, upward):
    hbm = pl.BlockSpec(memory_space=pltpu.HBM)
    return pl.pallas_call(
        atoms_kernel,
        in_specs=[hbm] * 8,
        out_specs=[VMEM] * 3,
        out_shape=[
            jax.ShapeDtypeStruct((8, 8, 128), F32),
            jax.ShapeDtypeStruct((296, 128), F32),
            jax.ShapeDtypeStruct((88, 128), F32),
        ],
        scratch_shapes=[
            pltpu.VMEM((8, 8, 128, 128), BF16),
            pltpu.VMEM((3, 8, 8, 128), F32),
            pltpu.SMEM((8, 4, 8), jnp.int32),
            pltpu.VMEM((128, 128), BF16),
            pltpu.VMEM((1, 128), BF16),
            pltpu.VMEM((3, 128), F32),
            pltpu.VMEM((1, 128), F32),
            pltpu.VMEM((2, 8, 128, 128), BF16),
            pltpu.VMEM((256, 128), F32),
            pltpu.VMEM((8, 4, 8, 128), F32),
            pltpu.VMEM((4, 4, 2, 128), F32),
            pltpu.SemaphoreType.DMA((8,)),
            pltpu.SemaphoreType.DMA((7,)),
        ],
        compiler_params=pltpu.CompilerParams(vmem_limit_bytes=58 << 20),
        name="atoms",
    )(features, positions, box_counts, w_hidden, w_charge, wave, phases, upward)


def glue_x_kernel(ra_ref, rb_ref, own_ref, _, __, leafx_ref, midx_ref, topx_ref, ya_ref, yb_ref):
    odd = lax.axis_index("gx") % 2
    leafx_ref[2:10] = own_ref[0:256, :].reshape(8, 4, 8, 128)
    for x in range(4):
        for y in range(4):
            row = 256 + (x * 4 + y) * 2
            midx_ref[2 + x, y] = own_ref[row : row + 2, :]
    for ref, high in ((ra_ref, 1 - odd), (rb_ref, odd)):
        for x in range(2):
            for z in range(4):
                row = (x * 4 + z) * 8
                leafx_ref[high * 10 + x, z] = ref[row : row + 8, :]
            for y in range(4):
                row = 64 + (x * 4 + y) * 2
                midx_ref[high * 6 + x, y] = ref[row : row + 2, :]
    ta, tb = ra_ref[80:84, :], rb_ref[80:84, :]
    topx_ref[...] = jnp.concatenate(
        [
            jnp.where(odd == 1, ta, tb),
            own_ref[288:292, :],
            jnp.where(odd == 1, tb, ta),
            jnp.zeros((4, 128), F32),
        ],
        axis=0,
    )
    odd_y = lax.axis_index("gy") % 2
    for x in range(12):
        for z in range(4):
            tile = leafx_ref[x, z]
            low, high = tile[0:2], tile[6:8]
            row = (x * 4 + z) * 2
            ya_ref[row : row + 2, :] = jnp.where(odd_y == 1, low, high)
            yb_ref[row : row + 2, :] = jnp.where(odd_y == 1, high, low)
    for ref, side in ((ya_ref, 1 - odd_y), (yb_ref, odd_y)):
        for x in range(8):
            for y in range(2):
                row = 96 + (x * 2 + y) * 2
                ref[row : row + 2, :] = midx_ref[x, side * 2 + y]
        ref[128:144, :] = topx_ref[...]


def glue_x(ra, rb, own, front, scale):
    return pl.pallas_call(
        glue_x_kernel,
        in_specs=[VMEM] * 3 + [pl.BlockSpec(memory_space=pl.ANY)] * 2,
        out_specs=[VMEM] * 5,
        out_shape=[
            jax.ShapeDtypeStruct((12, 4, 8, 128), F32),
            jax.ShapeDtypeStruct((8, 4, 2, 128), F32),
            jax.ShapeDtypeStruct((16, 128), F32),
            jax.ShapeDtypeStruct((144, 128), F32),
            jax.ShapeDtypeStruct((144, 128), F32),
        ],
        compiler_params=pltpu.CompilerParams(vmem_limit_bytes=8 << 20),
        name="glue_x",
    )(ra, rb, own, front, scale)


def glue_y_kernel(ra_ref, rb_ref, leafx_ref, midx_ref, topx_ref, _, leafxy_ref, midxy_ref, topxy_ref, za_ref, zb_ref):
    odd = lax.axis_index("gy") % 2
    for x in range(12):
        for z in range(4):
            row = (x * 4 + z) * 2
            a, b = ra_ref[row : row + 2, :], rb_ref[row : row + 2, :]
            leafxy_ref[x, z, 0:2, :] = jnp.where(odd == 1, a, b)
            leafxy_ref[x, z, 2:10, :] = leafx_ref[x, z]
            leafxy_ref[x, z, 10:12, :] = jnp.where(odd == 1, b, a)
    for x in range(8):
        midxy_ref[x, 2:6] = midx_ref[x]
        for ref, high in ((ra_ref, 1 - odd), (rb_ref, odd)):
            for y in range(2):
                row = 96 + (x * 2 + y) * 2
                midxy_ref[x, high * 6 + y] = ref[row : row + 2, :]
    for x in range(6):
        row = 128 + x * 2
        a, b = ra_ref[row : row + 2, :], rb_ref[row : row + 2, :]
        topxy_ref[x * 6 : x * 6 + 2, :] = jnp.where(odd == 1, a, b)
        topxy_ref[x * 6 + 2 : x * 6 + 4, :] = topx_ref[x * 2 : x * 2 + 2, :]
        topxy_ref[x * 6 + 4 : x * 6 + 6, :] = jnp.where(odd == 1, b, a)
    topxy_ref[36:40, :] = jnp.zeros((4, 128), F32)
    odd_z = lax.axis_index("gz") % 2
    for ref, side in ((za_ref, 1 - odd_z), (zb_ref, odd_z)):
        for x in range(12):
            for z in range(2):
                row = (x * 2 + z) * 12
                ref[row : row + 12, :] = leafxy_ref[x, side * 2 + z]
        for x in range(8):
            for y in range(8):
                row = 288 + (x * 8 + y) * 2
                ref[row : row + 2, :] = midxy_ref[x, y]
    za_ref[416:456, :] = topxy_ref[...]
    zb_ref[416:456, :] = topxy_ref[...]


def glue_y(ra, rb, leafx, midx, topx, back):
    return pl.pallas_call(
        glue_y_kernel,
        in_specs=[VMEM] * 5 + [pl.BlockSpec(memory_space=pl.ANY)],
        out_specs=[VMEM] * 5,
        out_shape=[
            jax.ShapeDtypeStruct((12, 4, 12, 128), F32),
            jax.ShapeDtypeStruct((8, 8, 2, 128), F32),
            jax.ShapeDtypeStruct((40, 128), F32),
            jax.ShapeDtypeStruct((456, 128), F32),
            jax.ShapeDtypeStruct((456, 128), F32),
        ],
        compiler_params=pltpu.CompilerParams(vmem_limit_bytes=8 << 20),
        name="glue_y",
    )(ra, rb, leafx, midx, topx, back)


def glue_z_kernel(ra_ref, topxy_ref, pair_ref):
    odd = lax.axis_index("gz") % 2
    mine, other = topxy_ref[0:36, :], ra_ref[416:452, :]
    pair_ref[...] = jnp.concatenate(
        [jnp.where(odd == 1, other, mine), jnp.where(odd == 1, mine, other)], axis=0
    )


def glue_z(ra, topxy):
    return pl.pallas_call(
        glue_z_kernel,
        in_specs=[VMEM] * 2,
        out_specs=VMEM,
        out_shape=jax.ShapeDtypeStruct((72, 128), F32),
        compiler_params=pltpu.CompilerParams(vmem_limit_bytes=8 << 20),
        name="glue_z",
    )(ra, topxy)


def offset_tiles(out_ref, table, cz, masked):
    zero = jnp.zeros((2, 128), F32)
    keep_rows = lax.broadcasted_iota(jnp.int32, (8, 128), 0)
    near = (keep_rows >= 1 + cz) & (keep_rows <= 3 + cz)
    for xy in range(49):
        start = xy * 7 + 1 - cz
        tile = jnp.concatenate([table[start : start + 6, :], zero], axis=0)
        if masked and 2 <= xy // 7 <= 4 and 2 <= xy % 7 <= 4:
            tile = jnp.where(near, 0.0, tile)
        out_ref[xy] = tile


def tables_kernel(in_ref, out_ref, _, scale_ref, tin_ref, tout_ref, top_in_ref, top_out_ref):
    scale_ref[...] = in_ref[0]
    for x in range(2, 5):
        for y in range(2, 5):
            row = x * 49 + y * 7 + 2
            scale_ref[row : row + 3, :] = jnp.zeros((3, 128), F32)
    for cz in range(2):
        offset_tiles(tin_ref.at[cz], in_ref.at[1], cz, True)
        offset_tiles(tout_ref.at[cz], out_ref.at[1], cz, False)
    odd = lax.axis_index("gz") % 2
    lanes = lax.broadcasted_iota(jnp.int32, (8, 128), 0)
    near = (lanes >= 1 + odd) & (lanes <= 3 + odd)
    for xy in range(49):
        for ref, table, masked in ((top_in_ref, in_ref, True), (top_out_ref, out_ref, False)):
            rows = table[2, xy * 7 : xy * 7 + 7, :]
            tile = jnp.where(odd == 1, rows[0:6], rows[1:7])
            tile = jnp.concatenate([tile, jnp.zeros((2, 128), F32)], axis=0)
            if masked and 2 <= xy // 7 <= 4 and 2 <= xy % 7 <= 4:
                tile = jnp.where(near, 0.0, tile)
            ref[xy] = tile


def run_tables(in_scale, out_scale, after):
    return pl.pallas_call(
        tables_kernel,
        in_specs=[VMEM] * 2 + [pl.BlockSpec(memory_space=pl.ANY)],
        out_specs=[VMEM] * 5,
        out_shape=[
            jax.ShapeDtypeStruct((343, 128), F32),
            jax.ShapeDtypeStruct((2, 49, 8, 128), F32),
            jax.ShapeDtypeStruct((2, 49, 8, 128), F32),
            jax.ShapeDtypeStruct((49, 8, 128), F32),
            jax.ShapeDtypeStruct((49, 8, 128), F32),
        ],
        cost_estimate=pl.CostEstimate(flops=1 << 28, bytes_accessed=3 << 20, transcendentals=0),
        compiler_params=pltpu.CompilerParams(vmem_limit_bytes=8 << 20),
        name="tables",
    )(in_scale, out_scale, after)


def far_kernel(
    leafxy_ref, midxy_ref, ra_ref, rb_ref, scale_ref, tin_ref, tout_ref, out_ref, core_ref,
    far0_ref, far1_ref,
    leaf_ref, mid_ref, acc_ref, even_ref, odd_ref,
):
    odd = lax.axis_index("gz") % 2
    leaf_ref[:, 2:6] = leafxy_ref[...]
    for ref, high in ((ra_ref, 1 - odd), (rb_ref, odd)):
        for x in range(12):
            for z in range(2):
                row = (x * 2 + z) * 12
                leaf_ref[x, high * 6 + z] = ref[row : row + 12, :]
    for x in range(8):
        for y in range(8):
            row = 288 + (x * 8 + y) * 2
            a, b = ra_ref[row : row + 2, :], rb_ref[row : row + 2, :]
            mid_ref[x, y] = jnp.concatenate(
                [
                    jnp.where(odd == 1, a, b),
                    midxy_ref[x, y],
                    jnp.where(odd == 1, b, a),
                    jnp.zeros((2, 128), F32),
                ],
                axis=0,
            )
    def products(operand_ref, core):
        rows = 192
        return [dot(operand_ref[i * rows : i * rows + rows, :], core) for i in range(8)]

    far0_ref[...] = jnp.zeros((8, 32, 128), F32)
    core0 = core_ref[0]

    def row_of(qx, qy, qz, pair, cz):
        return (qx + 1 - pair // 2) * 49 + (qy + 1 - pair % 2) * 7 + qz + 1 - cz

    def build_leaf(step, operand_ref):
        qx, qz = step // 6, step % 6
        for qy in range(6):
            tiles = []
            for x in range(4):
                for z in range(2):
                    tiles.append(leaf_ref[2 * x + qx, 2 * z + qz, pl.ds(qy, 4, stride=2), :])
            source = jnp.concatenate(tiles, axis=0)
            for pair in range(4):
                for cz in range(2):
                    start = ((pair * 2 + cz) * 6 + qy) * 32
                    row = row_of(qx, qy, qz, pair, cz)
                    scale = jnp.broadcast_to(scale_ref[pl.ds(row, 1), :], (32, 128))
                    operand_ref[start : start + 32, :] = (source * scale).astype(BF16)

    def apply_leaf(step, image):
        qx, qz = step // 6, step % 6
        for pair in range(4):
            for cz in range(2):
                total = far0_ref[pair * 2 + cz]
                for qy in range(6):
                    row = row_of(qx, qy, qz, pair, cz)
                    scale = jnp.broadcast_to(out_ref[0, pl.ds(row, 1), :], (32, 128))
                    start = ((pair * 2 + cz) * 6 + qy) * 32
                    total = total + scale * image[start // 192][start % 192 : start % 192 + 32]
                far0_ref[pair * 2 + cz] = total

    build_leaf(0, even_ref)

    @pl.loop(0, 18)
    def _(turn):
        image = products(even_ref, core0)
        build_leaf(2 * turn + 1, odd_ref)
        apply_leaf(2 * turn, image)
        image = products(odd_ref, core0)
        build_leaf(jnp.minimum(2 * turn + 2, 35), even_ref)
        apply_leaf(2 * turn + 1, image)

    acc_ref[...] = jnp.zeros((8, 32, 128), F32)
    core1 = core_ref[1]

    def build_mid(qx, operand_ref):
        for qy in range(6):
            tiles = [mid_ref[2 * x + qx, 2 * y + qy] for x in range(2) for y in range(2)]
            for pair in range(4):
                xy = (qx + 1 - pair // 2) * 7 + qy + 1 - pair % 2
                for cz in range(2):
                    scale = tin_ref[cz, xy]
                    start = ((pair * 2 + cz) * 6 + qy) * 32
                    operand_ref[start : start + 32, :] = jnp.concatenate(
                        [tile * scale for tile in tiles], axis=0
                    ).astype(BF16)

    def apply_mid(qx, image):
        for pair in range(4):
            for cz in range(2):
                total = acc_ref[pair * 2 + cz]
                for qy in range(6):
                    scale = tout_ref[cz, (qx + 1 - pair // 2) * 7 + qy + 1 - pair % 2]
                    scale = jnp.concatenate([scale] * 4, axis=0)
                    start = ((pair * 2 + cz) * 6 + qy) * 32
                    total = total + scale * image[start // 192][start % 192 : start % 192 + 32]
                acc_ref[pair * 2 + cz] = total

    build_mid(0, even_ref)

    @pl.loop(0, 3)
    def _(turn):
        image = products(even_ref, core1)
        build_mid(2 * turn + 1, odd_ref)
        apply_mid(2 * turn, image)
        image = products(odd_ref, core1)
        build_mid(jnp.minimum(2 * turn + 2, 5), even_ref)
        apply_mid(2 * turn + 1, image)

    for child in range(8):
        for parent in range(4):
            tile = acc_ref[child, parent * 8 : parent * 8 + 8, :]
            far1_ref[child * 4 + parent : child * 4 + parent + 1, :] = jnp.sum(
                tile, axis=0, keepdims=True
            )


def run_far(leafxy, midxy, ra, rb, scale, tin, tout, out_scale, transfer):
    return pl.pallas_call(
        far_kernel,
        in_specs=[VMEM] * 9,
        out_specs=[VMEM] * 2,
        out_shape=[
            jax.ShapeDtypeStruct((8, 32, 128), F32),
            jax.ShapeDtypeStruct((32, 128), F32),
        ],
        scratch_shapes=[
            pltpu.VMEM((12, 8, 12, 128), F32),
            pltpu.VMEM((8, 8, 8, 128), F32),
            pltpu.VMEM((8, 32, 128), F32),
            pltpu.VMEM((1536, 128), BF16),
            pltpu.VMEM((1536, 128), BF16),
        ],
        cost_estimate=pl.CostEstimate(flops=4 << 30, bytes_accessed=4 << 20, transcendentals=0),
        compiler_params=pltpu.CompilerParams(vmem_limit_bytes=24 << 20),
        name="far",
    )(leafxy, midxy, ra, rb, scale, tin, tout, out_scale, transfer)


def force_kernel(
    far0_ref, far1_ref, pair_ref, side_ref, far_ref, next_ref, tin_ref, tout_ref, core_ref, down_ref,
    charge_ref, front_ref, back_ref, pos_ref, wave_ref,
    forces_ref, share_ref,
    window_ref, operand_ref, mid_ref, local_ref,
):
    odd = lax.axis_index("gz") % 2
    near, beyond = side_ref[416:452, :], far_ref[0:36, :]
    first, second = next_ref[0:36, :], next_ref[36:72, :]
    lines = [
        jnp.where(odd == 1, first, beyond),
        jnp.where(odd == 1, second, near),
        pair_ref[0:36, :],
        pair_ref[36:72, :],
        jnp.where(odd == 1, near, first),
        jnp.where(odd == 1, beyond, second),
    ]
    for xy in range(36):
        window_ref[xy] = jnp.concatenate(
            [line[xy : xy + 1] for line in lines] + [jnp.zeros((2, 128), F32)], axis=0
        )
    for qx in range(6):
        for qy in range(6):
            source = window_ref[qx * 6 + qy]
            tiles = []
            for pair in range(4):
                cx, cy = pair // 2, pair % 2
                tiles.append(source * tin_ref[(qx + 1 - cx) * 7 + qy + 1 - cy])
            start = (qx * 6 + qy) * 32
            operand_ref[start : start + 32, :] = jnp.concatenate(tiles, axis=0).astype(BF16)
    totals = [jnp.zeros((8, 128), F32) for _ in range(4)]
    for qx in range(6):
        image = dot(operand_ref[qx * 192 : qx * 192 + 192, :], core_ref[2])
        for qy in range(6):
            for pair in range(4):
                cx, cy = pair // 2, pair % 2
                scale = tout_ref[(qx + 1 - cx) * 7 + qy + 1 - cy]
                start = qy * 32 + pair * 8
                totals[pair] = totals[pair] + scale * image[start : start + 8]
    local_top = jnp.concatenate(
        [jnp.sum(total, axis=0, keepdims=True) for total in totals] + [jnp.zeros((4, 128), F32)],
        axis=0,
    ).astype(BF16)
    for child in range(8):
        cx, cy, cz = child // 4, child // 2 % 2, child % 2
        rows = far1_ref[child * 4 : child * 4 + 4, :] + dot(local_top, down_ref[1, child])[0:4]
        for parent in range(4):
            row = ((2 * (parent // 2) + cx) * 2 + cz) * 4 + 2 * (parent % 2) + cy
            mid_ref[row : row + 1, :] = rows[parent : parent + 1]
    local_mid = mid_ref[...].astype(BF16)
    for child in range(8):
        cx, cy, cz = child // 4, child // 2 % 2, child % 2
        rows = far0_ref[child] + dot(local_mid, down_ref[0, child])
        for x in range(4):
            for z in range(2):
                start = (x * 2 + z) * 4
                local_ref[2 * x + cx, 2 * z + cz, pl.ds(cy, 4, stride=2), :] = rows[start : start + 4]

    lane_box = lax.broadcasted_iota(jnp.int32, (8, 128), 1) // 32
    row_y = lax.broadcasted_iota(jnp.int32, (8, 128), 0)
    base_x = lax.axis_index("gx") * 8
    base_y = lax.axis_index("gy") * 8
    base_z = lax.axis_index("gz") * 4
    place_y0 = (base_y + row_y).astype(F32)
    place_z0 = (base_z + lane_box).astype(F32)

    def one_plane(x, sums, sines):
        local = local_ref[x].reshape(32, 128)
        weights = jnp.concatenate([local * wave_ref[d : d + 1, :] for d in range(3)], axis=0)
        high = weights.astype(BF16)
        low = (weights - high.astype(F32)).astype(BF16)
        product = dot(
            jnp.concatenate([high, low], axis=1), jnp.concatenate([sines, sines], axis=0)
        )
        charge = charge_ref[x]
        found = []
        for d in range(3):
            picked = jnp.zeros((8, 128), F32)
            for z in range(4):
                start = (d * 4 + z) * 8
                for y in range(8):
                    picked = jnp.where(
                        (row_y == y) & (lane_box == z),
                        product[start : start + 8, y * 128 : y * 128 + 128],
                        picked,
                    )
            picked = picked * charge
            forces_ref[d, x] = picked
            found.append(picked)
        places = (
            ((base_x + x).astype(F32) + pos_ref[0, x]) * (1.0 / 32),
            (place_y0 + pos_ref[1, x]) * (1.0 / 64),
            (place_z0 + pos_ref[2, x]) * (1.0 / 64),
        )
        return tuple(
            sums[d * 3 + e] + places[d] * found[e] for d in range(3) for e in range(3)
        )

    sums = (jnp.zeros((8, 128), F32),) * 9
    sums = lax.fori_loop(0, 4, lambda x, sums: one_plane(x, sums, front_ref[x]), sums)
    sums = lax.fori_loop(0, 4, lambda x, sums: one_plane(x + 4, sums, back_ref[x]), sums)
    lane = lax.broadcasted_iota(jnp.int32, (8, 128), 1)
    row = jnp.zeros((8, 128), F32)
    for i in range(9):
        row = jnp.where(lane == i, jnp.sum(sums[i]), row)
    share_ref[...] = jnp.broadcast_to(row[0:1], (512, 128))


def run_forces(far0, far1, pair, side, beyond, following, top_in, top_out, transfer, downward, charge, front, back, positions, wave):
    return pl.pallas_call(
        force_kernel,
        in_specs=[VMEM] * 15,
        out_specs=[VMEM] * 2,
        out_shape=[
            jax.ShapeDtypeStruct((3, 8, 8, 128), F32),
            jax.ShapeDtypeStruct((512, 128), F32),
        ],
        scratch_shapes=[
            pltpu.VMEM((36, 8, 128), F32),
            pltpu.VMEM((1152, 128), BF16),
            pltpu.VMEM((32, 128), F32),
            pltpu.VMEM((8, 4, 8, 128), F32),
        ],
        compiler_params=pltpu.CompilerParams(vmem_limit_bytes=24 << 20),
        name="forces",
    )(far0, far1, pair, side, beyond, following, top_in, top_out, transfer, downward, charge, front, back, positions, wave)


def virial_kernel(scale, rows_ref, virial_ref):
    row = jnp.sum(rows_ref[...], axis=0, keepdims=True) * scale
    for d in range(3):
        virial_ref[d : d + 1, :] = row[:, d * 3 : d * 3 + 3]


def run_virial(rows, scale):
    return pl.pallas_call(
        lambda rows_ref, virial_ref: virial_kernel(scale, rows_ref, virial_ref),
        in_specs=[VMEM],
        out_specs=VMEM,
        out_shape=jax.ShapeDtypeStruct((3, 3), F32),
        compiler_params=pltpu.CompilerParams(vmem_limit_bytes=8 << 20),
        name="virial",
    )(rows)


def swapped(value, axis, kind):
    count = lax.axis_size(axis)
    pairs = []
    for i in range(count):
        hop = (1, -1, 3)[kind]
        pairs.append((i, (i + hop) % count if i % 2 == 0 else (i - hop) % count))
    return lax.ppermute(value, axis, pairs)


def shards(
    features, positions, box_counts, w_hidden, w_charge, wave_numbers, phases,
    upward, downward, transfer, out_scale, in_scale,
):
    phases = phases.reshape(1, 128)
    charge, own, xb = run_atoms(
        features, positions, box_counts.transpose(0, 2, 1), w_hidden, w_charge.reshape(1, 128),
        wave_numbers, phases, upward,
    )
    rb = swapped(xb, "gx", 1)
    front, xa = run_front(positions, wave_numbers, phases, own, 4)
    scale, tin, tout, top_in, top_out = run_tables(in_scale, out_scale, own)
    ra = swapped(xa, "gx", 0)
    leaf, mid, top, ya, yb = glue_x(ra, rb, own, front, scale)
    back = run_sines(positions, wave_numbers, phases, top, 4, 4)
    ra, rb = swapped(ya, "gy", 0), swapped(yb, "gy", 1)
    leaf, mid, top, za, zb = glue_y(ra, rb, leaf, mid, top, back)
    ra, rb = swapped(za, "gz", 0), swapped(zb, "gz", 1)
    beyond = lax.ppermute(
        top, "gz", [(i, (i + (-2 if i % 2 else 2)) % 16) for i in range(16)]
    )
    pair = glue_z(ra, top)
    following = swapped(pair, "gz", 2)
    far0, far1 = run_far(leaf, mid, ra, rb, scale, tin, tout, out_scale, transfer)
    forces, share = run_forces(
        far0, far1, pair, rb, beyond, following, top_in, top_out, transfer, downward, charge, front, back,
        positions, wave_numbers,
    )
    rows = lax.all_to_all(share, ("gx", "gy", "gz"), 0, 0, tiled=True)
    return forces, run_virial(rows, 1.0 / math.sqrt(4194304))


def solution(mesh):
    in_specs = (
        P("gx", "gy", "gz", None),
        P(None, "gx", "gy", "gz"),
        P("gx", "gy", "gz"),
    ) + (P(),) * 9
    out_specs = (P(None, "gx", "gy", "gz"), P())
    return jax.shard_map(shards, mesh=mesh, in_specs=in_specs, out_specs=out_specs, check_vma=False)
```
